32 devices in a mesh: fsdp: 8 (over z, y), dp: 4 (over x, core).
Axes of the slice: x: 2, y: 2, z: 4, core: 2. Of those that a mesh axis runs over, the one named last changes fastest.
Arguments:
- patches: bfloat16 [32768, 128], P(('fsdp', 'dp')), may hold values from -6 to 6
- targets: float32 [32768, 128], P(('fsdp', 'dp')), may hold values from -6 to 6
- size_ids: int32 [32768], P(('fsdp', 'dp')), may hold values from 0 to 4
- time_ids: int32 [32768], P(('fsdp', 'dp')), may hold values from 0 to 255
- variate_ids: int32 [32768], P(('fsdp', 'dp')), may hold values from 0 to 3
- lengths: int32 [512], P(('fsdp', 'dp')), may hold values from 32 to 64, as said below
- w_in: float32 [248, 384], P(None, 'fsdp'), may hold values from -0.75 to 0.75
- w_qkv: float32 [3, 384, 1152], P(None, 'fsdp'), may hold values from -0.3125 to 0.3125
- w_o: float32 [3, 384, 384], P(None, 'fsdp'), may hold values from -1.25 to 1.25
- w_gu: float32 [3, 384, 2048], P(None, 'fsdp'), may hold values from -0.3125 to 0.3125
- w_down: float32 [3, 1024, 384], P(None, 'fsdp'), may hold values from -0.1875 to 0.1875
- w_head: float32 [384, 1152], P('fsdp'), may hold values from -0.3125 to 0.3125
- gains: float32 [7, 384], P(None, 'fsdp'), may hold values from 0.4 to 1.8
- var_bias: float32 [3, 2, 6], replicated, may hold values from -4 to 4
- first_in: float32 [248, 384], P(None, 'fsdp'), may hold values from -2.9802322e-07 to 2.9802322e-07
- first_qkv: float32 [3, 384, 1152], P(None, 'fsdp'), may hold values from -2.9802322e-07 to 2.9802322e-07
- first_o: float32 [3, 384, 384], P(None, 'fsdp'), may hold values from -2.9802322e-07 to 2.9802322e-07
- first_gu: float32 [3, 384, 2048], P(None, 'fsdp'), may hold values from -2.9802322e-07 to 2.9802322e-07
- first_down: float32 [3, 1024, 384], P(None, 'fsdp'), may hold values from -2.9802322e-07 to 2.9802322e-07
- first_head: float32 [384, 1152], P('fsdp'), may hold values from -2.9802322e-07 to 2.9802322e-07
- first_gains: float32 [7, 384], P(None, 'fsdp'), may hold values from -1.1920929e-06 to 1.1920929e-06
- first_bias: float32 [3, 2, 6], replicated, may hold values from -4.172325e-07 to 4.172325e-07
- second_in: float32 [248, 384], P(None, 'fsdp'), may hold values from 8.99339e-15 to 3.590517e-14
- second_qkv: float32 [3, 384, 1152], P(None, 'fsdp'), may hold values from 8.99339e-15 to 3.590517e-14
- second_o: float32 [3, 384, 384], P(None, 'fsdp'), may hold values from 8.99339e-15 to 3.590517e-14
- second_gu: float32 [3, 384, 2048], P(None, 'fsdp'), may hold values from 8.99339e-15 to 3.590517e-14
- second_down: float32 [3, 1024, 384], P(None, 'fsdp'), may hold values from 8.99339e-15 to 3.590517e-14
- second_head: float32 [384, 1152], P('fsdp'), may hold values from 8.99339e-15 to 3.590517e-14
- second_gains: float32 [7, 384], P(None, 'fsdp'), may hold values from 1.4362068e-13 to 5.813218e-13
- second_bias: float32 [3, 2, 6], replicated, may hold values from 2.0175286e-14 to 8.035919e-14
Outputs:
- loss_sum: float32 [], replicated
- target_count: float32 [], replicated
- grad_norm: float32 [], replicated
- new_in: float32 [248, 384], P(None, 'fsdp')
- new_qkv: float32 [3, 384, 1152], P(None, 'fsdp')
- new_o: float32 [3, 384, 384], P(None, 'fsdp')
- new_gu: float32 [3, 384, 2048], P(None, 'fsdp')
- new_down: float32 [3, 1024, 384], P(None, 'fsdp')
- new_head: float32 [384, 1152], P('fsdp')
- new_gains: float32 [7, 384], P(None, 'fsdp')
- new_bias: float32 [3, 2, 6], replicated
- first_in_new: float32 [248, 384], P(None, 'fsdp')
- first_qkv_new: float32 [3, 384, 1152], P(None, 'fsdp')
- first_o_new: float32 [3, 384, 384], P(None, 'fsdp')
- first_gu_new: float32 [3, 384, 2048], P(None, 'fsdp')
- first_down_new: float32 [3, 1024, 384], P(None, 'fsdp')
- first_head_new: float32 [384, 1152], P('fsdp')
- first_gains_new: float32 [7, 384], P(None, 'fsdp')
- first_bias_new: float32 [3, 2, 6], replicated
- second_in_new: float32 [248, 384], P(None, 'fsdp')
- second_qkv_new: float32 [3, 384, 1152], P(None, 'fsdp')
- second_o_new: float32 [3, 384, 384], P(None, 'fsdp')
- second_gu_new: float32 [3, 384, 2048], P(None, 'fsdp')
- second_down_new: float32 [3, 1024, 384], P(None, 'fsdp')
- second_head_new: float32 [384, 1152], P('fsdp')
- second_gains_new: float32 [7, 384], P(None, 'fsdp')
- second_bias_new: float32 [3, 2, 6], replicated
The draws below stay inside these ranges and needn't reach their ends.
Inputs may be any that keep to these rules, and one draw needn't show every extreme that they name: `lengths`: live tokens at the head of each bucket of 64 slots; the rest are padding.
All inputs are finite; a program needn't handle non-finite values.
Results may differ from the reference program's by a relative error of at most 0.03.
Values may be sent and summed in bfloat16 or wider, within the bound.
No kernel may reach another device: no remote copies, remote signals or barrier semaphores. Data moves between devices by JAX's collectives and lax.ppermute only.
A program may use at most 256 MiB of HBM per device.

```python
import math
import jax
import jax.numpy as jnp
from jax import lax

D = 384
H = 6
HD = 64
FF = 1024
PMAX = 128
NQ = 9
BUCKET = 64
L = 3
STEP_NUM = 10
TOK_MB = 512
TOK_DEV = 1024
TOKENS = 32768
IN_CAT = 248
NGAIN = 7
PARAMS = 5848740
N_FSDP = 8
N_DP = 4


def draw_lengths(key, part):
    buckets = TOKENS // BUCKET
    per_device = TOK_DEV // BUCKET
    bucket_ids = jnp.arange(buckets, dtype=jnp.int32)
    device = bucket_ids // per_device
    fsdp_pos = device // N_DP
    dp_pos = device % N_DP
    floor_len = BUCKET // 2
    ceiling = BUCKET * 5 // 8 + BUCKET * 3 // 8 * (fsdp_pos + dp_pos) // (N_FSDP + N_DP - 2)
    raw_bits = jax.random.randint(key, (buckets,), 0, 1 << 20, dtype=jnp.int32)
    drawn_len = raw_bits % (ceiling - floor_len + 1) + floor_len
    slot_id = bucket_ids % per_device
    drawn_len = jnp.where(slot_id == 0, ceiling, drawn_len)
    return jnp.where(slot_id == 1, floor_len, drawn_len).astype(jnp.int32)


def draw_size_ids(key, part):
    token = jnp.arange(TOKENS, dtype=jnp.int32)
    device = token // TOK_DEV
    fsdp_pos = device // N_DP
    dp_pos = device % N_DP
    key_base = jax.random.fold_in(key, 11)
    key_fsdp = jax.random.fold_in(key, 12)
    key_dp = jax.random.fold_in(key, 13)
    base = jax.random.randint(key_base, (TOKENS,), 0, 4, dtype=jnp.int32)
    lift_fsdp = (jax.random.randint(key_fsdp, (TOKENS,), 0, N_FSDP - 1, dtype=jnp.int32) < fsdp_pos).astype(jnp.int32)
    lift_dp = (jax.random.randint(key_dp, (TOKENS,), 0, N_DP - 1, dtype=jnp.int32) < dp_pos).astype(jnp.int32)
    return jnp.minimum(base + lift_fsdp + lift_dp, 4).astype(jnp.int32)


def draw_gains(key, part):
    key = jax.random.fold_in(key, 21)
    column = jnp.arange(D, dtype=jnp.float32) / D
    uniform_part = jax.random.uniform(key, (NGAIN, D), jnp.float32, 0.0, 1.0)
    noise = 0.8 + 0.4 * uniform_part
    return (0.5 + column)[None, :] * noise


def place_ends(array, rng, low, top_value):
    longest = array.shape.index(max(array.shape))
    spots = []
    for shift in (0, 1):
        where = [jax.random.randint(jax.random.fold_in(rng, axis), (), 0, length) for axis, length in enumerate(array.shape)]
        where[longest] = (where[longest] + shift) % array.shape[longest]
        spots.append(tuple(where))
    return array.at[spots[0]].set(low).at[spots[1]].set(top_value)


def shard_levels(rng, shape, cuts, smallest, largest):
    loudness, own = 1.0, jax.random.fold_in(rng, 6)
    for axis_at, blocks in cuts:
        draws = jnp.exp(jax.random.uniform(jax.random.fold_in(own, axis_at), (blocks,), jnp.float32, smallest / len(cuts), largest / len(cuts)))
        loudness = loudness * jnp.repeat(draws, shape[axis_at] // blocks).reshape([-1 if axis == axis_at else 1 for axis in range(len(shape))])
    return loudness


def gaussian(stream_key, dims, deviation, reach, cuts=(), kind=jnp.bfloat16):
    entries = jax.random.normal(stream_key, dims, jnp.float32) * deviation
    if len(cuts) > 0:
        entries = shard_levels(stream_key, dims, cuts, -0.22, 0.18) * entries
    return jnp.clip(entries, min=-reach, max=reach).astype(kind)


def setup_inputs(seed: int = 0) -> dict:
    keys = jax.random.split(jax.random.key(seed), 31)
    patches = gaussian(keys[0], (TOKENS, PMAX), 1.0, 6.0, ((0, 32),))
    targets = gaussian(keys[1], (TOKENS, PMAX), 1.0, 6.0, ((0, 32),), jnp.float32)
    size_ids = draw_size_ids(jax.random.fold_in(keys[30], 71), 0)
    time_ids = place_ends(jax.random.randint(keys[3], (TOKENS,), 0, 256), jax.random.fold_in(keys[3], 1), 0, 255).astype(jnp.int32)
    variate_ids = place_ends(jax.random.randint(keys[4], (TOKENS,), 0, 4), jax.random.fold_in(keys[4], 1), 0, 3).astype(jnp.int32)
    lengths = draw_lengths(jax.random.fold_in(keys[30], 71), 0)
    w_in = gaussian(keys[6], (IN_CAT, D), (PMAX // 2) ** -0.5, 0.75, ((1, 8),), jnp.float32)
    w_qkv = gaussian(keys[7], (L, D, 3 * D), D ** -0.5, 0.3125, ((1, 8),), jnp.float32)
    w_o = gaussian(keys[8], (L, D, D), (D // 16) ** -0.5, 1.25, ((1, 8),), jnp.float32)
    w_gu = gaussian(keys[9], (L, D, 2 * FF), D ** -0.5, 0.3125, ((1, 8),), jnp.float32)
    w_down = gaussian(keys[10], (L, FF, D), FF ** -0.5, 0.1875, ((1, 8),), jnp.float32)
    w_head = gaussian(keys[11], (D, NQ * PMAX), D ** -0.5, 0.3125, ((0, 8),), jnp.float32)
    gains = draw_gains(jax.random.fold_in(keys[30], 71), 0)
    var_bias = gaussian(keys[13], (L, 2, H), 1.0, 4.0, (), jnp.float32)
    first_in = gaussian(keys[14], (IN_CAT, D), (0.000111 / PARAMS ** 0.5), 2.980232238769531e-07, ((1, 8),), jnp.float32)
    first_qkv = gaussian(keys[15], (L, D, 3 * D), (0.000111 / PARAMS ** 0.5), 2.980232238769531e-07, ((1, 8),), jnp.float32)
    first_o = gaussian(keys[16], (L, D, D), (0.000111 / PARAMS ** 0.5), 2.980232238769531e-07, ((1, 8),), jnp.float32)
    first_gu = gaussian(keys[17], (L, D, 2 * FF), (0.000111 / PARAMS ** 0.5), 2.980232238769531e-07, ((1, 8),), jnp.float32)
    first_down = gaussian(keys[18], (L, FF, D), (0.000111 / PARAMS ** 0.5), 2.980232238769531e-07, ((1, 8),), jnp.float32)
    first_head = gaussian(keys[19], (D, NQ * PMAX), (0.000111 / PARAMS ** 0.5), 2.980232238769531e-07, ((0, 8),), jnp.float32)
    first_gains = gaussian(keys[20], (NGAIN, D), (0.000444 / PARAMS ** 0.5), 1.1920928955078125e-06, ((1, 8),), jnp.float32)
    first_bias = gaussian(keys[21], (L, 2, H), (0.000167 / PARAMS ** 0.5), 4.172325134277344e-07, (), jnp.float32)
    second_in = jnp.clip(jnp.exp(math.log(3.590517098049639e-14) - 1.3843914 * jax.random.uniform(keys[22], (IN_CAT, D), jnp.float32) ** shard_levels(keys[22], (IN_CAT, D), ((1, 8),), -0.2, 0.2)), 8.993390105164426e-15, 3.590517098049639e-14)
    second_qkv = jnp.clip(jnp.exp(math.log(3.590517098049639e-14) - 1.3843914 * jax.random.uniform(keys[23], (L, D, 3 * D), jnp.float32) ** shard_levels(keys[23], (L, D, 3 * D), ((1, 8),), -0.2, 0.2)), 8.993390105164426e-15, 3.590517098049639e-14)
    second_o = jnp.clip(jnp.exp(math.log(3.590517098049639e-14) - 1.3843914 * jax.random.uniform(keys[24], (L, D, D), jnp.float32) ** shard_levels(keys[24], (L, D, D), ((1, 8),), -0.2, 0.2)), 8.993390105164426e-15, 3.590517098049639e-14)
    second_gu = jnp.clip(jnp.exp(math.log(3.590517098049639e-14) - 1.3843914 * jax.random.uniform(keys[25], (L, D, 2 * FF), jnp.float32) ** shard_levels(keys[25], (L, D, 2 * FF), ((1, 8),), -0.2, 0.2)), 8.993390105164426e-15, 3.590517098049639e-14)
    second_down = jnp.clip(jnp.exp(math.log(3.590517098049639e-14) - 1.3843914 * jax.random.uniform(keys[26], (L, FF, D), jnp.float32) ** shard_levels(keys[26], (L, FF, D), ((1, 8),), -0.2, 0.2)), 8.993390105164426e-15, 3.590517098049639e-14)
    second_head = jnp.clip(jnp.exp(math.log(3.590517098049639e-14) - 1.3843914 * jax.random.uniform(keys[27], (D, NQ * PMAX), jnp.float32) ** shard_levels(keys[27], (D, NQ * PMAX), ((0, 8),), -0.2, 0.2)), 8.993390105164426e-15, 3.590517098049639e-14)
    second_gains = jnp.clip(jnp.exp(math.log(5.813217745717636e-13) - 1.3981287 * jax.random.uniform(keys[28], (NGAIN, D), jnp.float32) ** shard_levels(keys[28], (NGAIN, D), ((1, 8),), -0.2, 0.2)), 1.4362068392198557e-13, 5.813217745717636e-13)
    second_bias = jnp.clip(jnp.exp(jax.random.uniform(keys[29], (L, 2, H), jnp.float32, math.log(2.01752863412041e-14), math.log(8.035918799961447e-14))), 2.01752863412041e-14, 8.035918799961447e-14)
    return dict(patches=patches, targets=targets, size_ids=size_ids, time_ids=time_ids, variate_ids=variate_ids, lengths=lengths, w_in=w_in, w_qkv=w_qkv, w_o=w_o, w_gu=w_gu, w_down=w_down, w_head=w_head, gains=gains, var_bias=var_bias, first_in=first_in, first_qkv=first_qkv, first_o=first_o, first_gu=first_gu, first_down=first_down, first_head=first_head, first_gains=first_gains, first_bias=first_bias, second_in=second_in, second_qkv=second_qkv, second_o=second_o, second_gu=second_gu, second_down=second_down, second_head=second_head, second_gains=second_gains, second_bias=second_bias)


@jax.custom_vjp
def low(v):
    return lax.optimization_barrier(v.astype(jnp.bfloat16)).astype(jnp.float32)

@jax.custom_vjp
def low_back(v):
    return v

def low_keep(v):
    return (low(v), None)

def low_pass(kept, grad):
    return (grad,)

def back_keep(v):
    return (v, None)

def back_low(kept, grad):
    return (low(grad),)
low.defvjp(low_keep, low_pass)
low_back.defvjp(back_keep, back_low)
EPS_NORM = 1e-05
SMOOTH = 0.5
THETA = 10000.0
MASKED_SCORE = -1e+30
CLIP_NORM = 0.001
BETA_ONE = 0.9
BETA_TWO = 0.95
ADAM_EPS = 1e-08
WEIGHT_DECAY = 0.1
RATE_MATRIX = 0.15
RATE_GAIN = 0.8

def matmul_hi(left_side, right_side):
    return jnp.dot(left_side, right_side, precision=lax.Precision.HIGHEST, preferred_element_type=jnp.float32)

def rms_norm(stream, gain_row):
    return stream * lax.rsqrt(lax.optimization_barrier(jnp.mean(stream * stream, axis=-1, keepdims=True)) + EPS_NORM) * gain_row

def half_turn(tensor):
    middle = tensor.shape[-1] // 2
    return jnp.concatenate([-tensor[..., middle:], tensor[..., :middle]], axis=-1)

def rotary(tensor, cos_table, sin_table):
    return tensor * cos_table + half_turn(tensor) * sin_table

def angle_tables(time_ids):
    frequency = THETA ** (-2.0 * jnp.arange(HD // 2, dtype=jnp.float32) / HD)
    phase_table = time_ids.astype(jnp.float32)[:, None] * frequency[None, :]
    phase_table = jnp.concatenate([phase_table, phase_table], axis=-1)[:, None, :]
    return (jnp.cos(phase_table), jnp.sin(phase_table))

def target_table(size_ids, lengths_block, row_count):
    position = jnp.arange(row_count, dtype=jnp.int32)
    live_rows = position % BUCKET < jnp.repeat(lengths_block, BUCKET, total_repeat_length=row_count)
    widths = sum(((size_ids == size_id).astype(jnp.int32) * (PMAX >> 4 - size_id) for size_id in range(5)))
    target_mask = (live_rows[:, None] & (jnp.arange(PMAX, dtype=jnp.int32)[None, :] < widths[:, None])).astype(jnp.float32)
    return (target_mask, live_rows)

def patch_concat(patches, size_ids):
    pieces = []
    for size_id in range(5):
        span_cols = PMAX >> 4 - size_id
        pieces.append(patches[:, :span_cols] * (size_ids == size_id).astype(jnp.float32)[:, None])
    return jnp.concatenate(pieces, axis=1)

def block_loss(params, block_data):
    w_in, w_qkv, w_o, w_gu, w_down, w_head, gains, var_bias = params
    patches, targets, size_ids, time_ids, variate_ids, lengths_block = block_data
    row_count = patches.shape[0]
    target_mask, live_rows = target_table(size_ids, lengths_block, row_count)
    bucket_id = jnp.arange(row_count, dtype=jnp.int32) // BUCKET
    key_mask = (bucket_id[:, None] == bucket_id[None, :]) & live_rows[None, :]
    same_var = variate_ids[:, None] == variate_ids[None, :]
    cos_table, sin_table = angle_tables(time_ids)
    stream = low_back(matmul_hi(low(patch_concat(patches, size_ids)), w_in))
    for layer_id in range(L):
        normed = low(rms_norm(stream, gains[2 * layer_id]))
        qkv_out = low_back(matmul_hi(normed, w_qkv[layer_id])).reshape(row_count, 3, H, HD)
        queries = low(rotary(qkv_out[:, 0], cos_table, sin_table))
        keys_rot = low(rotary(qkv_out[:, 1], cos_table, sin_table))
        values = low(qkv_out[:, 2])
        score_bias = jnp.where(same_var[None], var_bias[layer_id, 1][:, None, None], var_bias[layer_id, 0][:, None, None])
        scores = jnp.einsum('qhd,khd->hqk', queries, keys_rot, precision=lax.Precision.HIGHEST)
        scores = low_back(scores * HD ** (-0.5) + score_bias)
        scores = jnp.where(key_mask[None], scores, MASKED_SCORE)
        shifted = jnp.exp(scores - lax.optimization_barrier(jnp.max(scores, axis=-1, keepdims=True)))
        attn_prob = shifted / lax.optimization_barrier(jnp.sum(shifted, axis=-1, keepdims=True))
        mixed_out = jnp.einsum('hqk,khd->qhd', low(attn_prob), values, precision=lax.Precision.HIGHEST).reshape(row_count, D)
        stream = stream + low_back(matmul_hi(low(low_back(mixed_out)), w_o[layer_id]))
        ffn_in = low(rms_norm(stream, gains[2 * layer_id + 1]))
        gate_up = low_back(matmul_hi(ffn_in, w_gu[layer_id]))
        hidden = low(jax.nn.silu(gate_up[:, :FF]) * gate_up[:, FF:])
        stream = stream + low_back(matmul_hi(hidden, w_down[layer_id]))
    final_in = low(rms_norm(stream, gains[2 * L]))
    predicted = low_back(matmul_hi(final_in, w_head)).reshape(row_count, NQ, PMAX)
    residual = targets[:, None, :] - predicted
    levels = (jnp.arange(NQ, dtype=jnp.float32) + 1.0) / (NQ + 1)
    pinball = levels[None, :, None] * residual + SMOOTH * jax.nn.softplus(-residual / SMOOTH)
    return jnp.sum(pinball * target_mask[:, None, :])

def adam_update(master, clipped, first_old, second_old, matrix):
    first_new = BETA_ONE * first_old + (1.0 - BETA_ONE) * clipped
    second_new = BETA_TWO * second_old + (1.0 - BETA_TWO) * clipped * clipped
    first_hat = first_new / (1.0 - BETA_ONE ** STEP_NUM)
    second_hat = second_new / (1.0 - BETA_TWO ** STEP_NUM)
    direction = first_hat / (jnp.sqrt(second_hat) + ADAM_EPS)
    if matrix:
        master_new = master - RATE_MATRIX * (direction + WEIGHT_DECAY * master)
    else:
        master_new = master - RATE_GAIN * direction
    return (master_new, first_new, second_new)

def reference(patches, targets, size_ids, time_ids, variate_ids, lengths, w_in, w_qkv, w_o, w_gu, w_down, w_head, gains, var_bias, first_in, first_qkv, first_o, first_gu, first_down, first_head, first_gains, first_bias, second_in, second_qkv, second_o, second_gu, second_down, second_head, second_gains, second_bias):
    masters = (w_in, w_qkv, w_o, w_gu, w_down, w_head, gains, var_bias)
    firsts = (first_in, first_qkv, first_o, first_gu, first_down, first_head, first_gains, first_bias)
    seconds = (second_in, second_qkv, second_o, second_gu, second_down, second_head, second_gains, second_bias)
    blocks = TOKENS // TOK_MB
    block_stack = (patches.astype(jnp.float32).reshape(blocks, TOK_MB, PMAX), targets.reshape(blocks, TOK_MB, PMAX), size_ids.reshape(blocks, TOK_MB), time_ids.reshape(blocks, TOK_MB), variate_ids.reshape(blocks, TOK_MB), lengths.reshape(blocks, TOK_MB // BUCKET))
    count_mask, unused = target_table(size_ids, lengths, TOKENS)
    target_count = jnp.sum(count_mask)

    def total_loss(params):
        rounded = tuple((low(member) for member in params[:7])) + (params[7],)
        checked = jax.checkpoint(block_loss)

        def accumulate(running, block_data):
            return (running + checked(rounded, block_data), None)
        summed, unused_out = lax.scan(accumulate, jnp.zeros((), jnp.float32), block_stack)
        return summed
    loss_sum, pull_back = jax.vjp(total_loss, masters)
    gradients, = pull_back(1.0 / target_count)
    grad_norm = jnp.sqrt(sum((jnp.sum(member * member) for member in gradients)))
    factor = jnp.minimum(1.0, CLIP_NORM / grad_norm)
    fresh = [adam_update(masters[member_id], gradients[member_id] * factor, firsts[member_id], seconds[member_id], member_id < 6) for member_id in range(8)]
    return (loss_sum, target_count, grad_norm, fresh[0][0], fresh[1][0], fresh[2][0], fresh[3][0], fresh[4][0], fresh[5][0], fresh[6][0], fresh[7][0], fresh[0][1], fresh[1][1], fresh[2][1], fresh[3][1], fresh[4][1], fresh[5][1], fresh[6][1], fresh[7][1], fresh[0][2], fresh[1][2], fresh[2][2], fresh[3][2], fresh[4][2], fresh[5][2], fresh[6][2], fresh[7][2])
```

```python
import functools

import jax
import jax.numpy as jnp
from jax import lax
from jax.experimental import pallas as pl
from jax.experimental.pallas import tpu as pltpu
from jax.sharding import PartitionSpec as P

D = 384
H = 6
HD = 64
FF = 1024
PMAX = 128
NQ = 9
BUCKET = 64
L = 3
STEP_NUM = 10
IN_CAT = 248
NGAIN = 7
QKV = 3 * D
HEADW = NQ * PMAX
PAIRS = H // 2
LANES = 2 * HD

TILE = 256

EPS_NORM = 1e-05
SMOOTH = 0.5
THETA = 10000.0
MASKED_SCORE = -1e30
CLIP_NORM = 0.001
BETA_ONE = 0.9
BETA_TWO = 0.95
ADAM_EPS = 1e-08
WEIGHT_DECAY = 0.1
RATE_MATRIX = 0.15
RATE_GAIN = 0.8

BF = jnp.bfloat16
F32 = jnp.float32
AXES = ("fsdp", "dp")


def dot_nn(a, b):
    return lax.dot_general(a, b, (((1,), (0,)), ((), ())), preferred_element_type=F32)


def dot_nt(a, b):
    return lax.dot_general(a, b, (((1,), (1,)), ((), ())), preferred_element_type=F32)


def dot_tn(a, b):
    return lax.dot_general(a, b, (((0,), (0,)), ((), ())), preferred_element_type=F32)


def unit(x):
    inverse = lax.rsqrt(jnp.mean(x * x, axis=-1, keepdims=True) + EPS_NORM)
    return x * inverse, inverse


def rms_backward(u, inverse, gain_row, grad):
    grad_unit = grad * gain_row
    grad_x = inverse * (grad_unit - u * jnp.mean(grad_unit * u, axis=-1, keepdims=True))
    return grad_x, rows_to_eight(grad * u)


def rows_to_eight(x):
    return jnp.sum(x.reshape(x.shape[0] // 8, 8, x.shape[1]), axis=0)


def lane_of(shape):
    return lax.broadcasted_iota(jnp.int32, shape, len(shape) - 1)


def swap_halves(x):
    lane = lane_of(x.shape)
    return jnp.where((lane & 32) == 0, pltpu.roll(x, 96, 1), pltpu.roll(x, 32, 1))


def low_lanes(shape):
    return lane_of(shape) < HD


def two_blocks(x):
    keep = low_lanes(x.shape)
    zero = jnp.zeros_like(x)
    return jnp.concatenate([jnp.where(keep, x, zero), jnp.where(keep, zero, x)], axis=0)


def fold_blocks(x):
    return jnp.where(low_lanes((BUCKET, LANES)), x[:BUCKET], x[BUCKET:])


def half_max(x):
    keep = low_lanes(x.shape)
    floor = jnp.full_like(x, -3e38)
    left = jnp.max(jnp.where(keep, x, floor), axis=-1, keepdims=True)
    right = jnp.max(jnp.where(keep, floor, x), axis=-1, keepdims=True)
    return jnp.where(keep, left, right)


def half_sum(x):
    keep = low_lanes(x.shape)
    zero = jnp.zeros_like(x)
    left = jnp.sum(jnp.where(keep, x, zero), axis=-1, keepdims=True)
    right = jnp.sum(jnp.where(keep, zero, x), axis=-1, keepdims=True)
    return jnp.where(keep, left, right)


def forward_body(first, *refs):
    if first:
        (
            x_ref,
            win_ref,
            wqkv_ref,
            wo_ref,
            wgu_ref,
            wdown_ref,
            gain_ref,
            bias_ref,
            cos_ref,
            sin_ref,
            code_ref,
            base_ref,
            out_ref,
            qkv_ref,
            prob_ref,
            mixed_ref,
            mid_ref,
            gu_ref,
        ) = refs
        stream = dot_nt(x_ref[...], win_ref[...])
        base_ref[...] = stream
    else:
        (
            x_ref,
            wqkv_ref,
            wo_ref,
            wgu_ref,
            wdown_ref,
            gain_ref,
            bias_ref,
            cos_ref,
            sin_ref,
            code_ref,
            out_ref,
            qkv_ref,
            prob_ref,
            mixed_ref,
            mid_ref,
            gu_ref,
        ) = refs
        stream = x_ref[...]
    rows = stream.shape[0]
    normed = (unit(stream)[0] * gain_ref[0:1, :]).astype(BF)
    cos = cos_ref[...]
    sin = sin_ref[...]
    qk = dot_nn(normed, wqkv_ref[:, : 2 * D])
    for j in range(2 * PAIRS):
        part = qk[:, j * LANES : (j + 1) * LANES]
        qkv_ref[:, j * LANES : (j + 1) * LANES] = (part * cos + swap_halves(part) * sin).astype(BF)
    qkv_ref[:, 2 * D :] = dot_nn(normed, wqkv_ref[:, 2 * D :]).astype(BF)
    for b in range(rows // BUCKET):
        here = slice(b * BUCKET, (b + 1) * BUCKET)
        code = code_ref[here, :]
        for p in range(PAIRS):
            q = qkv_ref[here, p * LANES : (p + 1) * LANES]
            k = qkv_ref[here, D + p * LANES : D + (p + 1) * LANES]
            v = qkv_ref[here, 2 * D + p * LANES : 2 * D + (p + 1) * LANES]
            scores = dot_nt(q, two_blocks(k)) * HD ** (-0.5)
            bias = jnp.where(code > 0.5, bias_ref[p + 8 : p + 9, :], bias_ref[p : p + 1, :])
            scores = jnp.where(code < -0.5, MASKED_SCORE, scores + bias)
            e = jnp.exp(scores - half_max(scores))
            prob = (e / half_sum(e)).astype(BF)
            prob_ref[here, p * LANES : (p + 1) * LANES] = prob
            mixed_ref[here, p * LANES : (p + 1) * LANES] = dot_nn(prob, two_blocks(v)).astype(BF)
    middle = stream + dot_nn(mixed_ref[...], wo_ref[...])
    mid_ref[...] = middle
    ffn_in = (unit(middle)[0] * gain_ref[1:2, :]).astype(BF)
    gate_up = dot_nn(ffn_in, wgu_ref[...])
    gu_ref[...] = gate_up.astype(BF)
    gate = gate_up[:, :FF]
    hidden = (gate * (1.0 / (1.0 + jnp.exp(-gate))) * gate_up[:, FF:]).astype(BF)
    out_ref[...] = middle + dot_nn(hidden, wdown_ref[...])


def rows_spec(width):
    return pl.BlockSpec((TILE, width), lambda i: (i, 0))


def whole_spec(shape):
    zeros = (0,) * len(shape)
    return pl.BlockSpec(shape, lambda i: zeros)


def params(limit):
    return pltpu.CompilerParams(
        dimension_semantics=("arbitrary",), vmem_limit_bytes=limit * 1024 * 1024
    )


def forward_layer(x, win, weights, gain_pair, bias_rows, tables):
    first = win is not None
    rows = x.shape[0]
    args = [x] + ([win] if first else []) + list(weights) + [gain_pair, bias_rows] + list(tables)
    in_specs = (
        [rows_spec(x.shape[1])]
        + ([whole_spec(win.shape)] if first else [])
        + [whole_spec(w.shape) for w in weights]
        + [whole_spec(gain_pair.shape), whole_spec(bias_rows.shape)]
        + [rows_spec(LANES)] * 3
    )
    outs = ([(D, F32)] if first else []) + [
        (D, F32),
        (QKV, BF),
        (D, BF),
        (D, BF),
        (D, F32),
        (2 * FF, BF),
    ]
    flops = 2 * rows * (D * QKV + D * D + 3 * D * FF)
    got = pl.pallas_call(
        functools.partial(forward_body, first),
        grid=(rows // TILE,),
        in_specs=in_specs,
        out_specs=[rows_spec(w) for w, _ in outs],
        out_shape=[jax.ShapeDtypeStruct((rows, w), t) for w, t in outs],
        compiler_params=params(48),
        cost_estimate=pl.CostEstimate(flops=flops, bytes_accessed=16 << 20, transcendentals=0),
    )(*args)
    if first:
        return got[1], [got[0]] + list(got[2:])
    return got[0], [x] + list(got[1:])


def head_body(x_ref, target_ref, mask_ref, whead_ref, gain_ref, dx_ref, dw_ref, dg_ref, loss_ref, acc_ref):
    step = pl.program_id(0)

    @pl.when(step == 0)
    def _():
        acc_ref[...] = jnp.zeros_like(acc_ref)
        dg_ref[...] = jnp.zeros_like(dg_ref)
        loss_ref[...] = jnp.zeros_like(loss_ref)

    u, inverse = unit(x_ref[...])
    gain_row = gain_ref[0:1, :]
    final_in = (u * gain_row).astype(BF)
    predicted = dot_nn(final_in, whead_ref[...])
    target = target_ref[...]
    mask = mask_ref[...]
    loss = jnp.zeros((8, PMAX), F32)
    grads = []
    for q in range(NQ):
        level = (q + 1.0) / (NQ + 1)
        r = target - predicted[:, q * PMAX : (q + 1) * PMAX]
        a = r * (-1.0 / SMOOTH)
        e = jnp.exp(-jnp.abs(a))
        recip = 1.0 / (1.0 + e)
        sigmoid = jnp.where(a >= 0, recip, e * recip)
        softplus = jnp.maximum(a, 0.0) + jnp.log(1.0 + e)
        loss = loss + rows_to_eight((level * r + SMOOTH * softplus) * mask)
        grads.append(((sigmoid - level) * mask).astype(BF))
    loss_ref[...] += loss
    grad_pred = jnp.concatenate(grads, axis=1)
    acc_ref[...] += dot_tn(final_in, grad_pred)
    grad_x, grad_gain = rms_backward(u, inverse, gain_row, dot_nt(grad_pred, whead_ref[...]))
    dx_ref[...] = grad_x
    dg_ref[...] += grad_gain

    @pl.when(step == pl.num_programs(0) - 1)
    def _():
        dw_ref[...] = acc_ref[...].astype(BF)


def head(x, targets, mask, whead, gain):
    rows = x.shape[0]
    return pl.pallas_call(
        head_body,
        grid=(rows // TILE,),
        in_specs=[
            rows_spec(D),
            rows_spec(PMAX),
            rows_spec(PMAX),
            whole_spec(whead.shape),
            whole_spec(gain.shape),
        ],
        out_specs=[
            rows_spec(D),
            whole_spec((D, HEADW)),
            whole_spec((8, D)),
            whole_spec((8, PMAX)),
        ],
        out_shape=[
            jax.ShapeDtypeStruct((rows, D), F32),
            jax.ShapeDtypeStruct((D, HEADW), BF),
            jax.ShapeDtypeStruct((8, D), F32),
            jax.ShapeDtypeStruct((8, PMAX), F32),
        ],
        scratch_shapes=[pltpu.VMEM((D, HEADW), F32)],
        compiler_params=params(40),
        cost_estimate=pl.CostEstimate(
            flops=6 * rows * D * HEADW, bytes_accessed=8 << 20, transcendentals=0
        ),
    )(x, targets, mask, whead, gain)


def backward_body(first, *refs):
    if first:
        concat_ref, refs = refs[0], refs[1:]
    (
        dout_ref,
        x_ref,
        qkv_ref,
        prob_ref,
        mixed_ref,
        mid_ref,
        gu_ref,
        wqkv_ref,
        wo_ref,
        wgu_ref,
        wdown_ref,
        gain_ref,
        cos_ref,
        sin_ref,
        code_ref,
        *refs,
    ) = refs
    if first:
        dwin_ref, refs = refs[0], refs[1:]
    else:
        dx_ref, refs = refs[0], refs[1:]
    dqkv_w_ref, do_w_ref, dgu_w_ref, ddown_w_ref, dg_ref, db_ref, *refs = refs
    aqkv_ref, ao_ref, agu_ref, adown_ref, dgu_ref, dqkv_ref = refs[:6]
    step = pl.program_id(0)

    @pl.when(step == 0)
    def _():
        aqkv_ref[...] = jnp.zeros_like(aqkv_ref)
        ao_ref[...] = jnp.zeros_like(ao_ref)
        agu_ref[...] = jnp.zeros_like(agu_ref)
        adown_ref[...] = jnp.zeros_like(adown_ref)
        dg_ref[...] = jnp.zeros_like(dg_ref)
        db_ref[...] = jnp.zeros_like(db_ref)
        if first:
            refs[6][...] = jnp.zeros_like(refs[6])

    dout = dout_ref[...]
    rows = dout.shape[0]
    dout_low = dout.astype(BF)
    gate = gu_ref[:, :FF].astype(F32)
    up = gu_ref[:, FF:].astype(F32)
    sig = 1.0 / (1.0 + jnp.exp(-gate))
    silu = gate * sig
    adown_ref[...] += dot_tn((silu * up).astype(BF), dout_low)
    grad_hidden = dot_nt(dout_low, wdown_ref[...])
    dgu_ref[:, :FF] = (grad_hidden * up * (sig + silu * (1.0 - sig))).astype(BF)
    dgu_ref[:, FF:] = (grad_hidden * silu).astype(BF)
    u_mid, inverse_mid = unit(mid_ref[...])
    gain_mid = gain_ref[1:2, :]
    agu_ref[...] += dot_tn((u_mid * gain_mid).astype(BF), dgu_ref[...])
    grad_mid, dgain_mid = rms_backward(
        u_mid, inverse_mid, gain_mid, dot_nt(dgu_ref[...], wgu_ref[...])
    )
    dg_ref[8:16, :] += dgain_mid
    grad_mid = grad_mid + dout
    grad_attn_low = grad_mid.astype(BF)
    ao_ref[...] += dot_tn(mixed_ref[...], grad_attn_low)
    grad_mixed = dot_nt(grad_attn_low, wo_ref[...]).astype(BF)
    for p in range(PAIRS):
        other_sum = jnp.zeros((8, LANES), F32)
        same_sum = jnp.zeros((8, LANES), F32)
        cols = slice(p * LANES, (p + 1) * LANES)
        kcols = slice(D + p * LANES, D + (p + 1) * LANES)
        vcols = slice(2 * D + p * LANES, 2 * D + (p + 1) * LANES)
        for b in range(rows // BUCKET):
            here = slice(b * BUCKET, (b + 1) * BUCKET)
            code = code_ref[here, :]
            cos = cos_ref[here, :]
            sin = sin_ref[here, :]
            q = qkv_ref[here, cols]
            k2 = two_blocks(qkv_ref[here, kcols])
            v2 = two_blocks(qkv_ref[here, vcols])
            prob_low = prob_ref[here, cols]
            prob = prob_low.astype(F32)
            dm = grad_mixed[here, cols]
            dprob = dot_nt(dm, v2)
            ds = prob * (dprob - half_sum(prob * dprob))
            ds_low = ds.astype(BF)
            ds = ds_low.astype(F32)
            same = code > 0.5
            same_sum = same_sum + rows_to_eight(jnp.where(same, ds, 0.0))
            other_sum = other_sum + rows_to_eight(jnp.where(same, 0.0, ds))
            dq = dot_nn(ds_low, k2) * HD ** (-0.5)
            dk = fold_blocks(dot_tn(ds_low, q)) * HD ** (-0.5)
            dv = fold_blocks(dot_tn(prob_low, dm))
            dqkv_ref[here, cols] = (dq * cos + swap_halves(dq * sin)).astype(BF)
            dqkv_ref[here, kcols] = (dk * cos + swap_halves(dk * sin)).astype(BF)
            dqkv_ref[here, vcols] = dv.astype(BF)
        db_ref[p * 8 : (p + 1) * 8, :] += other_sum
        db_ref[(PAIRS + p) * 8 : (PAIRS + p + 1) * 8, :] += same_sum
    u, inverse = unit(x_ref[...])
    gain_row = gain_ref[0:1, :]
    aqkv_ref[...] += dot_tn((u * gain_row).astype(BF), dqkv_ref[...])
    grad_x, dgain = rms_backward(u, inverse, gain_row, dot_nt(dqkv_ref[...], wqkv_ref[...]))
    dg_ref[0:8, :] += dgain
    grad_x = grad_x + grad_mid
    if first:
        refs[6][...] += dot_tn(grad_x.astype(BF), concat_ref[...])
    else:
        dx_ref[...] = grad_x

    @pl.when(step == pl.num_programs(0) - 1)
    def _():
        dqkv_w_ref[...] = aqkv_ref[...].astype(BF)
        do_w_ref[...] = ao_ref[...].astype(BF)
        dgu_w_ref[...] = agu_ref[...].astype(BF)
        ddown_w_ref[...] = adown_ref[...].astype(BF)
        if first:
            dwin_ref[...] = refs[6][...].astype(BF)


def backward_layer(concat, dout, saved, weights, gain_pair, tables):
    first = concat is not None
    rows = dout.shape[0]
    args = (
        ([concat] if first else [])
        + [dout]
        + list(saved)
        + list(weights)
        + [gain_pair]
        + list(tables)
    )
    in_specs = (
        ([rows_spec(concat.shape[1])] if first else [])
        + [rows_spec(D)]
        + [rows_spec(s.shape[1]) for s in saved]
        + [whole_spec(w.shape) for w in weights]
        + [whole_spec(gain_pair.shape)]
        + [rows_spec(LANES)] * 3
    )
    if first:
        out_specs = [whole_spec((D, concat.shape[1]))]
        out_shape = [jax.ShapeDtypeStruct((D, concat.shape[1]), BF)]
    else:
        out_specs = [rows_spec(D)]
        out_shape = [jax.ShapeDtypeStruct((rows, D), F32)]
    shapes = [(D, QKV), (D, D), (D, 2 * FF), (FF, D)]
    out_specs += [whole_spec(s) for s in shapes] + [whole_spec((16, D)), whole_spec((48, LANES))]
    out_shape += [jax.ShapeDtypeStruct(s, BF) for s in shapes] + [
        jax.ShapeDtypeStruct((16, D), F32),
        jax.ShapeDtypeStruct((48, LANES), F32),
    ]
    scratch = [pltpu.VMEM(s, F32) for s in shapes]
    scratch += [pltpu.VMEM((TILE, 2 * FF), BF), pltpu.VMEM((TILE, QKV), BF)]
    if first:
        scratch.append(pltpu.VMEM((D, concat.shape[1]), F32))
    flops = 4 * rows * (D * QKV + D * D + 3 * D * FF)
    return pl.pallas_call(
        functools.partial(backward_body, first),
        grid=(rows // TILE,),
        in_specs=in_specs,
        out_specs=out_specs,
        out_shape=out_shape,
        scratch_shapes=scratch,
        compiler_params=params(56),
        cost_estimate=pl.CostEstimate(flops=flops, bytes_accessed=24 << 20, transcendentals=0),
    )(*args)


def partners(sizes, fsdp_mask, dp_mask):
    fsdp, dp = sizes
    return [
        (f * dp + d, (f ^ fsdp_mask) * dp + (d ^ dp_mask)) for f in range(fsdp) for d in range(dp)
    ]


def masks_of(size):
    masks = []
    size //= 2
    while size:
        masks.append(size)
        size //= 2
    return masks


def slot_of(offset, masks):
    slot = 0
    for bit, mask in enumerate(masks):
        slot = slot + jnp.where((offset & mask) != 0, 1 << bit, 0)
    return slot


def swap(x, sizes, fsdp_mask, dp_mask):
    return lax.ppermute(x, AXES, partners(sizes, fsdp_mask, dp_mask))


def reorder(slots, masks):
    me = lax.axis_index("fsdp")
    return jnp.stack(
        [
            lax.dynamic_index_in_dim(slots, slot_of(me ^ j, masks), 0, keepdims=False)
            for j in range(slots.shape[0])
        ]
    )


def gather(halves, sizes):
    core = lax.axis_index("dp") & 1
    masks = masks_of(sizes[0])
    mine = jnp.where(core == 0, halves[0], halves[1])[None]
    for mask in masks:
        mine = jnp.concatenate([mine, swap(mine, sizes, mask, 0)], axis=0)
    other = swap(mine, sizes, 0, 1)
    low = jnp.where(core == 0, mine, other)
    high = jnp.where(core == 0, other, mine)
    return reorder(low, masks), reorder(high, masks)


def add(a, b):
    return (a.astype(F32) + b.astype(F32)).astype(BF)


def to_slots(shards, masks):
    me = lax.axis_index("fsdp")
    slots = [None] * shards.shape[0]
    for v in range(shards.shape[0]):
        slot = sum((1 << bit) for bit, mask in enumerate(masks) if v & mask)
        slots[slot] = lax.dynamic_index_in_dim(shards, me ^ v, 0, keepdims=False)
    return jnp.stack(slots)


def scatter(halves, sizes):
    core = lax.axis_index("dp") & 1
    masks = masks_of(sizes[0])
    low, high = halves
    keep = jnp.where(core == 0, low, high)
    give = jnp.where(core == 0, high, low)
    total = to_slots(add(keep, swap(give, sizes, 0, 1)), masks)
    for mask in reversed(masks):
        half = total.shape[0] // 2
        total = add(total[:half], swap(total[half:], sizes, mask, 0))
    total = total[0]
    dp_mask = 2
    while dp_mask < sizes[1]:
        total = add(total, swap(total, sizes, 0, dp_mask))
        dp_mask *= 2
    return total


def exchange(total, sizes):
    core = lax.axis_index("dp") & 1
    other = swap(total, sizes, 0, 1)
    return jnp.where(core == 0, total, other), jnp.where(core == 0, other, total)


def pad_rows(x, rows):
    return jnp.pad(x, ((0, 0),) * (x.ndim - 2) + ((0, rows - x.shape[-2]), (0, 0)))


def pack_layer(qkv, out, gate_up, down):
    rows = qkv.shape[-2]
    parts = [pad_rows(down[..., i * rows : (i + 1) * rows, :], rows) for i in range(3)]
    blank = jnp.zeros(qkv.shape[:-1] + (LANES,), qkv.dtype)
    low = jnp.concatenate([qkv, out, parts[0], parts[1], blank], axis=-1)
    high = jnp.concatenate([gate_up, parts[2]], axis=-1)
    return low, high


def unpack_layer(low, high, down_rows):
    rows = low.shape[-2]
    qkv = low[..., :QKV]
    out = low[..., QKV : QKV + D]
    first = low[..., QKV + D : QKV + 2 * D]
    second = low[..., QKV + 2 * D : QKV + 3 * D]
    gate_up = high[..., : 2 * FF]
    third = high[..., : down_rows - 2 * rows, 2 * FF :]
    return qkv, out, gate_up, jnp.concatenate([first, second, third], axis=-2)


def pack_ends(head_w, in_rows):
    low = head_w[..., : 6 * LANES]
    blank = jnp.zeros(head_w.shape[:-1] + (LANES,), head_w.dtype)
    return low, jnp.concatenate([head_w[..., 6 * LANES :], in_rows, blank], axis=-1)


def unpack_ends(low, high):
    head_w = jnp.concatenate([low, high[..., : 3 * LANES]], axis=-1)
    return head_w, high[..., 3 * LANES : 5 * LANES]


def join_rows(x):
    return x.reshape(x.shape[0] * x.shape[1], x.shape[2])


def rotary_tables(time_ids):
    frequency = THETA ** (-2.0 * jnp.arange(HD // 2, dtype=F32) / HD)
    phase = time_ids.astype(F32)[:, None] * frequency[None, :]
    cos, sin = jnp.cos(phase), jnp.sin(phase)
    return jnp.concatenate([cos] * 4, axis=1), jnp.concatenate([-sin, sin, -sin, sin], axis=1)


def token_tables(size_ids, variate_ids, lengths):
    rows = size_ids.shape[0]
    buckets = rows // BUCKET
    live = jnp.arange(BUCKET, dtype=jnp.int32)[None, :] < lengths[:, None]
    widths = jnp.where(live.reshape(rows), PMAX >> (4 - size_ids), 0)
    mask = (jnp.arange(PMAX, dtype=jnp.int32)[None, :] < widths[:, None]).astype(F32)
    variates = variate_ids.reshape(buckets, BUCKET)
    same = (variates[:, :, None] == variates[:, None, :]).astype(F32)
    code = jnp.where(live[:, None, :], same, -1.0).reshape(rows, BUCKET)
    return mask, jnp.concatenate([code, code], axis=1)


def patch_concat(patches, size_ids):
    pieces = []
    for size_id in range(5):
        span = PMAX >> 4 - size_id
        chosen = (size_ids == size_id)[:, None]
        pieces.append(jnp.where(chosen, patches[:, :span], jnp.zeros((), BF)))
    pieces.append(jnp.zeros((patches.shape[0], 2 * PMAX - IN_CAT), BF))
    return jnp.concatenate(pieces, axis=1)


def adam_update(master, clipped, first_old, second_old, matrix):
    first_new = BETA_ONE * first_old + (1.0 - BETA_ONE) * clipped
    second_new = BETA_TWO * second_old + (1.0 - BETA_TWO) * clipped * clipped
    first_hat = first_new / (1.0 - BETA_ONE**STEP_NUM)
    second_hat = second_new / (1.0 - BETA_TWO**STEP_NUM)
    direction = first_hat / (jnp.sqrt(second_hat) + ADAM_EPS)
    if matrix:
        master_new = master - RATE_MATRIX * (direction + WEIGHT_DECAY * master)
    else:
        master_new = master - RATE_GAIN * direction
    return (master_new, first_new, second_new)


def all_sum(x, sizes, dp_from=1):
    dp_mask = dp_from
    while dp_mask < sizes[1]:
        x = x + swap(x, sizes, 0, dp_mask)
        dp_mask *= 2
    for mask in masks_of(sizes[0]):
        x = x + swap(x, sizes, mask, 0)
    return x


def per_device(sizes, *args):
    patches, targets, size_ids, time_ids, variate_ids, lengths = args[:6]
    masters = args[6:14]
    firsts = args[14:22]
    seconds = args[22:30]
    w_in, w_qkv, w_o, w_gu, w_down, w_head, gains, var_bias = masters
    own = w_head.shape[0]
    down_rows = w_down.shape[1]

    lows, highs = [], []
    for layer in range(L):
        low, high = pack_layer(
            *(w[layer].astype(BF) for w in (w_qkv, w_o, w_gu, w_down))
        )
        lows.append(low)
        highs.append(high)
    in_rows = jnp.concatenate(
        [w_in.T, gains.T, jnp.zeros((own, 2 * PMAX - IN_CAT - NGAIN), F32)], axis=1
    ).astype(BF)
    low, high = pack_ends(w_head.astype(BF), in_rows)
    lows.append(low)
    highs.append(high)
    low, high = gather((jnp.concatenate(lows, axis=1), jnp.concatenate(highs, axis=1)), sizes)
    layer_width = lows[0].shape[1]
    weights = []
    for layer in range(L):
        cols = slice(layer * layer_width, (layer + 1) * layer_width)
        parts = unpack_layer(low[..., cols], high[..., cols], down_rows)
        weights.append(tuple(join_rows(part) for part in parts))
    head_full, in_full = unpack_ends(low[..., L * layer_width :], high[..., L * layer_width :])
    head_full, in_full = join_rows(head_full), join_rows(in_full)
    gain_full = in_full[:, IN_CAT : IN_CAT + NGAIN].T.astype(F32)
    gain_full = jnp.concatenate([gain_full, jnp.zeros((1, D), F32)], axis=0)

    cos, sin = rotary_tables(time_ids)
    mask, code = token_tables(size_ids, variate_ids, lengths)
    tables = (cos, sin, code)
    concat = patch_concat(patches, size_ids)
    count = jnp.sum(mask)
    bias_lanes = jnp.repeat(var_bias, HD, axis=2).reshape(L, 2, PAIRS, LANES)
    bias_lanes = jnp.pad(bias_lanes, ((0, 0), (0, 0), (0, 8 - PAIRS), (0, 0)))
    bias_lanes = bias_lanes.reshape(L, 16, LANES)

    stream = concat
    kept = []
    for layer in range(L):
        stream, saved = forward_layer(
            stream,
            in_full if layer == 0 else None,
            weights[layer],
            gain_full[2 * layer : 2 * layer + 2],
            bias_lanes[layer],
            tables,
        )
        kept.append(saved)
    grad, head_grad, gain_grad, loss = head(
        stream, targets, mask, head_full, gain_full[2 * L : 2 * L + 2]
    )
    loss = jnp.sum(loss)
    gain_grads = {2 * L: jnp.sum(gain_grad, axis=0)}
    bias_grads = [None] * L
    layer_grads = [None] * L
    for layer in reversed(range(L)):
        first, *matrices, gain_grad, bias_grad = backward_layer(
            concat if layer == 0 else None,
            grad,
            kept[layer],
            weights[layer],
            gain_full[2 * layer : 2 * layer + 2],
            tables,
        )
        if layer == 0:
            in_grad = first
        else:
            grad = first
        layer_grads[layer] = matrices
        gain_grads[2 * layer] = jnp.sum(gain_grad[:8], axis=0)
        gain_grads[2 * layer + 1] = jnp.sum(gain_grad[8:], axis=0)
        bias_grads[layer] = jnp.sum(bias_grad.reshape(2, PAIRS, 8, 2, HD), axis=(2, 4)).reshape(2, H)
    gain_grad = jnp.stack([gain_grads[g] for g in range(NGAIN)], axis=1).astype(BF)
    bias_grad = jnp.stack(bias_grads)

    fsdp = sizes[0]

    def shards_of(x):
        return x.reshape(fsdp, x.shape[0] // fsdp, x.shape[1])

    lows, highs = [], []
    for layer in range(L):
        low, high = pack_layer(*(shards_of(g) for g in layer_grads[layer]))
        lows.append(low)
        highs.append(high)
    in_grad = jnp.concatenate(
        [in_grad[:, :IN_CAT], gain_grad, jnp.zeros((D, 2 * PMAX - IN_CAT - NGAIN), BF)], axis=1
    )
    low, high = pack_ends(shards_of(head_grad), shards_of(in_grad))
    lows.append(low)
    highs.append(high)
    total = scatter((jnp.concatenate(lows, axis=-1), jnp.concatenate(highs, axis=-1)), sizes)
    low, high = exchange(total, sizes)

    sums = jnp.concatenate([jnp.stack([loss, count]), bias_grad.reshape(-1)])
    sums = all_sum(jnp.pad(sums, (0, PMAX - sums.shape[0])).reshape(1, PMAX), sizes)[0]
    loss_sum, total_count = sums[0], sums[1]
    inverse_count = 1.0 / total_count
    bias_grad = sums[2 : 2 + bias_grad.size].reshape(bias_grad.shape) * inverse_count

    squares = jnp.sum(jnp.square(low.astype(F32))) + jnp.sum(jnp.square(high.astype(F32)))
    squares = all_sum(squares.reshape(1, 1), sizes, dp_from=sizes[1])[0, 0]
    grad_norm = jnp.sqrt(
        squares * (inverse_count * inverse_count) + jnp.sum(bias_grad * bias_grad)
    )
    factor = jnp.minimum(1.0, CLIP_NORM / grad_norm)
    scale = factor * inverse_count

    pieces = []
    for layer in range(L):
        cols = slice(layer * layer_width, (layer + 1) * layer_width)
        pieces.append(unpack_layer(low[:, cols], high[:, cols], down_rows))
    head_piece, in_piece = unpack_ends(low[:, L * layer_width :], high[:, L * layer_width :])
    gradients = [in_piece[:, :IN_CAT].T]
    gradients += [jnp.stack([pieces[layer][m] for layer in range(L)]) for m in range(4)]
    gradients += [head_piece, in_piece[:, IN_CAT : IN_CAT + NGAIN].T]
    clipped = [g.astype(F32) * scale for g in gradients] + [bias_grad * factor]
    fresh = [
        adam_update(masters[m], clipped[m], firsts[m], seconds[m], m < 6) for m in range(8)
    ]
    return (
        (loss_sum, total_count, grad_norm)
        + tuple(f[0] for f in fresh)
        + tuple(f[1] for f in fresh)
        + tuple(f[2] for f in fresh)
    )


def solution(mesh):
    sizes = (mesh.shape["fsdp"], mesh.shape["dp"])
    tokens = P(("fsdp", "dp"))
    tokens_two = P(("fsdp", "dp"), None)
    columns = P(None, "fsdp")
    stacked = P(None, "fsdp", None)
    states = (columns, stacked, stacked, stacked, stacked, P("fsdp", None), columns, P())
    in_specs = (tokens_two, tokens_two, tokens, tokens, tokens, tokens) + states * 3
    out_specs = (P(), P(), P()) + states * 3
    return jax.shard_map(
        functools.partial(per_device, sizes),
        mesh=mesh,
        in_specs=in_specs,
        out_specs=out_specs,
        check_vma=False,
    )
```

```python
import functools

import jax
import jax.numpy as jnp
from jax import lax
from jax.experimental import pallas as pl
from jax.experimental.pallas import tpu as pltpu
from jax.sharding import PartitionSpec as P

D = 384
H = 6
HD = 64
FF = 1024
PMAX = 128
NQ = 9
BUCKET = 64
L = 3
STEP_NUM = 10
IN_CAT = 248
NGAIN = 7
QKV = 3 * D
HEADW = NQ * PMAX
PAIRS = H // 2
LANES = 2 * HD

TILE = 256

EPS_NORM = 1e-05
SMOOTH = 0.5
THETA = 10000.0
MASKED_SCORE = -1e30
CLIP_NORM = 0.001
BETA_ONE = 0.9
BETA_TWO = 0.95
ADAM_EPS = 1e-08
WEIGHT_DECAY = 0.1
RATE_MATRIX = 0.15
RATE_GAIN = 0.8

BF = jnp.bfloat16
F32 = jnp.float32
AXES = ("fsdp", "dp")


def dot_nn(a, b):
    return lax.dot_general(a, b, (((1,), (0,)), ((), ())), preferred_element_type=F32)


def dot_nt(a, b):
    return lax.dot_general(a, b, (((1,), (1,)), ((), ())), preferred_element_type=F32)


def dot_tn(a, b):
    return lax.dot_general(a, b, (((0,), (0,)), ((), ())), preferred_element_type=F32)


def unit(x):
    inverse = lax.rsqrt(jnp.mean(x * x, axis=-1, keepdims=True) + EPS_NORM)
    return x * inverse, inverse


def rms_backward(u, inverse, gain_row, grad):
    grad_unit = grad * gain_row
    grad_x = inverse * (grad_unit - u * jnp.mean(grad_unit * u, axis=-1, keepdims=True))
    return grad_x, rows_to_eight(grad * u)


def rows_to_eight(x):
    return jnp.sum(x.reshape(x.shape[0] // 8, 8, x.shape[1]), axis=0)


def lane_of(shape):
    return lax.broadcasted_iota(jnp.int32, shape, len(shape) - 1)


def swap_halves(x):
    lane = lane_of(x.shape)
    return jnp.where((lane & 32) == 0, pltpu.roll(x, 96, 1), pltpu.roll(x, 32, 1))


def low_lanes(shape):
    return lane_of(shape) < HD


def two_blocks(x):
    keep = low_lanes(x.shape)
    zero = jnp.zeros_like(x)
    return jnp.concatenate([jnp.where(keep, x, zero), jnp.where(keep, zero, x)], axis=0)


def fold_blocks(x):
    return jnp.where(low_lanes((BUCKET, LANES)), x[:BUCKET], x[BUCKET:])


def sigmoid_of(x):
    return 0.5 * jnp.tanh(0.5 * x) + 0.5


class Group:
    def __init__(self, extra, shards, rows, down_rows):
        self.shards, self.rows, self.down_rows = shards, rows, down_rows
        fields = [("qkv", QKV), ("o", D), ("d0", D), ("d1", D), ("gu", 2 * FF), ("d2", D)] + extra
        used = sum(width for _, width in fields)
        self.half = -(-used // (2 * LANES)) * LANES
        self.pad = 2 * self.half - used
        self.fields = fields
        self.pieces = []
        at = 0
        for name, width in fields:
            done = 0
            while done < width:
                half = (at + done) // self.half
                take = min(width - done, (half + 1) * self.half - at - done)
                self.pieces.append((half, at + done - half * self.half, name, done, take))
                done += take
            at += width

    def row_span(self, name):
        if name[0] == "d":
            first = int(name[1]) * self.rows
            return first, min(self.rows, self.down_rows - first), self.down_rows
        return 0, self.rows, self.rows

    def pack(self, parts):
        parts = dict(parts)
        if "d" in parts:
            down = parts.pop("d")
            for i in range(3):
                part = down[..., i * self.rows : (i + 1) * self.rows, :]
                parts[f"d{i}"] = pad_rows(part, self.rows)
        halves = [[], []]
        for half, _, name, start, width in self.pieces:
            halves[half].append(parts[name][..., start : start + width])
        if self.pad:
            like = halves[1][0]
            halves[1].append(jnp.zeros(like.shape[:-1] + (self.pad,), like.dtype))
        return tuple(jnp.concatenate(h, axis=-1) for h in halves)

    def unpack(self, halves):
        found = {}
        for half, at, name, _, width in self.pieces:
            part = halves[half][..., at : at + width]
            found[name] = jnp.concatenate([found[name], part], axis=-1) if name in found else part
        downs = [found.pop(f"d{i}") for i in range(3)]
        downs[2] = downs[2][..., : self.row_span("d2")[1], :]
        found["d"] = jnp.concatenate(downs, axis=-2)
        return found


def place(group):
    if group.shards == 1:
        return 0, 0
    return lax.axis_index("fsdp"), lax.axis_index("dp") & 1


def copies(group, halves, core, me, targets, sems, outward):
    masks = masks_of(group.shards)
    made = {}
    for n, (half, at, name, start, width) in enumerate(group.pieces):
        if name not in targets:
            continue
        first, count, stride = group.row_span(name)
        for v in range(group.shards):
            row = (me ^ v) * stride + first if group.shards > 1 else first
            if group.shards > 1:
                row = pl.multiple_of(row, 16)
            whole = targets[name].at[pl.ds(row, count), pl.ds(start, width)]
            slots = [h.at[slot_index(v, masks), pl.ds(0, count), pl.ds(at, width)] for h in halves]
            ends = [(whole, slot) if outward else (slot, whole) for slot in slots]
            pair = [
                functools.partial(pltpu.make_async_copy, a, b, sems.at[n, v]) for a, b in ends
            ]
            made.setdefault(name, []).append((half, pair))
    return made


def start_copies(group, made, core):
    def go(which):
        for items in made.values():
            for half, pair in items:
                pair[0 if half == which else 1]().start()

    if group.shards == 1:
        go(0)
    else:
        pl.when(core == 0)(functools.partial(go, 0))
        pl.when(core == 1)(functools.partial(go, 1))


def wait_copies(made, names):
    for name in names:
        for _, pair in made.get(name, []):
            pair[0]().wait()


def slot_index(v, masks):
    return sum((1 << bit) for bit, mask in enumerate(masks) if v & mask)


def masks_of(size):
    masks = []
    size //= 2
    while size:
        masks.append(size)
        size //= 2
    return masks


def any_spec():
    return pl.BlockSpec(memory_space=pl.ANY)


WEIGHTS = {"qkv": (D, QKV), "o": (D, D), "gu": (D, 2 * FF), "d": (FF, D)}


def weight_scratch(group, more=()):
    shapes = [WEIGHTS[name] for name in WEIGHTS] + list(more)
    return [pltpu.VMEM(shape, BF) for shape in shapes] + [
        pltpu.SemaphoreType.DMA((len(group.pieces), group.shards))
    ]


def down_fields(targets):
    targets = dict(targets)
    down = targets.pop("d")
    return {**targets, "d0": down, "d1": down, "d2": down}


def forward_body(first, group, *refs):
    refs = list(refs)
    x_ref, mine_ref, other_ref = refs[:3]
    refs = refs[3:]
    gain_ref = None if first else refs.pop(0)
    bias_ref, cos_ref, sin_ref, code_ref = refs[:4]
    refs = refs[4:]
    if first:
        base_ref, rows_ref = refs[:2]
        refs = refs[2:]
    out_ref, qkv_ref, prob_ref, mixed_ref, mid_ref, gu_ref = refs[:6]
    wqkv_ref, wo_ref, wgu_ref, wdown_ref = refs[6:10]
    sems = refs[-1]
    targets = {"qkv": wqkv_ref, "o": wo_ref, "gu": wgu_ref, "d": wdown_ref}
    if first:
        win_ref, gain_ref = refs[10], refs[11]
        targets["in"] = win_ref
    me, core = place(group)
    made = copies(
        group, (mine_ref, other_ref), core, me, down_fields(targets), sems, outward=False
    )
    opening = pl.program_id(0) == 0

    @pl.when(opening)
    def _():
        start_copies(group, made, core)
        wait_copies(made, ("in", "qkv"))
        if first:
            turned = win_ref[:, PMAX:].astype(F32).T
            gain_ref[...] = turned[IN_CAT - PMAX : IN_CAT - PMAX + 8, :]
            rows_ref[...] = gain_ref[...]

    if first:
        stream = dot_nt(x_ref[...], win_ref[...])
        base_ref[...] = stream
        gains = (gain_ref[0:1, :], gain_ref[1:2, :])
    else:
        stream = x_ref[...]
        gains = (gain_ref[0:1, :], gain_ref[1:2, :])
    rows = stream.shape[0]
    normed = (unit(stream)[0] * gains[0]).astype(BF)
    cos = cos_ref[...]
    sin = sin_ref[...]
    qk = dot_nn(normed, wqkv_ref[:, : 2 * D])
    for j in range(2 * PAIRS):
        part = qk[:, j * LANES : (j + 1) * LANES]
        qkv_ref[:, j * LANES : (j + 1) * LANES] = (part * cos + swap_halves(part) * sin).astype(BF)
    qkv_ref[:, 2 * D :] = dot_nn(normed, wqkv_ref[:, 2 * D :]).astype(BF)
    spots = [(b, p) for b in range(rows // BUCKET) for p in range(PAIRS)]
    scores = []
    for b, p in spots:
        here = slice(b * BUCKET, (b + 1) * BUCKET)
        q = qkv_ref[here, p * LANES : (p + 1) * LANES]
        k = qkv_ref[here, D + p * LANES : D + (p + 1) * LANES]
        scores.append(dot_nt(k, two_blocks(q)))
    probs = []
    for (b, p), score in zip(spots, scores):
        code = code_ref[b * BUCKET : (b + 1) * BUCKET, :]
        bias = jnp.where(code > 0.5, bias_ref[p + 8 : p + 9, :], bias_ref[p : p + 1, :])
        score = jnp.where(code < -0.5, MASKED_SCORE, score * HD ** (-0.5) + bias)
        e = jnp.exp(score - jnp.max(score, axis=0, keepdims=True))
        probs.append((e * (1.0 / jnp.sum(e, axis=0, keepdims=True))).astype(BF))
    for (b, p), prob in zip(spots, probs):
        here = slice(b * BUCKET, (b + 1) * BUCKET)
        cols = slice(p * LANES, (p + 1) * LANES)
        v = qkv_ref[here, 2 * D + p * LANES : 2 * D + (p + 1) * LANES]
        prob_ref[here, cols] = prob
        mixed_ref[here, cols] = fold_blocks(dot_tn(prob, v)).astype(BF)

    @pl.when(opening)
    def _():
        wait_copies(made, ("o", "d0", "d1", "gu", "d2"))

    middle = stream + dot_nn(mixed_ref[...], wo_ref[...])
    mid_ref[...] = middle
    ffn_in = (unit(middle)[0] * gains[1]).astype(BF)
    gate_up = dot_nn(ffn_in, wgu_ref[...])
    gu_ref[...] = gate_up.astype(BF)
    gate = gate_up[:, :FF]
    hidden = (gate * sigmoid_of(gate) * gate_up[:, FF:]).astype(BF)
    out_ref[...] = middle + dot_nn(hidden, wdown_ref[...])


def rows_spec(width):
    return pl.BlockSpec((TILE, width), lambda i: (i, 0))


def whole_spec(shape):
    zeros = (0,) * len(shape)
    return pl.BlockSpec(shape, lambda i: zeros)


def params(limit):
    return pltpu.CompilerParams(
        dimension_semantics=("arbitrary",), vmem_limit_bytes=limit * 1024 * 1024
    )


def forward_layer(x, first, group, halves, gain_pair, bias_rows, tables):
    rows = x.shape[0]
    args = [x, *halves] + ([] if first else [gain_pair]) + [bias_rows, *tables]
    in_specs = [rows_spec(x.shape[1]), any_spec(), any_spec()]
    in_specs += [] if first else [whole_spec(gain_pair.shape)]
    in_specs += [whole_spec(bias_rows.shape)] + [rows_spec(LANES)] * 3
    outs = [(D, F32), (QKV, BF), (D, BF), (D, BF), (D, F32), (2 * FF, BF)]
    out_specs = [rows_spec(w) for w, _ in outs]
    out_shape = [jax.ShapeDtypeStruct((rows, w), t) for w, t in outs]
    scratch = weight_scratch(group, [(D, 2 * PMAX)] if first else [])
    if first:
        out_specs = [rows_spec(D), whole_spec((8, D))] + out_specs
        out_shape = [
            jax.ShapeDtypeStruct((rows, D), F32),
            jax.ShapeDtypeStruct((8, D), F32),
        ] + out_shape
        scratch.insert(-1, pltpu.VMEM((8, D), F32))
    flops = 2 * rows * (D * QKV + D * D + 3 * D * FF)
    got = pl.pallas_call(
        functools.partial(forward_body, first, group),
        grid=(rows // TILE,),
        in_specs=in_specs,
        out_specs=out_specs,
        out_shape=out_shape,
        scratch_shapes=scratch,
        compiler_params=params(48),
        cost_estimate=pl.CostEstimate(flops=flops, bytes_accessed=40 << 20, transcendentals=0),
    )(*args)
    if first:
        return got[2], [got[0]] + list(got[3:]), got[1]
    return got[0], [x] + list(got[1:]), None


def head_body(
    group,
    x_ref,
    target_ref,
    mask_ref,
    mine_ref,
    other_ref,
    gain_ref,
    dx_ref,
    dw_ref,
    dg_ref,
    loss_ref,
    acc_ref,
    whead_ref,
    sems,
):
    step = pl.program_id(0)
    me, core = place(group)
    made = copies(
        group, (mine_ref, other_ref), core, me, {"head": whead_ref}, sems, outward=False
    )

    @pl.when(step == 0)
    def _():
        acc_ref[...] = jnp.zeros_like(acc_ref)
        dg_ref[...] = jnp.zeros_like(dg_ref)
        loss_ref[...] = jnp.zeros_like(loss_ref)
        start_copies(group, made, core)
        wait_copies(made, ("head",))

    u, inverse = unit(x_ref[...])
    gain_row = gain_ref[0:1, :]
    final_in = (u * gain_row).astype(BF)
    predicted = dot_nn(final_in, whead_ref[...])
    target = target_ref[...]
    mask = mask_ref[...]
    loss = jnp.zeros((8, PMAX), F32)
    grads = []
    for q in range(NQ):
        level = (q + 1.0) / (NQ + 1)
        r = target - predicted[:, q * PMAX : (q + 1) * PMAX]
        a = r * (-1.0 / SMOOTH)
        e = jnp.exp(-jnp.abs(a))
        recip = 1.0 / (1.0 + e)
        sigmoid = jnp.where(a >= 0, recip, e * recip)
        softplus = jnp.maximum(a, 0.0) + jnp.log(1.0 + e)
        loss = loss + rows_to_eight((level * r + SMOOTH * softplus) * mask)
        grads.append(((sigmoid - level) * mask).astype(BF))
    loss_ref[...] += loss
    grad_pred = jnp.concatenate(grads, axis=1)
    acc_ref[...] += dot_tn(final_in, grad_pred)
    grad_x, grad_gain = rms_backward(u, inverse, gain_row, dot_nt(grad_pred, whead_ref[...]))
    dx_ref[...] = grad_x
    dg_ref[...] += grad_gain

    @pl.when(step == pl.num_programs(0) - 1)
    def _():
        dw_ref[...] = acc_ref[...].astype(BF)


def head(x, targets, mask, group, halves, gain):
    rows = x.shape[0]
    return pl.pallas_call(
        functools.partial(head_body, group),
        grid=(rows // TILE,),
        in_specs=[
            rows_spec(D),
            rows_spec(PMAX),
            rows_spec(PMAX),
            any_spec(),
            any_spec(),
            whole_spec(gain.shape),
        ],
        out_specs=[
            rows_spec(D),
            whole_spec((D, HEADW)),
            whole_spec((8, D)),
            whole_spec((8, PMAX)),
        ],
        out_shape=[
            jax.ShapeDtypeStruct((rows, D), F32),
            jax.ShapeDtypeStruct((D, HEADW), BF),
            jax.ShapeDtypeStruct((8, D), F32),
            jax.ShapeDtypeStruct((8, PMAX), F32),
        ],
        scratch_shapes=[
            pltpu.VMEM((D, HEADW), F32),
            pltpu.VMEM((D, HEADW), BF),
            pltpu.SemaphoreType.DMA((len(group.pieces), group.shards)),
        ],
        compiler_params=params(40),
        cost_estimate=pl.CostEstimate(
            flops=6 * rows * D * HEADW, bytes_accessed=8 << 20, transcendentals=0
        ),
    )(x, targets, mask, *halves, gain)


def backward_body(extra, group, *refs):
    refs = list(refs)
    extra_ref = refs.pop(0) if extra else None
    dout_ref, x_ref, qkv_ref, prob_ref, mixed_ref, mid_ref, gu_ref = refs[:7]
    mine_ref, other_ref, gain_ref, cos_ref, sin_ref, code_ref = refs[7:13]
    refs = refs[13:]
    dx_ref = None if extra == "in" else refs.pop(0)
    keep_ref, give_ref, dg_ref, db_ref = refs[:4]
    aqkv_ref, ao_ref, agu_ref, adown_ref, dgu_ref, dqkv_ref = refs[4:10]
    wqkv_ref, wo_ref, wgu_ref, wdown_ref, gqkv_ref, go_ref, ggu_ref, gdown_ref = refs[10:18]
    sems, out_sems = refs[18:20]
    if extra == "in":
        ain_ref, gin_ref = refs[20:]
    step = pl.program_id(0)
    me, core = place(group)
    made = copies(
        group,
        (mine_ref, other_ref),
        core,
        me,
        down_fields({"qkv": wqkv_ref, "o": wo_ref, "gu": wgu_ref, "d": wdown_ref}),
        sems,
        outward=False,
    )
    grads = {"qkv": gqkv_ref, "o": go_ref, "gu": ggu_ref, "d": gdown_ref}
    if extra == "in":
        grads["in"] = gin_ref
    if extra == "head":
        grads["head"] = extra_ref
    sent = copies(
        group, (keep_ref, give_ref), core, me, down_fields(grads), out_sems, outward=True
    )

    @pl.when(step == 0)
    def _():
        start_copies(group, made, core)
        aqkv_ref[...] = jnp.zeros_like(aqkv_ref)
        ao_ref[...] = jnp.zeros_like(ao_ref)
        agu_ref[...] = jnp.zeros_like(agu_ref)
        adown_ref[...] = jnp.zeros_like(adown_ref)
        dg_ref[...] = jnp.zeros_like(dg_ref)
        db_ref[...] = jnp.zeros_like(db_ref)
        if extra == "in":
            ain_ref[...] = jnp.zeros_like(ain_ref)
        wait_copies(made, ("qkv", "o", "d0", "d1", "gu", "d2"))

    dout = dout_ref[...]
    rows = dout.shape[0]
    dout_low = dout.astype(BF)
    gate = gu_ref[:, :FF].astype(F32)
    up = gu_ref[:, FF:].astype(F32)
    sig = sigmoid_of(gate)
    silu = gate * sig
    adown_ref[...] += dot_tn((silu * up).astype(BF), dout_low)
    grad_hidden = dot_nt(dout_low, wdown_ref[...])
    dgu_ref[:, :FF] = (grad_hidden * up * (sig + silu * (1.0 - sig))).astype(BF)
    dgu_ref[:, FF:] = (grad_hidden * silu).astype(BF)
    u_mid, inverse_mid = unit(mid_ref[...])
    gain_mid = gain_ref[1:2, :]
    agu_ref[...] += dot_tn((u_mid * gain_mid).astype(BF), dgu_ref[...])
    grad_mid, dgain_mid = rms_backward(
        u_mid, inverse_mid, gain_mid, dot_nt(dgu_ref[...], wgu_ref[...])
    )
    dg_ref[8:16, :] += dgain_mid
    grad_mid = grad_mid + dout
    grad_attn_low = grad_mid.astype(BF)
    ao_ref[...] += dot_tn(mixed_ref[...], grad_attn_low)
    grad_mixed = dot_nt(grad_attn_low, wo_ref[...]).astype(BF)
    spots = [(b, p) for p in range(PAIRS) for b in range(rows // BUCKET)]
    dprobs = []
    for b, p in spots:
        here = slice(b * BUCKET, (b + 1) * BUCKET)
        dm2 = two_blocks(grad_mixed[here, p * LANES : (p + 1) * LANES])
        v = qkv_ref[here, 2 * D + p * LANES : 2 * D + (p + 1) * LANES]
        dprobs.append(dot_nt(v, dm2))
    dscores = []
    for (b, p), dprob in zip(spots, dprobs):
        prob = prob_ref[b * BUCKET : (b + 1) * BUCKET, p * LANES : (p + 1) * LANES].astype(F32)
        ds = prob * (dprob - jnp.sum(prob * dprob, axis=0, keepdims=True))
        dscores.append(ds.astype(BF))
    for p in range(PAIRS):
        other_sum = jnp.zeros((8, LANES), F32)
        same_sum = jnp.zeros((8, LANES), F32)
        for b in range(rows // BUCKET):
            ds = dscores[p * (rows // BUCKET) + b].astype(F32)
            same = code_ref[b * BUCKET : (b + 1) * BUCKET, :] > 0.5
            same_sum = same_sum + rows_to_eight(jnp.where(same, ds, 0.0))
            other_sum = other_sum + rows_to_eight(jnp.where(same, 0.0, ds))
        db_ref[p * 8 : (p + 1) * 8, :] += other_sum
        db_ref[(PAIRS + p) * 8 : (PAIRS + p + 1) * 8, :] += same_sum
    for (b, p), ds in zip(spots, dscores):
        here = slice(b * BUCKET, (b + 1) * BUCKET)
        cols = slice(p * LANES, (p + 1) * LANES)
        kcols = slice(D + p * LANES, D + (p + 1) * LANES)
        vcols = slice(2 * D + p * LANES, 2 * D + (p + 1) * LANES)
        cos = cos_ref[here, :] * HD ** (-0.5)
        sin = sin_ref[here, :] * HD ** (-0.5)
        dm2 = two_blocks(grad_mixed[here, cols])
        dq = fold_blocks(dot_tn(ds, qkv_ref[here, kcols]))
        dk = dot_nn(ds, two_blocks(qkv_ref[here, cols]))
        dv = dot_nn(prob_ref[here, cols], dm2)
        dqkv_ref[here, cols] = (dq * cos + swap_halves(dq * sin)).astype(BF)
        dqkv_ref[here, kcols] = (dk * cos + swap_halves(dk * sin)).astype(BF)
        dqkv_ref[here, vcols] = dv.astype(BF)
    u, inverse = unit(x_ref[...])
    gain_row = gain_ref[0:1, :]
    aqkv_ref[...] += dot_tn((u * gain_row).astype(BF), dqkv_ref[...])
    grad_x, dgain = rms_backward(u, inverse, gain_row, dot_nt(dqkv_ref[...], wqkv_ref[...]))
    dg_ref[0:8, :] += dgain
    grad_x = grad_x + grad_mid
    if extra == "in":
        ain_ref[...] += dot_tn(grad_x.astype(BF), extra_ref[...])
    else:
        dx_ref[...] = grad_x

    @pl.when(step == pl.num_programs(0) - 1)
    def _():
        gqkv_ref[...] = aqkv_ref[...].astype(BF)
        go_ref[...] = ao_ref[...].astype(BF)
        ggu_ref[...] = agu_ref[...].astype(BF)
        gdown_ref[...] = adown_ref[...].astype(BF)
        if extra == "in":
            gin_ref[...] = ain_ref[...].astype(BF)
        start_copies(group, sent, core)
        wait_copies(sent, list(sent))


def backward_layer(extra, extra_array, dout, saved, group, halves, gain_pair, tables):
    rows = dout.shape[0]
    args = ([extra_array] if extra else []) + [dout, *saved, *halves, gain_pair, *tables]
    in_specs = []
    if extra:
        in_specs = [rows_spec(2 * PMAX) if extra == "in" else whole_spec((D, HEADW))]
    in_specs += (
        [rows_spec(D)]
        + [rows_spec(s.shape[1]) for s in saved]
        + [any_spec(), any_spec(), whole_spec(gain_pair.shape)]
        + [rows_spec(LANES)] * 3
    )
    slots = (group.shards, group.rows, group.half)
    out_specs = [any_spec(), any_spec(), whole_spec((16, D)), whole_spec((48, LANES))]
    out_shape = [
        jax.ShapeDtypeStruct(slots, BF),
        jax.ShapeDtypeStruct(slots, BF),
        jax.ShapeDtypeStruct((16, D), F32),
        jax.ShapeDtypeStruct((48, LANES), F32),
    ]
    if extra != "in":
        out_specs = [rows_spec(D)] + out_specs
        out_shape = [jax.ShapeDtypeStruct((rows, D), F32)] + out_shape
    shapes = list(WEIGHTS.values())
    semaphores = pltpu.SemaphoreType.DMA((len(group.pieces), group.shards))
    scratch = [pltpu.VMEM(s, F32) for s in shapes]
    scratch += [pltpu.VMEM((TILE, 2 * FF), BF), pltpu.VMEM((TILE, QKV), BF)]
    scratch += [pltpu.VMEM(s, BF) for s in shapes * 2] + [semaphores, semaphores]
    if extra == "in":
        scratch += [pltpu.VMEM((D, 2 * PMAX), F32), pltpu.VMEM((D, 2 * PMAX), BF)]
    flops = 4 * rows * (D * QKV + D * D + 3 * D * FF)
    got = pl.pallas_call(
        functools.partial(backward_body, extra, group),
        grid=(rows // TILE,),
        in_specs=in_specs,
        out_specs=out_specs,
        out_shape=out_shape,
        scratch_shapes=scratch,
        compiler_params=params(56),
        cost_estimate=pl.CostEstimate(flops=flops, bytes_accessed=80 << 20, transcendentals=0),
    )(*args)
    return ([None] if extra == "in" else []) + list(got)


def partners(sizes, fsdp_mask, dp_mask):
    fsdp, dp = sizes
    return [
        (f * dp + d, (f ^ fsdp_mask) * dp + (d ^ dp_mask)) for f in range(fsdp) for d in range(dp)
    ]


def slot_of(offset, masks):
    slot = 0
    for bit, mask in enumerate(masks):
        slot = slot + jnp.where((offset & mask) != 0, 1 << bit, 0)
    return slot


def swap(x, sizes, fsdp_mask, dp_mask):
    return lax.ppermute(x, AXES, partners(sizes, fsdp_mask, dp_mask))


def reorder(slots, masks):
    me = lax.axis_index("fsdp")
    return jnp.stack(
        [
            lax.dynamic_index_in_dim(slots, slot_of(me ^ j, masks), 0, keepdims=False)
            for j in range(slots.shape[0])
        ]
    )


class Gather:
    def __init__(self, halves, sizes):
        core = lax.axis_index("dp") & 1
        self.sizes = sizes
        self.mine = jnp.where(core == 0, halves[0], halves[1])[None]
        self.masks = masks_of(sizes[0])

    def step(self, mask):
        self.mine = jnp.concatenate([self.mine, swap(self.mine, self.sizes, mask, 0)], axis=0)

    def along(self):
        for mask in self.masks[:-1]:
            self.step(mask)

    def last(self):
        self.got = swap(self.mine, self.sizes, self.masks[-1], 0)

    def pair(self):
        self.mine = jnp.concatenate([self.mine, self.got], axis=0)
        return self.mine, swap(self.mine, self.sizes, 0, 1)


def by_core(mine, other):
    core = lax.axis_index("dp") & 1
    return jnp.where(core == 0, mine, other), jnp.where(core == 0, other, mine)


def add(a, b):
    return (a.astype(F32) + b.astype(F32)).astype(BF)


def to_slots(shards, masks):
    me = lax.axis_index("fsdp")
    slots = [None] * shards.shape[0]
    for v in range(shards.shape[0]):
        slots[slot_index(v, masks)] = lax.dynamic_index_in_dim(shards, me ^ v, 0, keepdims=False)
    return jnp.stack(slots)


class Scatter:
    def __init__(self, keep, give, sizes):
        self.sizes = sizes
        self.keep = keep
        self.got = swap(give, sizes, 0, 1)
        self.moves = [(mask, 0) for mask in reversed(masks_of(sizes[0]))]
        dp_mask = 2
        while dp_mask < sizes[1]:
            self.moves.append((0, dp_mask))
            dp_mask *= 2

    def ready(self):
        if self.moves and self.moves[0][0]:
            half = self.keep.shape[0] // 2
            self.away = add(self.keep[half:], self.got[half:])
            self.keep = add(self.keep[:half], self.got[:half])
        else:
            self.keep = add(self.keep, self.got)
            self.away = self.keep

    def move(self):
        self.got = swap(self.away, self.sizes, *self.moves.pop(0))

    def end(self):
        while self.moves:
            self.ready()
            self.move()
        total = add(self.keep, self.got)[0]
        return by_core(total, swap(total, self.sizes, 0, 1))


def hold(x, *scatters):
    for one in scatters:
        one.ready()
    held = lax.optimization_barrier((x, [(one.keep, one.away) for one in scatters]))
    for one, (keep, away) in zip(scatters, held[1]):
        one.keep, one.away = keep, away
        one.move()
    return held[0]


def pad_rows(x, rows):
    return jnp.pad(x, ((0, 0),) * (x.ndim - 2) + ((0, rows - x.shape[-2]), (0, 0)))


def to_whole(group, whole, mine, other, sizes):
    masks = masks_of(sizes[0])
    low, high = by_core(mine, other)
    parts = group.unpack((reorder(low, masks), reorder(high, masks)))
    parts = {n: p.reshape(1, p.shape[0] * p.shape[1], p.shape[2]) for n, p in parts.items()}
    return whole.pack(parts)


def from_whole(group, whole, low, high, sizes):
    parts = whole.unpack((low, high))
    fsdp = sizes[0]
    parts = {n: p.reshape(fsdp, p.shape[1] // fsdp, p.shape[2]) for n, p in parts.items()}
    low, high = group.pack(parts)
    masks = masks_of(fsdp)
    return by_core(to_slots(low, masks), to_slots(high, masks))


def rotary_tables(time_ids):
    frequency = THETA ** (-2.0 * jnp.arange(HD // 2, dtype=F32) / HD)
    phase = time_ids.astype(F32)[:, None] * frequency[None, :]
    cos, sin = jnp.cos(phase), jnp.sin(phase)
    return jnp.concatenate([cos] * 4, axis=1), jnp.concatenate([-sin, sin, -sin, sin], axis=1)


def token_tables(size_ids, variate_ids, lengths):
    rows = size_ids.shape[0]
    buckets = rows // BUCKET
    live = jnp.arange(BUCKET, dtype=jnp.int32)[None, :] < lengths[:, None]
    widths = jnp.where(live.reshape(rows), PMAX >> (4 - size_ids), 0)
    mask = (jnp.arange(PMAX, dtype=jnp.int32)[None, :] < widths[:, None]).astype(F32)
    variates = variate_ids.reshape(buckets, BUCKET)
    same = (variates[:, :, None] == variates[:, None, :]).astype(F32)
    code = jnp.where(live[:, :, None], same, -1.0).reshape(rows, BUCKET)
    return mask, jnp.concatenate([code, code], axis=1)


def patch_concat(patches, size_ids):
    pieces = []
    for size_id in range(5):
        span = PMAX >> 4 - size_id
        chosen = (size_ids == size_id)[:, None]
        pieces.append(jnp.where(chosen, patches[:, :span], jnp.zeros((), BF)))
    pieces.append(jnp.zeros((patches.shape[0], 2 * PMAX - IN_CAT), BF))
    return jnp.concatenate(pieces, axis=1)


def adam_update(master, clipped, first_old, second_old, matrix):
    first_new = BETA_ONE * first_old + (1.0 - BETA_ONE) * clipped
    second_new = BETA_TWO * second_old + (1.0 - BETA_TWO) * clipped * clipped
    first_hat = first_new / (1.0 - BETA_ONE**STEP_NUM)
    second_hat = second_new / (1.0 - BETA_TWO**STEP_NUM)
    direction = first_hat / (jnp.sqrt(second_hat) + ADAM_EPS)
    if matrix:
        master_new = master - RATE_MATRIX * (direction + WEIGHT_DECAY * master)
    else:
        master_new = master - RATE_GAIN * direction
    return (master_new, first_new, second_new)


def all_sum(x, sizes, dp_from=1):
    dp_mask = dp_from
    while dp_mask < sizes[1]:
        x = x + swap(x, sizes, 0, dp_mask)
        dp_mask *= 2
    for mask in masks_of(sizes[0]):
        x = x + swap(x, sizes, mask, 0)
    return x


def per_device(sizes, *args):
    patches, targets, size_ids, time_ids, variate_ids, lengths = args[:6]
    masters = args[6:14]
    firsts = args[14:22]
    seconds = args[22:30]
    w_in, w_qkv, w_o, w_gu, w_down, w_head, gains, var_bias = masters
    own = w_head.shape[0]
    down_rows = w_down.shape[1]
    direct = own % 16 == 0 and down_rows % 16 == 0
    extras = [[("in", 2 * PMAX)], [], [("head", HEADW)]]
    groups = [Group(extra, sizes[0], own, down_rows) for extra in extras]
    wholes = groups if direct else [Group(extra, 1, D, FF) for extra in extras]

    in_rows = jnp.concatenate(
        [w_in.T, gains.T, jnp.zeros((own, 2 * PMAX - IN_CAT - NGAIN), F32)], axis=1
    ).astype(BF)
    weights = []
    for layer in range(L):
        parts = {"qkv": w_qkv, "o": w_o, "gu": w_gu, "d": w_down}
        parts = {name: w[layer].astype(BF) for name, w in parts.items()}
        if layer == 0:
            parts["in"] = in_rows
        if layer == L - 1:
            parts["head"] = w_head.astype(BF)
        weights.append(Gather(groups[layer].pack(parts), sizes))

    def arrived(layer):
        pair = weights[layer].pair()
        return pair if direct else to_whole(groups[layer], wholes[layer], *pair, sizes)

    for layer in range(L):
        weights[layer].along()
    weights[0].last()

    cos, sin = rotary_tables(time_ids)
    mask, code = token_tables(size_ids, variate_ids, lengths)
    tables = (cos, sin, code)
    concat = patch_concat(patches, size_ids)
    count = jnp.sum(mask)
    bias_lanes = jnp.repeat(var_bias, HD, axis=2).reshape(L, 2, PAIRS, LANES)
    bias_lanes = jnp.pad(bias_lanes, ((0, 0), (0, 0), (0, 8 - PAIRS), (0, 0)))
    bias_lanes = bias_lanes.reshape(L, 16, LANES)

    stream = concat
    kept = []
    gain_pairs = []
    halves = []
    for layer in range(L):
        halves.append(arrived(layer))
        if layer + 1 < L:
            weights[layer + 1].last()
        stream, saved, found = forward_layer(
            stream,
            layer == 0,
            wholes[layer],
            halves[layer],
            None if layer == 0 else gain_pairs[layer],
            bias_lanes[layer],
            tables,
        )
        if layer == 0:
            gain_pairs = [found[0:2], found[2:4], found[4:6], found[6:8]]
        kept.append(saved)
        if layer + 1 < L:
            held = lax.optimization_barrier((stream, weights[layer + 1].got))
            stream, weights[layer + 1].got = held
    grad, head_grad, gain_grad, loss = head(
        stream, targets, mask, wholes[-1], halves[-1], gain_pairs[L]
    )
    gain_grads = {2 * L: jnp.sum(gain_grad, axis=0)}
    bias_grads = [None] * L
    totals = [None] * L
    for layer in reversed(range(L)):
        extra, extra_array = None, None
        if layer == 0:
            extra, extra_array = "in", concat
        elif layer == L - 1:
            extra, extra_array = "head", head_grad
        grad, keep, give, gain_grad, bias_grad = backward_layer(
            extra,
            extra_array,
            grad,
            kept[layer],
            wholes[layer],
            halves[layer],
            gain_pairs[layer],
            tables,
        )
        if not direct:
            keep, give = from_whole(groups[layer], wholes[layer], keep, give, sizes)
        flying = totals[layer + 1 :]
        give, landed = lax.optimization_barrier((give, [one.got for one in flying]))
        for one, got in zip(flying, landed):
            one.got = got
        totals[layer] = Scatter(keep, give, sizes)
        if layer:
            grad = hold(grad, *totals[layer:])
        gain_grads[2 * layer] = jnp.sum(gain_grad[:8], axis=0)
        gain_grads[2 * layer + 1] = jnp.sum(gain_grad[8:], axis=0)
        bias_grads[layer] = jnp.sum(bias_grad.reshape(2, PAIRS, 8, 2, HD), axis=(2, 4)).reshape(2, H)

    small = [jnp.sum(loss)[None], count[None], jnp.stack(bias_grads).reshape(-1)]
    small = jnp.concatenate(small)
    small = jnp.pad(small, (0, D - small.shape[0]))
    rows = [gain_grads[g] for g in range(NGAIN)] + [small]
    rows = all_sum(hold(jnp.stack(rows), totals[0]), sizes)
    loss_sum, total_count = rows[NGAIN, 0], rows[NGAIN, 1]
    inverse_count = 1.0 / total_count
    bias_grad = rows[NGAIN, 2 : 2 + var_bias.size].reshape(var_bias.shape) * inverse_count
    gain_all = rows[:NGAIN]
    gain_own = lax.dynamic_slice_in_dim(gain_all, lax.axis_index("fsdp") * own, own, axis=1)

    pieces = [groups[layer].unpack(totals[layer].end()) for layer in range(L)]
    in_piece = pieces[0]["in"][:, :IN_CAT]
    head_piece = pieces[-1]["head"]
    matrices = [[pieces[layer][m] for layer in range(L)] for m in ("qkv", "o", "gu", "d")]
    squares = 0.0
    for piece in [in_piece, head_piece] + sum(matrices, []):
        squares = squares + jnp.sum(jnp.square(piece.astype(F32)))
    squares = all_sum(squares.reshape(1, 1), sizes, dp_from=sizes[1])[0, 0]
    squares = squares + jnp.sum(jnp.square(gain_all))
    grad_norm = jnp.sqrt(
        squares * (inverse_count * inverse_count) + jnp.sum(bias_grad * bias_grad)
    )
    factor = jnp.minimum(1.0, CLIP_NORM / grad_norm)
    scale = factor * inverse_count

    gradients = [in_piece.T] + [jnp.stack(m) for m in matrices] + [head_piece, gain_own]
    clipped = [g.astype(F32) * scale for g in gradients] + [bias_grad * factor]
    fresh = [
        adam_update(masters[m], clipped[m], firsts[m], seconds[m], m < 6) for m in range(8)
    ]
    return (
        (loss_sum, total_count, grad_norm)
        + tuple(f[0] for f in fresh)
        + tuple(f[1] for f in fresh)
        + tuple(f[2] for f in fresh)
    )


def solution(mesh):
    sizes = (mesh.shape["fsdp"], mesh.shape["dp"])
    tokens = P(("fsdp", "dp"))
    tokens_two = P(("fsdp", "dp"), None)
    columns = P(None, "fsdp")
    stacked = P(None, "fsdp", None)
    states = (columns, stacked, stacked, stacked, stacked, P("fsdp", None), columns, P())
    in_specs = (tokens_two, tokens_two, tokens, tokens, tokens, tokens) + states * 3
    out_specs = (P(), P(), P()) + states * 3
    return jax.shard_map(
        functools.partial(per_device, sizes),
        mesh=mesh,
        in_specs=in_specs,
        out_specs=out_specs,
        check_vma=False,
    )
```

```python
import functools

import jax
import jax.numpy as jnp
from jax import lax
from jax.experimental import pallas as pl
from jax.experimental.pallas import tpu as pltpu
from jax.sharding import PartitionSpec as P

D = 384
H = 6
HD = 64
FF = 1024
PMAX = 128
NQ = 9
BUCKET = 64
L = 3
STEP_NUM = 10
IN_CAT = 248
NGAIN = 7
QKV = 3 * D
HEADW = NQ * PMAX
PAIRS = H // 2
LANES = 2 * HD

TILE = 256

EPS_NORM = 1e-05
SMOOTH = 0.5
THETA = 10000.0
MASKED_SCORE = -1e30
CLIP_NORM = 0.001
BETA_ONE = 0.9
BETA_TWO = 0.95
ADAM_EPS = 1e-08
WEIGHT_DECAY = 0.1
RATE_MATRIX = 0.15
RATE_GAIN = 0.8

BF = jnp.bfloat16
F32 = jnp.float32
AXES = ("fsdp", "dp")


def dot_nn(a, b):
    return lax.dot_general(a, b, (((1,), (0,)), ((), ())), preferred_element_type=F32)


def dot_nt(a, b):
    return lax.dot_general(a, b, (((1,), (1,)), ((), ())), preferred_element_type=F32)


def dot_tn(a, b):
    return lax.dot_general(a, b, (((0,), (0,)), ((), ())), preferred_element_type=F32)


def unit(x):
    inverse = lax.rsqrt(jnp.mean(x * x, axis=-1, keepdims=True) + EPS_NORM)
    return x * inverse, inverse


def rms_backward(u, inverse, gain_row, grad):
    grad_unit = grad * gain_row
    grad_x = inverse * (grad_unit - u * jnp.mean(grad_unit * u, axis=-1, keepdims=True))
    return grad_x, rows_to_eight(grad * u)


def rows_to_eight(x):
    return jnp.sum(x.reshape(x.shape[0] // 8, 8, x.shape[1]), axis=0)


def lane_of(shape):
    return lax.broadcasted_iota(jnp.int32, shape, len(shape) - 1)


def swap_halves(x):
    lane = lane_of(x.shape)
    return jnp.where((lane & 32) == 0, pltpu.roll(x, 96, 1), pltpu.roll(x, 32, 1))


def low_lanes(shape):
    return lane_of(shape) < HD


def two_blocks(x):
    keep = low_lanes(x.shape)
    zero = jnp.zeros_like(x)
    return jnp.concatenate([jnp.where(keep, x, zero), jnp.where(keep, zero, x)], axis=0)


def fold_blocks(x):
    return jnp.where(low_lanes((BUCKET, LANES)), x[:BUCKET], x[BUCKET:])


def sigmoid_of(x):
    return 0.5 * jnp.tanh(0.5 * x) + 0.5


class Group:
    def __init__(self, fields, parts, shards, rows, down_rows):
        self.parts, self.shards, self.rows, self.down_rows = parts, shards, rows, down_rows
        used = sum(width for _, width in fields)
        self.width = -(-used // (parts * LANES)) * LANES
        self.pad = parts * self.width - used
        self.fields = fields
        self.pieces = []
        at = 0
        for name, width in fields:
            done = 0
            while done < width:
                part = (at + done) // self.width
                take = min(width - done, (part + 1) * self.width - at - done)
                self.pieces.append((part, at + done - part * self.width, name, done, take))
                done += take
            at += width
        masks = masks_of(shards)
        self.slots = [slot_index(v, masks) if parts > 1 else v for v in range(shards)]

    def row_span(self, name):
        if name[0] == "d":
            first = int(name[1]) * self.rows
            return first, min(self.rows, self.down_rows - first), self.down_rows
        return 0, self.rows, self.rows

    def pack(self, fields):
        fields = dict(fields)
        if "d" in fields:
            down = fields.pop("d")
            for i in range(3):
                part = down[..., i * self.rows : (i + 1) * self.rows, :]
                fields[f"d{i}"] = pad_rows(part, self.rows)
        parts = [[] for _ in range(self.parts)]
        for part, _, name, start, width in self.pieces:
            parts[part].append(fields[name][..., start : start + width])
        if self.pad:
            like = parts[-1][0]
            parts[-1].append(jnp.zeros(like.shape[:-1] + (self.pad,), like.dtype))
        return tuple(jnp.concatenate(p, axis=-1) for p in parts)

    def unpack(self, parts):
        found = {}
        for part, at, name, _, width in self.pieces:
            got = parts[part][..., at : at + width]
            found[name] = jnp.concatenate([found[name], got], axis=-1) if name in found else got
        if "d0" in found:
            downs = [found.pop(f"d{i}") for i in range(3)]
            downs[2] = downs[2][..., : self.row_span("d2")[1], :]
            found["d"] = jnp.concatenate(downs, axis=-2)
        return found


    def squares(self, own):
        row = lax.broadcasted_iota(jnp.int32, own.shape, 0)
        col = lax.broadcasted_iota(jnp.int32, own.shape, 1)
        used = [jnp.zeros(own.shape, bool)] * 2
        for part, at, name, _, width in self.pieces:
            inside = (col >= at) & (col < at + width) & (row < self.row_span(name)[1])
            used[part] = used[part] | inside
        core = lax.axis_index("dp") & 1
        used = (used[0] & (core == 0)) | (used[1] & (core == 1))
        return jnp.sum(jnp.where(used, jnp.square(own.astype(F32)), 0.0)).reshape(1, 1)


def place(group):
    if group.shards == 1:
        return 0, 0
    return lax.axis_index("fsdp"), lax.axis_index("dp") & 1


def copies(group, arrays, me, targets, sems, outward):
    made = {}
    for n, (part, at, name, start, width) in enumerate(group.pieces):
        if name not in targets:
            continue
        first, count, stride = group.row_span(name)
        for v in range(group.shards):
            owner = v if group.parts == 1 else me ^ v
            row = owner * stride + first
            if not isinstance(row, int):
                row = pl.multiple_of(row, 16)
            whole = targets[name].at[pl.ds(row, count), pl.ds(start, width)]
            slots = [
                a.at[group.slots[v], pl.ds(0, count), pl.ds(at, width)] for a in arrays
            ]
            ends = [(whole, slot) if outward else (slot, whole) for slot in slots]
            pair = [functools.partial(pltpu.make_async_copy, a, b, sems.at[n, v]) for a, b in ends]
            made.setdefault(name, []).append((part, pair))
    return made


def start_copies(group, made, core):
    def go(which):
        for items in made.values():
            for part, pair in items:
                pair[part ^ which]().start()

    if group.shards == 1 or group.parts == 1:
        go(0)
    else:
        pl.when(core == 0)(functools.partial(go, 0))
        pl.when(core == 1)(functools.partial(go, 1))


def wait_copies(made, names):
    for name in names:
        for _, pair in made.get(name, []):
            pair[0]().wait()


def slot_index(v, masks):
    return sum((1 << bit) for bit, mask in enumerate(masks) if v & mask)


def masks_of(size):
    masks = []
    size //= 2
    while size:
        masks.append(size)
        size //= 2
    return masks


def any_spec():
    return pl.BlockSpec(memory_space=pl.ANY)


WEIGHTS = {"in": (D, 2 * PMAX), "qkv": (D, QKV), "o": (D, D), "gu": (D, 2 * FF), "d": (FF, D)}


def semaphores(group):
    return pltpu.SemaphoreType.DMA((len(group.pieces), group.shards))


class Taker:
    def __init__(self, refs):
        self.refs = list(refs)

    def __call__(self, count=1):
        taken, self.refs = self.refs[:count], self.refs[count:]
        return taken[0] if count == 1 else taken

    def named(self, names):
        return dict(zip(names, [self() for _ in names]))


def down_fields(targets):
    targets = dict(targets)
    if "d" in targets:
        down = targets.pop("d")
        targets.update(d0=down, d1=down, d2=down)
    return targets


ATTN, FFN = ("qkv", "o"), ("gu", "d")


def forward_body(names, group, *refs):
    first, attn, ffn = "in" in names, "qkv" in names, "gu" in names
    take = Taker(refs)
    x_ref = take()
    arrays = take.refs[: group.parts]
    take(group.parts)
    gain_ref = None if first else take()
    if attn:
        bias_ref, cos_ref, sin_ref, code_ref = take(4)
    if first:
        base_ref, rows_ref = take(2)
    if attn:
        qkv_ref, prob_ref, mixed_ref, mid_ref = take(4)
    if ffn:
        out_ref, gu_ref = take(2)
    w = take.named(names)
    sems = take()
    if first:
        gain_ref = take()
    me, core = place(group)
    made = copies(group, arrays, me, down_fields(w), sems, outward=False)
    opening = pl.program_id(0) == 0
    early = [n for n in made if n in ("in", "qkv")]
    late = [n for n in made if n not in early]

    @pl.when(opening)
    def _():
        start_copies(group, made, core)
        wait_copies(made, early)
        if first:
            turned = w["in"][:, PMAX:].astype(F32).T
            gain_ref[...] = turned[IN_CAT - PMAX : IN_CAT - PMAX + 8, :]
            rows_ref[...] = gain_ref[...]

    def rest():
        pl.when(opening)(functools.partial(wait_copies, made, late))

    if attn:
        if first:
            stream = dot_nt(x_ref[...], w["in"][...])
            base_ref[...] = stream
        else:
            stream = x_ref[...]
        rows = stream.shape[0]
        normed = (unit(stream)[0] * gain_ref[0:1, :]).astype(BF)
        cos = cos_ref[...]
        sin = sin_ref[...]
        qk = dot_nn(normed, w["qkv"][:, : 2 * D])
        for j in range(2 * PAIRS):
            cols = slice(j * LANES, (j + 1) * LANES)
            qkv_ref[:, cols] = (qk[:, cols] * cos + swap_halves(qk[:, cols]) * sin).astype(BF)
        qkv_ref[:, 2 * D :] = dot_nn(normed, w["qkv"][:, 2 * D :]).astype(BF)
        spots = [(b, p) for b in range(rows // BUCKET) for p in range(PAIRS)]
        scores = []
        for b, p in spots:
            here = slice(b * BUCKET, (b + 1) * BUCKET)
            q = qkv_ref[here, p * LANES : (p + 1) * LANES]
            k = qkv_ref[here, D + p * LANES : D + (p + 1) * LANES]
            scores.append(dot_nt(k, two_blocks(q)))
        probs = []
        for (b, p), score in zip(spots, scores):
            code = code_ref[b * BUCKET : (b + 1) * BUCKET, :]
            bias = jnp.where(code > 0.5, bias_ref[p + 8 : p + 9, :], bias_ref[p : p + 1, :])
            score = jnp.where(code < -0.5, MASKED_SCORE, score * HD ** (-0.5) + bias)
            e = jnp.exp(score - jnp.max(score, axis=0, keepdims=True))
            probs.append((e * (1.0 / jnp.sum(e, axis=0, keepdims=True))).astype(BF))
        for (b, p), prob in zip(spots, probs):
            here = slice(b * BUCKET, (b + 1) * BUCKET)
            cols = slice(p * LANES, (p + 1) * LANES)
            v = qkv_ref[here, 2 * D + p * LANES : 2 * D + (p + 1) * LANES]
            prob_ref[here, cols] = prob
            mixed_ref[here, cols] = fold_blocks(dot_tn(prob, v)).astype(BF)
        rest()
        middle = stream + dot_nn(mixed_ref[...], w["o"][...])
        mid_ref[...] = middle
    else:
        rest()
        middle = x_ref[...]
    if ffn:
        ffn_in = (unit(middle)[0] * gain_ref[1:2, :]).astype(BF)
        gate_up = dot_nn(ffn_in, w["gu"][...])
        gu_ref[...] = gate_up.astype(BF)
        gate = gate_up[:, :FF]
        hidden = (gate * sigmoid_of(gate) * gate_up[:, FF:]).astype(BF)
        out_ref[...] = middle + dot_nn(hidden, w["d"][...])


def rows_spec(width):
    return pl.BlockSpec((TILE, width), lambda i: (i, 0))


def whole_spec(shape):
    zeros = (0,) * len(shape)
    return pl.BlockSpec(shape, lambda i: zeros)


def params(limit):
    return pltpu.CompilerParams(
        dimension_semantics=("arbitrary",), vmem_limit_bytes=limit * 1024 * 1024
    )


def forward_layer(x, names, group, arrays, gain_pair, bias_rows, tables):
    first, attn, ffn = "in" in names, "qkv" in names, "gu" in names
    rows = x.shape[0]
    args = [x, *arrays]
    in_specs = [rows_spec(x.shape[1])] + [any_spec()] * group.parts
    if not first:
        args.append(gain_pair)
        in_specs.append(whole_spec(gain_pair.shape))
    if attn:
        args += [bias_rows, *tables]
        in_specs += [whole_spec(bias_rows.shape)] + [rows_spec(LANES)] * 3
    outs = [(D, F32)] if first else []
    outs += [(QKV, BF), (D, BF), (D, BF), (D, F32)] if attn else []
    outs += [(D, F32), (2 * FF, BF)] if ffn else []
    out_specs = [rows_spec(w) for w, _ in outs]
    out_shape = [jax.ShapeDtypeStruct((rows, w), t) for w, t in outs]
    scratch = [pltpu.VMEM(WEIGHTS[n], BF) for n in names] + [semaphores(group)]
    if first:
        out_specs.insert(1, whole_spec((8, D)))
        out_shape.insert(1, jax.ShapeDtypeStruct((8, D), F32))
        scratch.append(pltpu.VMEM((8, D), F32))
    size = sum(WEIGHTS[n][0] * WEIGHTS[n][1] for n in names)
    return pl.pallas_call(
        functools.partial(forward_body, names, group),
        grid=(rows // TILE,),
        in_specs=in_specs,
        out_specs=out_specs,
        out_shape=out_shape,
        scratch_shapes=scratch,
        compiler_params=params(48),
        cost_estimate=pl.CostEstimate(
            flops=2 * rows * size, bytes_accessed=24 * size, transcendentals=0
        ),
    )(*args)


def head_body(
    group,
    x_ref,
    target_ref,
    mask_ref,
    *refs,
):
    take = Taker(refs)
    arrays = take.refs[: group.parts]
    take(group.parts)
    gain_ref, dx_ref, dw_ref, dg_ref, loss_ref, acc_ref, whead_ref, sems = take(8)
    step = pl.program_id(0)
    me, core = place(group)
    made = copies(group, arrays, me, {"head": whead_ref}, sems, outward=False)

    @pl.when(step == 0)
    def _():
        acc_ref[...] = jnp.zeros_like(acc_ref)
        dg_ref[...] = jnp.zeros_like(dg_ref)
        loss_ref[...] = jnp.zeros_like(loss_ref)
        start_copies(group, made, core)
        wait_copies(made, ("head",))

    u, inverse = unit(x_ref[...])
    gain_row = gain_ref[0:1, :]
    final_in = (u * gain_row).astype(BF)
    predicted = dot_nn(final_in, whead_ref[...])
    target = target_ref[...]
    mask = mask_ref[...]
    loss = jnp.zeros((8, PMAX), F32)
    grads = []
    for q in range(NQ):
        level = (q + 1.0) / (NQ + 1)
        r = target - predicted[:, q * PMAX : (q + 1) * PMAX]
        a = r * (-1.0 / SMOOTH)
        e = jnp.exp(-jnp.abs(a))
        recip = 1.0 / (1.0 + e)
        sigmoid = jnp.where(a >= 0, recip, e * recip)
        softplus = jnp.maximum(a, 0.0) + jnp.log(1.0 + e)
        loss = loss + rows_to_eight((level * r + SMOOTH * softplus) * mask)
        grads.append(((sigmoid - level) * mask).astype(BF))
    loss_ref[...] += loss
    grad_pred = jnp.concatenate(grads, axis=1)
    acc_ref[...] += dot_tn(final_in, grad_pred)
    grad_x, grad_gain = rms_backward(u, inverse, gain_row, dot_nt(grad_pred, whead_ref[...]))
    dx_ref[...] = grad_x
    dg_ref[...] += grad_gain

    @pl.when(step == pl.num_programs(0) - 1)
    def _():
        dw_ref[...] = acc_ref[...].astype(BF)


def head(x, targets, mask, group, arrays, gain):
    rows = x.shape[0]
    return pl.pallas_call(
        functools.partial(head_body, group),
        grid=(rows // TILE,),
        in_specs=[
            rows_spec(D),
            rows_spec(PMAX),
            rows_spec(PMAX),
        ]
        + [any_spec()] * group.parts
        + [whole_spec(gain.shape)],
        out_specs=[
            rows_spec(D),
            whole_spec((D, HEADW)),
            whole_spec((8, D)),
            whole_spec((8, PMAX)),
        ],
        out_shape=[
            jax.ShapeDtypeStruct((rows, D), F32),
            jax.ShapeDtypeStruct((D, HEADW), BF),
            jax.ShapeDtypeStruct((8, D), F32),
            jax.ShapeDtypeStruct((8, PMAX), F32),
        ],
        scratch_shapes=[
            pltpu.VMEM((D, HEADW), F32),
            pltpu.VMEM((D, HEADW), BF),
            semaphores(group),
        ],
        compiler_params=params(40),
        cost_estimate=pl.CostEstimate(
            flops=6 * rows * D * HEADW, bytes_accessed=8 << 20, transcendentals=0
        ),
    )(x, targets, mask, *arrays, gain)


def backward_body(names, extra, group, out_group, *refs):
    first, attn, ffn = "in" in names, "qkv" in names, "gu" in names
    take = Taker(refs)
    dout_ref = take()
    if attn:
        x_ref, qkv_ref, prob_ref, mixed_ref = take(4)
    if ffn:
        mid_ref, gu_ref = take(2)
    concat_ref = take() if first else None
    extras = {extra: take()} if extra else {}
    arrays = take.refs[: group.parts]
    take(group.parts)
    gain_ref = take()
    if attn:
        cos_ref, sin_ref, code_ref = take(3)
    dx_ref = None if first else take()
    out_arrays = take.refs[: out_group.parts]
    take(out_group.parts)
    if attn:
        dg_attn, db_ref = take(2)
    if ffn:
        dg_ffn = take()
    loads = [n for n in names if n != "in"]
    w = take.named(loads)
    acc = take.named(names)
    grads = take.named(names)
    sems, out_sems = take(2)
    if attn:
        dqkv_ref = take()
    if ffn:
        dgu_ref = take()
    step = pl.program_id(0)
    me, core = place(group)
    made = copies(group, arrays, me, down_fields(w), sems, outward=False)
    sent = copies(
        out_group, out_arrays, me, {**down_fields(grads), **extras}, out_sems, outward=True
    )

    @pl.when(step == 0)
    def _():
        start_copies(group, made, core)
        for ref in acc.values():
            ref[...] = jnp.zeros_like(ref)
        if attn:
            dg_attn[...] = jnp.zeros_like(dg_attn)
            db_ref[...] = jnp.zeros_like(db_ref)
        if ffn:
            dg_ffn[...] = jnp.zeros_like(dg_ffn)
        wait_copies(made, list(made))

    dout = dout_ref[...]
    rows = dout.shape[0]
    grad_mid = dout
    if ffn:
        dout_low = dout.astype(BF)
        gate = gu_ref[:, :FF].astype(F32)
        up = gu_ref[:, FF:].astype(F32)
        sig = sigmoid_of(gate)
        silu = gate * sig
        acc["d"][...] += dot_tn((silu * up).astype(BF), dout_low)
        grad_hidden = dot_nt(dout_low, w["d"][...])
        dgu_ref[:, :FF] = (grad_hidden * up * (sig + silu * (1.0 - sig))).astype(BF)
        dgu_ref[:, FF:] = (grad_hidden * silu).astype(BF)
        u_mid, inverse_mid = unit(mid_ref[...])
        gain_mid = gain_ref[1:2, :]
        acc["gu"][...] += dot_tn((u_mid * gain_mid).astype(BF), dgu_ref[...])
        grad_mid, dgain_mid = rms_backward(
            u_mid, inverse_mid, gain_mid, dot_nt(dgu_ref[...], w["gu"][...])
        )
        dg_ffn[...] += dgain_mid
        grad_mid = grad_mid + dout
    grad_x = grad_mid
    if attn:
        grad_attn_low = grad_mid.astype(BF)
        acc["o"][...] += dot_tn(mixed_ref[...], grad_attn_low)
        grad_mixed = dot_nt(grad_attn_low, w["o"][...]).astype(BF)
        spots = [(b, p) for p in range(PAIRS) for b in range(rows // BUCKET)]
        dprobs = []
        for b, p in spots:
            here = slice(b * BUCKET, (b + 1) * BUCKET)
            dm2 = two_blocks(grad_mixed[here, p * LANES : (p + 1) * LANES])
            v = qkv_ref[here, 2 * D + p * LANES : 2 * D + (p + 1) * LANES]
            dprobs.append(dot_nt(v, dm2))
        dscores = []
        for (b, p), dprob in zip(spots, dprobs):
            prob = prob_ref[b * BUCKET : (b + 1) * BUCKET, p * LANES : (p + 1) * LANES].astype(F32)
            ds = prob * (dprob - jnp.sum(prob * dprob, axis=0, keepdims=True))
            dscores.append(ds.astype(BF))
        for p in range(PAIRS):
            other_sum = jnp.zeros((8, LANES), F32)
            same_sum = jnp.zeros((8, LANES), F32)
            for b in range(rows // BUCKET):
                ds = dscores[p * (rows // BUCKET) + b].astype(F32)
                same = code_ref[b * BUCKET : (b + 1) * BUCKET, :] > 0.5
                same_sum = same_sum + rows_to_eight(jnp.where(same, ds, 0.0))
                other_sum = other_sum + rows_to_eight(jnp.where(same, 0.0, ds))
            db_ref[p * 8 : (p + 1) * 8, :] += other_sum
            db_ref[(PAIRS + p) * 8 : (PAIRS + p + 1) * 8, :] += same_sum
        for (b, p), ds in zip(spots, dscores):
            here = slice(b * BUCKET, (b + 1) * BUCKET)
            cols = slice(p * LANES, (p + 1) * LANES)
            kcols = slice(D + p * LANES, D + (p + 1) * LANES)
            vcols = slice(2 * D + p * LANES, 2 * D + (p + 1) * LANES)
            cos = cos_ref[here, :] * HD ** (-0.5)
            sin = sin_ref[here, :] * HD ** (-0.5)
            dm2 = two_blocks(grad_mixed[here, cols])
            dq = fold_blocks(dot_tn(ds, qkv_ref[here, kcols]))
            dk = dot_nn(ds, two_blocks(qkv_ref[here, cols]))
            dv = dot_nn(prob_ref[here, cols], dm2)
            dqkv_ref[here, cols] = (dq * cos + swap_halves(dq * sin)).astype(BF)
            dqkv_ref[here, kcols] = (dk * cos + swap_halves(dk * sin)).astype(BF)
            dqkv_ref[here, vcols] = dv.astype(BF)
        u, inverse = unit(x_ref[...])
        gain_row = gain_ref[0:1, :]
        acc["qkv"][...] += dot_tn((u * gain_row).astype(BF), dqkv_ref[...])
        grad_x, dgain = rms_backward(u, inverse, gain_row, dot_nt(dqkv_ref[...], w["qkv"][...]))
        dg_attn[...] += dgain
        grad_x = grad_x + grad_mid
    if first:
        acc["in"][...] += dot_tn(grad_x.astype(BF), concat_ref[...])
    else:
        dx_ref[...] = grad_x

    @pl.when(step == pl.num_programs(0) - 1)
    def _():
        for name in names:
            grads[name][...] = acc[name][...].astype(BF)
        start_copies(out_group, sent, core)
        wait_copies(sent, list(sent))


def backward_layer(names, dout, saved, concat, extra, group, arrays, out_group, gain_pair, tables):
    first, attn, ffn = "in" in names, "qkv" in names, "gu" in names
    rows = dout.shape[0]
    args = [dout, *saved] + ([concat] if first else [])
    in_specs = [rows_spec(a.shape[1]) for a in args]
    if extra:
        args.append(extra[1])
        in_specs.append(whole_spec(extra[1].shape))
    args += [*arrays, gain_pair]
    in_specs += [any_spec()] * group.parts + [whole_spec(gain_pair.shape)]
    if attn:
        args += list(tables)
        in_specs += [rows_spec(LANES)] * 3
    out_specs, out_shape = [], []
    if not first:
        out_specs.append(rows_spec(D))
        out_shape.append(jax.ShapeDtypeStruct((rows, D), F32))
    slots = (out_group.shards, out_group.rows, out_group.width)
    out_specs += [any_spec()] * out_group.parts
    out_shape += [jax.ShapeDtypeStruct(slots, BF)] * out_group.parts
    small = ([(8, D), (48, LANES)] if attn else []) + ([(8, D)] if ffn else [])
    out_specs += [whole_spec(shape) for shape in small]
    out_shape += [jax.ShapeDtypeStruct(shape, F32) for shape in small]
    scratch = [pltpu.VMEM(WEIGHTS[n], BF) for n in names if n != "in"]
    scratch += [pltpu.VMEM(WEIGHTS[n], F32) for n in names]
    scratch += [pltpu.VMEM(WEIGHTS[n], BF) for n in names]
    scratch += [semaphores(group), semaphores(out_group)]
    scratch += [pltpu.VMEM((TILE, QKV), BF)] if attn else []
    scratch += [pltpu.VMEM((TILE, 2 * FF), BF)] if ffn else []
    size = sum(WEIGHTS[n][0] * WEIGHTS[n][1] for n in names)
    got = pl.pallas_call(
        functools.partial(backward_body, names, extra[0] if extra else None, group, out_group),
        grid=(rows // TILE,),
        in_specs=in_specs,
        out_specs=out_specs,
        out_shape=out_shape,
        scratch_shapes=scratch,
        compiler_params=params(56),
        cost_estimate=pl.CostEstimate(
            flops=4 * rows * size, bytes_accessed=48 * size, transcendentals=0
        ),
    )(*args)
    got = list(got)
    grad = None if first else got.pop(0)
    return grad, got[: out_group.parts], got[out_group.parts :]


def partners(sizes, fsdp_mask, dp_mask):
    fsdp, dp = sizes
    return [
        (f * dp + d, (f ^ fsdp_mask) * dp + (d ^ dp_mask)) for f in range(fsdp) for d in range(dp)
    ]


def slot_of(offset, masks):
    slot = 0
    for bit, mask in enumerate(masks):
        slot = slot + jnp.where((offset & mask) != 0, 1 << bit, 0)
    return slot


def swap(x, sizes, fsdp_mask, dp_mask):
    return lax.ppermute(x, AXES, partners(sizes, fsdp_mask, dp_mask))


def reorder(slots, masks):
    me = lax.axis_index("fsdp")
    return jnp.stack(
        [
            lax.dynamic_index_in_dim(slots, slot_of(me ^ j, masks), 0, keepdims=False)
            for j in range(slots.shape[0])
        ]
    )


class Gather:
    def __init__(self, halves, sizes):
        core = lax.axis_index("dp") & 1
        self.sizes = sizes
        self.mine = jnp.where(core == 0, halves[0], halves[1])[None]
        self.masks = masks_of(sizes[0])
        self.got = None

    def move(self, after=None):
        mine = self.land()
        if after is not None:
            mine, after.got = lax.optimization_barrier((mine, after.got))
        self.mine = mine
        self.got = swap(mine, self.sizes, self.masks.pop(0), 0)

    def land(self):
        if self.got is not None:
            self.mine = jnp.concatenate([self.mine, self.got], axis=0)
            self.got = None
        return self.mine

    def hold(self, x):
        x, self.got = lax.optimization_barrier((x, self.got))
        return x

    def pair(self):
        mine = self.land()
        return mine, swap(mine, self.sizes, 0, 1)


def by_core(mine, other):
    core = lax.axis_index("dp") & 1
    return jnp.where(core == 0, mine, other), jnp.where(core == 0, other, mine)


def add(a, b):
    return (a.astype(F32) + b.astype(F32)).astype(BF)


def to_slots(shards, masks):
    me = lax.axis_index("fsdp")
    slots = [None] * shards.shape[0]
    for v in range(shards.shape[0]):
        slots[slot_index(v, masks)] = lax.dynamic_index_in_dim(shards, me ^ v, 0, keepdims=False)
    return jnp.stack(slots)


class Scatter:
    def __init__(self, keep, give, sizes):
        self.sizes = sizes
        self.keep = keep
        self.got = swap(give, sizes, 0, 1)
        self.moves = [(mask, 0) for mask in reversed(masks_of(sizes[0]))]
        dp_mask = 2
        while dp_mask < sizes[1]:
            self.moves.append((0, dp_mask))
            dp_mask *= 2

    def ready(self):
        if self.moves and self.moves[0][0]:
            half = self.keep.shape[0] // 2
            self.away = add(self.keep[half:], self.got[half:])
            self.keep = add(self.keep[:half], self.got[:half])
        else:
            self.keep = add(self.keep, self.got)
            self.away = self.keep

    def move(self):
        self.got = swap(self.away, self.sizes, *self.moves.pop(0))

    def total(self):
        return add(self.keep, self.got)[0]


def hold(x, *scatters):
    for one in scatters:
        one.ready()
    held = lax.optimization_barrier((x, [(one.keep, one.away) for one in scatters]))
    for one, (keep, away) in zip(scatters, held[1]):
        one.keep, one.away = keep, away
        one.move()
    return held[0]


def after_landing(x, scatters):
    x, landed = lax.optimization_barrier((x, [one.got for one in scatters]))
    for one, got in zip(scatters, landed):
        one.got = got
    return x


def pad_rows(x, rows):
    return jnp.pad(x, ((0, 0),) * (x.ndim - 2) + ((0, rows - x.shape[-2]), (0, 0)))


def to_whole(group, whole, arrays, sizes):
    if group.parts == 2:
        masks = masks_of(sizes[0])
        arrays = [reorder(a, masks) for a in by_core(*arrays)]
    fields = group.unpack(arrays)
    fields = {n: p.reshape(1, p.shape[0] * p.shape[1], p.shape[2]) for n, p in fields.items()}
    return whole.pack(fields)


def from_whole(group, whole, arrays, sizes):
    fsdp = sizes[0]
    fields = whole.unpack(arrays)
    fields = {n: p.reshape(fsdp, p.shape[1] // fsdp, p.shape[2]) for n, p in fields.items()}
    arrays = group.pack(fields)
    if group.parts == 1:
        return arrays
    masks = masks_of(fsdp)
    return by_core(*[to_slots(a, masks) for a in arrays])


def rotary_tables(time_ids):
    frequency = THETA ** (-2.0 * jnp.arange(HD // 2, dtype=F32) / HD)
    phase = time_ids.astype(F32)[:, None] * frequency[None, :]
    cos, sin = jnp.cos(phase), jnp.sin(phase)
    return jnp.concatenate([cos] * 4, axis=1), jnp.concatenate([-sin, sin, -sin, sin], axis=1)


def live_slots(lengths):
    return jnp.arange(BUCKET, dtype=jnp.int32)[None, :] < lengths[:, None]


def target_mask(size_ids, lengths):
    widths = jnp.where(live_slots(lengths).reshape(size_ids.shape), PMAX >> (4 - size_ids), 0)
    return (jnp.arange(PMAX, dtype=jnp.int32)[None, :] < widths[:, None]).astype(F32)


def code_table(variate_ids, lengths):
    variates = variate_ids.reshape(-1, BUCKET)
    same = (variates[:, :, None] == variates[:, None, :]).astype(F32)
    code = jnp.where(live_slots(lengths)[:, :, None], same, -1.0).reshape(-1, BUCKET)
    return jnp.concatenate([code, code], axis=1)


def patch_concat(patches, size_ids):
    pieces = []
    for size_id in range(5):
        span = PMAX >> 4 - size_id
        chosen = (size_ids == size_id)[:, None]
        pieces.append(jnp.where(chosen, patches[:, :span], jnp.zeros((), BF)))
    pieces.append(jnp.zeros((patches.shape[0], 2 * PMAX - IN_CAT), BF))
    return jnp.concatenate(pieces, axis=1)


def adam_update(master, clipped, first_old, second_old, matrix):
    first_new = BETA_ONE * first_old + (1.0 - BETA_ONE) * clipped
    second_new = BETA_TWO * second_old + (1.0 - BETA_TWO) * clipped * clipped
    first_hat = first_new / (1.0 - BETA_ONE**STEP_NUM)
    second_hat = second_new / (1.0 - BETA_TWO**STEP_NUM)
    direction = first_hat / (jnp.sqrt(second_hat) + ADAM_EPS)
    if matrix:
        master_new = master - RATE_MATRIX * (direction + WEIGHT_DECAY * master)
    else:
        master_new = master - RATE_GAIN * direction
    return (master_new, first_new, second_new)


def sum_moves(sizes, dp_from=1):
    moves = []
    dp_mask = dp_from
    while dp_mask < sizes[1]:
        moves.append((0, dp_mask))
        dp_mask *= 2
    return moves + [(mask, 0) for mask in masks_of(sizes[0])]


def per_device(sizes, *args):
    patches, targets, size_ids, time_ids, variate_ids, lengths = args[:6]
    masters = args[6:14]
    firsts = args[14:22]
    seconds = args[22:30]
    w_in, w_qkv, w_o, w_gu, w_down, w_head, gains, var_bias = masters
    own = w_head.shape[0]
    down_rows = w_down.shape[1]
    direct = own % 16 == 0 and down_rows % 16 == 0
    attn_fields = [("qkv", QKV), ("o", D)]
    ffn_fields = [("d0", D), ("d1", D), ("gu", 2 * FF), ("d2", D)]
    plan = [
        (("in",) + ATTN, [("in", 2 * PMAX)] + attn_fields),
        (FFN, ffn_fields),
        (ATTN + FFN, attn_fields + ffn_fields),
        (ATTN + FFN, attn_fields + ffn_fields + [("head", HEADW)]),
    ]
    layers = [0, 0, 1, 2]
    count = len(plan)
    def groups_of(fields, parts):
        many = [Group(f, p, sizes[0], own, down_rows) for f, p in zip(fields, parts)]
        if direct:
            return many, many
        return many, [Group(f, p, 1, D, FF) for f, p in zip(fields, parts)]

    fields = [f for _, f in plan]
    groups, wholes = groups_of(fields, [2] * count)

    in_rows = jnp.concatenate(
        [w_in.T, gains.T, jnp.zeros((own, 2 * PMAX - IN_CAT - NGAIN), F32)], axis=1
    ).astype(BF)
    def packed(n, stacks, head_w=None):
        fields = {m: w[layers[n]].astype(BF) for m, w in zip(("qkv", "o", "gu", "d"), stacks)}
        if n == count - 1:
            fields["head"] = head_w.astype(BF)
        return groups[n].pack({**fields, "in": in_rows})

    stacks = (w_qkv, w_o, w_gu, w_down)
    gathers = [Gather(packed(0, stacks), sizes)]
    steps = len(gathers[0].masks)
    gathers[0].move()
    stacks, head_w, time_ids = gathers[0].hold((stacks, w_head, time_ids))
    gathers += [Gather(packed(n, stacks, head_w), sizes) for n in range(1, count)]
    cos, sin = rotary_tables(time_ids)
    for _ in range(steps - 2):
        gathers[0].move()
    early = (patches, size_ids, variate_ids, lengths)
    early, gathers[1].mine = gathers[0].hold((early, gathers[1].mine))
    patches, size_ids, variate_ids, lengths = early
    gathers[0].move()
    for _ in range(steps - 2):
        gathers[1].move()
    gathers[2].move(gathers[1])
    gathers[1].move()
    gathers[3].move(gathers[2])
    for _ in range(steps - 2):
        gathers[2].move()
    gathers[1].move()
    for _ in range(steps - 3):
        gathers[3].move()

    def arrived(n):
        arrays = gathers[n].pair()
        return arrays if direct else to_whole(groups[n], wholes[n], arrays, sizes)

    tables = (cos, sin, code_table(variate_ids, lengths))
    concat = patch_concat(patches, size_ids)
    bias_lanes = jnp.repeat(var_bias, HD, axis=2).reshape(L, 2, PAIRS, LANES)
    bias_lanes = jnp.pad(bias_lanes, ((0, 0), (0, 0), (0, 8 - PAIRS), (0, 0)))
    bias_lanes = bias_lanes.reshape(L, 16, LANES)

    stream = concat
    kept = [None] * count
    loaded = []
    gain_pairs = [None] * (L + 1)
    for n, layer in enumerate(layers):
        names = plan[n][0]
        loaded.append(arrived(n))
        for one in gathers[n + 1 :]:
            if n and one.masks:
                one.move()
        got = list(
            forward_layer(
                stream, names, wholes[n], loaded[n], gain_pairs[layer], bias_lanes[layer], tables
            )
        )
        if n == 0:
            stream, found = got[:2]
            got = got[2:]
            gain_pairs = [found[0:2], found[2:4], found[4:6], found[6:8]]
            kept[0] = [stream, *got[:3]]
            stream = got[3]
        elif n == 1:
            kept[1] = [stream, got[1]]
            stream = got[0]
        else:
            kept[n] = [stream, *got[:4], got[5]]
            stream = got[4]
        for one in gathers[n + 1 :]:
            stream = one.hold(stream)
        if n == 0:
            stream, size_ids, lengths = lax.optimization_barrier((stream, size_ids, lengths))
            mask = target_mask(size_ids, lengths)
            live = jnp.sum(mask)
    grad, head_grad, gain_grad, loss = head(
        stream, targets, mask, wholes[-1], loaded[-1], gain_pairs[L]
    )
    raw = [gain_grad, loss]
    totals = [None] * count
    for n in reversed(range(count)):
        names = plan[n][0]
        layer = layers[n]
        grad, arrays, small = backward_layer(
            names,
            grad,
            kept[n],
            concat,
            ("head", head_grad) if n == count - 1 else None,
            wholes[n],
            loaded[n],
            wholes[n],
            gain_pairs[layer],
            tables,
        )
        raw += small
        if not direct:
            arrays = from_whole(groups[n], wholes[n], arrays, sizes)
        keep, give = arrays
        flying = totals[n + 1 :]
        give = after_landing(give, flying)
        totals[n] = Scatter(keep, give, sizes)
        if n:
            grad = hold(grad, totals[n], *flying)

    gain_grad, loss, *raw = raw
    gain_grads, bias_grads = {2 * L: gain_grad}, [None] * L
    for n in reversed(range(count)):
        names = plan[n][0]
        layer = layers[n]
        if "qkv" in names:
            gain_grads[2 * layer] = raw.pop(0)
            bias_grads[layer] = raw.pop(0).reshape(2, PAIRS, 8, 2, HD)
        if "gu" in names:
            gain_grads[2 * layer + 1] = raw.pop(0)
    gain_grads = [jnp.sum(gain_grads[g], axis=0) for g in range(NGAIN)]
    bias_grads = jnp.sum(jnp.stack(bias_grads), axis=(3, 5)).reshape(L, 2, H)

    small = jnp.concatenate([jnp.sum(loss)[None], live[None], bias_grads.reshape(-1)])
    small = jnp.pad(small, (0, D - small.shape[0]))
    rows = jnp.stack(gain_grads + [small])
    orders = sum_moves(sizes)
    rows = rows + swap(rows, sizes, *orders.pop(0))
    own_parts = [None] * count
    active = list(range(count))
    while active:
        for n in active:
            if not totals[n].moves:
                own_parts[n] = totals[n].total()
        active = [n for n in active if own_parts[n] is None]
        if not active:
            break
        moving = [totals[n] for n in active]
        rows = hold(rows, *moving)
        if orders:
            rows = rows + swap(rows, sizes, *orders.pop(0))
    while orders:
        rows = rows + swap(rows, sizes, *orders.pop(0))
    loss_sum, total_count = rows[NGAIN, 0], rows[NGAIN, 1]
    inverse_count = 1.0 / total_count
    bias_grad = rows[NGAIN, 2 : 2 + var_bias.size].reshape(var_bias.shape) * inverse_count
    gain_all = rows[:NGAIN]
    gain_own = lax.dynamic_slice_in_dim(gain_all, lax.axis_index("fsdp") * own, own, axis=1)

    squares = jnp.zeros((1, 1), F32)
    for n in range(count):
        squares = squares + groups[n].squares(own_parts[n])
    for fsdp_mask, dp_mask in sum_moves(sizes):
        if dp_mask < 2:
            squares = squares + swap(squares, sizes, fsdp_mask, dp_mask)
    squares = squares[0, 0]

    pieces = []
    for n in range(count):
        low, high = by_core(own_parts[n], swap(own_parts[n], sizes, 0, 1))
        pieces.append(groups[n].unpack((low, high)))
    in_piece = pieces[0]["in"][:, :IN_CAT]
    head_piece = pieces[-1]["head"]
    matrices = [[piece[m] for piece in pieces if m in piece] for m in ("qkv", "o", "gu", "d")]
    squares = squares + jnp.sum(jnp.square(gain_all))
    grad_norm = jnp.sqrt(
        squares * (inverse_count * inverse_count) + jnp.sum(bias_grad * bias_grad)
    )
    factor = jnp.minimum(1.0, CLIP_NORM / grad_norm)
    scale = factor * inverse_count

    gradients = [in_piece.T] + [jnp.stack(m) for m in matrices] + [head_piece, gain_own]
    clipped = [g.astype(F32) * scale for g in gradients] + [bias_grad * factor]
    fresh = [
        adam_update(masters[m], clipped[m], firsts[m], seconds[m], m < 6) for m in range(8)
    ]
    return (
        (loss_sum, total_count, grad_norm)
        + tuple(f[0] for f in fresh)
        + tuple(f[1] for f in fresh)
        + tuple(f[2] for f in fresh)
    )


def solution(mesh):
    sizes = (mesh.shape["fsdp"], mesh.shape["dp"])
    tokens = P(("fsdp", "dp"))
    tokens_two = P(("fsdp", "dp"), None)
    columns = P(None, "fsdp")
    stacked = P(None, "fsdp", None)
    states = (columns, stacked, stacked, stacked, stacked, P("fsdp", None), columns, P())
    in_specs = (tokens_two, tokens_two, tokens, tokens, tokens, tokens) + states * 3
    out_specs = (P(), P(), P()) + states * 3
    return jax.shard_map(
        functools.partial(per_device, sizes),
        mesh=mesh,
        in_specs=in_specs,
        out_specs=out_specs,
        check_vma=False,
    )
```

```python
import functools

import jax
import jax.numpy as jnp
from jax import lax
from jax.experimental import pallas as pl
from jax.experimental.pallas import tpu as pltpu
from jax.sharding import PartitionSpec as P

D = 384
H = 6
HD = 64
FF = 1024
PMAX = 128
NQ = 9
BUCKET = 64
L = 3
STEP_NUM = 10
IN_CAT = 248
NGAIN = 7
QKV = 3 * D
HEADW = NQ * PMAX
PAIRS = H // 2
LANES = 2 * HD

TILE = 256
FORWARD_TILE = 512

EPS_NORM = 1e-05
SMOOTH = 0.5
THETA = 10000.0
MASKED_SCORE = -1e30
CLIP_NORM = 0.001
BETA_ONE = 0.9
BETA_TWO = 0.95
ADAM_EPS = 1e-08
WEIGHT_DECAY = 0.1
RATE_MATRIX = 0.15
RATE_GAIN = 0.8

BF = jnp.bfloat16
F32 = jnp.float32
AXES = ("fsdp", "dp")


def dot_nn(a, b):
    return lax.dot_general(a, b, (((1,), (0,)), ((), ())), preferred_element_type=F32)


def dot_nt(a, b):
    return lax.dot_general(a, b, (((1,), (1,)), ((), ())), preferred_element_type=F32)


def dot_tn(a, b):
    return lax.dot_general(a, b, (((0,), (0,)), ((), ())), preferred_element_type=F32)


def unit(x):
    inverse = lax.rsqrt(jnp.mean(x * x, axis=-1, keepdims=True) + EPS_NORM)
    return x * inverse, inverse


def rms_backward(u, inverse, gain_row, grad):
    grad_unit = grad * gain_row
    grad_x = inverse * (grad_unit - u * jnp.mean(grad_unit * u, axis=-1, keepdims=True))
    return grad_x, rows_to_eight(grad * u)


def rows_to_eight(x):
    return jnp.sum(x.reshape(x.shape[0] // 8, 8, x.shape[1]), axis=0)


def lane_of(shape):
    return lax.broadcasted_iota(jnp.int32, shape, len(shape) - 1)


def swap_halves(x):
    lane = lane_of(x.shape)
    return jnp.where((lane & 32) == 0, pltpu.roll(x, 96, 1), pltpu.roll(x, 32, 1))


def low_lanes(shape):
    return lane_of(shape) < HD


def two_blocks(x):
    keep = low_lanes(x.shape)
    zero = jnp.zeros_like(x)
    return jnp.concatenate([jnp.where(keep, x, zero), jnp.where(keep, zero, x)], axis=0)


def fold_blocks(x):
    return jnp.where(low_lanes((BUCKET, LANES)), x[:BUCKET], x[BUCKET:])


def sigmoid_of(x):
    return 0.5 * jnp.tanh(0.5 * x) + 0.5


class Group:
    def __init__(self, fields, parts, shards, rows, down_rows):
        self.parts, self.shards, self.rows, self.down_rows = parts, shards, rows, down_rows
        used = sum(width for _, width in fields)
        self.width = -(-used // (parts * LANES)) * LANES
        self.pad = parts * self.width - used
        self.fields = fields
        self.pieces = []
        at = 0
        for name, width in fields:
            done = 0
            while done < width:
                part = (at + done) // self.width
                take = min(width - done, (part + 1) * self.width - at - done)
                self.pieces.append((part, at + done - part * self.width, name, done, take))
                done += take
            at += width
        masks = masks_of(shards)
        self.slots = [slot_index(v, masks) if parts > 1 else v for v in range(shards)]

    def row_span(self, name):
        if name[0] == "d":
            first = int(name[1]) * self.rows
            return first, min(self.rows, self.down_rows - first), self.down_rows
        return 0, self.rows, self.rows

    def pack(self, fields):
        fields = dict(fields)
        if "d" in fields:
            down = fields.pop("d")
            for i in range(3):
                part = down[..., i * self.rows : (i + 1) * self.rows, :]
                fields[f"d{i}"] = pad_rows(part, self.rows)
        parts = [[] for _ in range(self.parts)]
        for part, _, name, start, width in self.pieces:
            parts[part].append(fields[name][..., start : start + width])
        if self.pad:
            like = parts[-1][0]
            parts[-1].append(jnp.zeros(like.shape[:-1] + (self.pad,), like.dtype))
        return tuple(jnp.concatenate(p, axis=-1) for p in parts)

    def unpack(self, parts):
        found = {}
        for part, at, name, _, width in self.pieces:
            got = parts[part][..., at : at + width]
            found[name] = jnp.concatenate([found[name], got], axis=-1) if name in found else got
        if "d0" in found:
            downs = [found.pop(f"d{i}") for i in range(3)]
            downs[2] = downs[2][..., : self.row_span("d2")[1], :]
            found["d"] = jnp.concatenate(downs, axis=-2)
        return found


    def squares(self, own):
        row = lax.broadcasted_iota(jnp.int32, own.shape, 0)
        col = lax.broadcasted_iota(jnp.int32, own.shape, 1)
        used = [jnp.zeros(own.shape, bool)] * 2
        for part, at, name, _, width in self.pieces:
            inside = (col >= at) & (col < at + width) & (row < self.row_span(name)[1])
            used[part] = used[part] | inside
        core = lax.axis_index("dp") & 1
        used = (used[0] & (core == 0)) | (used[1] & (core == 1))
        return jnp.sum(jnp.where(used, jnp.square(own.astype(F32)), 0.0)).reshape(1, 1)


def place(group):
    if group.shards == 1:
        return 0, 0
    return lax.axis_index("fsdp"), lax.axis_index("dp") & (group.parts - 1)


def copies(group, arrays, me, targets, sems, outward):
    made = {}
    for n, (part, at, name, start, width) in enumerate(group.pieces):
        if name not in targets:
            continue
        first, count, stride = group.row_span(name)
        for v in range(group.shards):
            owner = v if group.parts == 1 else me ^ v
            row = owner * stride + first
            if not isinstance(row, int):
                row = pl.multiple_of(row, 16)
            whole = targets[name].at[pl.ds(row, count), pl.ds(start, width)]
            slots = [
                a.at[group.slots[v], pl.ds(0, count), pl.ds(at, width)] for a in arrays
            ]
            ends = [(whole, slot) if outward else (slot, whole) for slot in slots]
            pair = [functools.partial(pltpu.make_async_copy, a, b, sems.at[n, v]) for a, b in ends]
            made.setdefault(name, []).append((part, pair))
    return made


def start_copies(group, made, core):
    def go(which):
        for items in made.values():
            for part, pair in items:
                pair[part ^ which]().start()

    if group.shards == 1 or group.parts == 1:
        go(0)
    else:
        for which in range(group.parts):
            pl.when(core == which)(functools.partial(go, which))


def wait_copies(made, names):
    for name in names:
        for _, pair in made.get(name, []):
            pair[0]().wait()


def slot_index(v, masks):
    return sum((1 << bit) for bit, mask in enumerate(masks) if v & mask)


def masks_of(size):
    masks = []
    size //= 2
    while size:
        masks.append(size)
        size //= 2
    return masks


def any_spec():
    return pl.BlockSpec(memory_space=pl.ANY)


WEIGHTS = {"in": (D, 2 * PMAX), "qkv": (D, QKV), "o": (D, D), "gu": (D, 2 * FF), "d": (FF, D)}


def semaphores(group):
    return pltpu.SemaphoreType.DMA((len(group.pieces), group.shards))


class Taker:
    def __init__(self, refs):
        self.refs = list(refs)

    def __call__(self, count=1):
        taken, self.refs = self.refs[:count], self.refs[count:]
        return taken[0] if count == 1 else taken

    def named(self, names):
        return dict(zip(names, [self() for _ in names]))


def down_fields(targets):
    targets = dict(targets)
    if "d" in targets:
        down = targets.pop("d")
        targets.update(d0=down, d1=down, d2=down)
    return targets


ATTN, FFN = ("qkv", "o"), ("gu", "d")


def forward_body(names, group, *refs):
    first, attn, ffn = "in" in names, "qkv" in names, "gu" in names
    take = Taker(refs)
    x_ref = take()
    arrays = take.refs[: group.parts]
    take(group.parts)
    gain_ref = None if first else take()
    if attn:
        bias_ref, cos_ref, sin_ref, code_ref = take(4)
    if first:
        base_ref, rows_ref = take(2)
    if attn:
        qkv_ref, prob_ref, mixed_ref, mid_ref = take(4)
    if ffn:
        out_ref, gu_ref = take(2)
    w = take.named(names)
    sems = take()
    if first:
        gain_ref = take()
    me, core = place(group)
    made = copies(group, arrays, me, down_fields(w), sems, outward=False)
    opening = pl.program_id(0) == 0
    early = [n for n in made if n in ("in", "qkv")]
    late = [n for n in made if n not in early]

    @pl.when(opening)
    def _():
        start_copies(group, made, core)
        wait_copies(made, early)
        if first:
            turned = w["in"][:, PMAX:].astype(F32).T
            gain_ref[...] = turned[IN_CAT - PMAX : IN_CAT - PMAX + 8, :]
            rows_ref[...] = gain_ref[...]

    def rest():
        pl.when(opening)(functools.partial(wait_copies, made, late))

    if attn:
        if first:
            stream = dot_nt(x_ref[...], w["in"][...])
            base_ref[...] = stream
        else:
            stream = x_ref[...]
        rows = stream.shape[0]
        normed = (unit(stream)[0] * gain_ref[0:1, :]).astype(BF)
        cos = cos_ref[...]
        sin = sin_ref[...]
        qk = dot_nn(normed, w["qkv"][:, : 2 * D])
        for j in range(2 * PAIRS):
            cols = slice(j * LANES, (j + 1) * LANES)
            qkv_ref[:, cols] = (qk[:, cols] * cos + swap_halves(qk[:, cols]) * sin).astype(BF)
        qkv_ref[:, 2 * D :] = dot_nn(normed, w["qkv"][:, 2 * D :]).astype(BF)
        spots = [(b, p) for b in range(rows // BUCKET) for p in range(PAIRS)]
        scores = []
        for b, p in spots:
            here = slice(b * BUCKET, (b + 1) * BUCKET)
            q = qkv_ref[here, p * LANES : (p + 1) * LANES]
            k = qkv_ref[here, D + p * LANES : D + (p + 1) * LANES]
            scores.append(dot_nt(k, two_blocks(q)))
        probs = []
        for (b, p), score in zip(spots, scores):
            code = code_ref[b * BUCKET : (b + 1) * BUCKET, :]
            bias = jnp.where(code > 0.5, bias_ref[p + 8 : p + 9, :], bias_ref[p : p + 1, :])
            score = jnp.where(code < -0.5, MASKED_SCORE, score * HD ** (-0.5) + bias)
            e = jnp.exp(score - jnp.max(score, axis=0, keepdims=True))
            probs.append((e * (1.0 / jnp.sum(e, axis=0, keepdims=True))).astype(BF))
        for (b, p), prob in zip(spots, probs):
            here = slice(b * BUCKET, (b + 1) * BUCKET)
            cols = slice(p * LANES, (p + 1) * LANES)
            v = qkv_ref[here, 2 * D + p * LANES : 2 * D + (p + 1) * LANES]
            prob_ref[here, cols] = prob
            mixed_ref[here, cols] = fold_blocks(dot_tn(prob, v)).astype(BF)
        rest()
        middle = stream + dot_nn(mixed_ref[...], w["o"][...])
        mid_ref[...] = middle
    else:
        rest()
        middle = x_ref[...]
    if ffn:
        ffn_in = (unit(middle)[0] * gain_ref[1:2, :]).astype(BF)
        gate_up = dot_nn(ffn_in, w["gu"][...])
        gu_ref[...] = gate_up.astype(BF)
        gate = gate_up[:, :FF]
        hidden = (gate * sigmoid_of(gate) * gate_up[:, FF:]).astype(BF)
        out_ref[...] = middle + dot_nn(hidden, w["d"][...])


def rows_spec(width, tile=TILE):
    return pl.BlockSpec((tile, width), lambda i: (i, 0))


def whole_spec(shape):
    zeros = (0,) * len(shape)
    return pl.BlockSpec(shape, lambda i: zeros)


def params(limit):
    return pltpu.CompilerParams(
        dimension_semantics=("arbitrary",), vmem_limit_bytes=limit * 1024 * 1024
    )


def forward_layer(x, names, group, arrays, gain_pair, bias_rows, tables):
    first, attn, ffn = "in" in names, "qkv" in names, "gu" in names
    rows = x.shape[0]
    args = [x, *arrays]
    in_specs = [rows_spec(x.shape[1], FORWARD_TILE)] + [any_spec()] * group.parts
    if not first:
        args.append(gain_pair)
        in_specs.append(whole_spec(gain_pair.shape))
    if attn:
        args += [bias_rows, *tables]
        in_specs += [whole_spec(bias_rows.shape)] + [rows_spec(LANES, FORWARD_TILE)] * 3
    outs = [(D, F32)] if first else []
    outs += [(QKV, BF), (D, BF), (D, BF), (D, F32)] if attn else []
    outs += [(D, F32), (2 * FF, BF)] if ffn else []
    out_specs = [rows_spec(w, FORWARD_TILE) for w, _ in outs]
    out_shape = [jax.ShapeDtypeStruct((rows, w), t) for w, t in outs]
    scratch = [pltpu.VMEM(WEIGHTS[n], BF) for n in names] + [semaphores(group)]
    if first:
        out_specs.insert(1, whole_spec((8, D)))
        out_shape.insert(1, jax.ShapeDtypeStruct((8, D), F32))
        scratch.append(pltpu.VMEM((8, D), F32))
    size = sum(WEIGHTS[n][0] * WEIGHTS[n][1] for n in names)
    return pl.pallas_call(
        functools.partial(forward_body, names, group),
        grid=(rows // FORWARD_TILE,),
        in_specs=in_specs,
        out_specs=out_specs,
        out_shape=out_shape,
        scratch_shapes=scratch,
        compiler_params=params(48),
        cost_estimate=pl.CostEstimate(
            flops=2 * rows * size, bytes_accessed=24 * size, transcendentals=0
        ),
    )(*args)


def head_body(
    group,
    x_ref,
    target_ref,
    mask_ref,
    *refs,
):
    take = Taker(refs)
    arrays = take.refs[: group.parts]
    take(group.parts)
    gain_ref, dx_ref, dw_ref, dg_ref, loss_ref, acc_ref, whead_ref, sems = take(8)
    step = pl.program_id(0)
    me, core = place(group)
    made = copies(group, arrays, me, {"head": whead_ref}, sems, outward=False)

    @pl.when(step == 0)
    def _():
        acc_ref[...] = jnp.zeros_like(acc_ref)
        dg_ref[...] = jnp.zeros_like(dg_ref)
        loss_ref[...] = jnp.zeros_like(loss_ref)
        start_copies(group, made, core)
        wait_copies(made, ("head",))

    u, inverse = unit(x_ref[...])
    gain_row = gain_ref[0:1, :]
    final_in = (u * gain_row).astype(BF)
    predicted = dot_nn(final_in, whead_ref[...])
    target = target_ref[...]
    mask = mask_ref[...]
    loss = jnp.zeros((8, PMAX), F32)
    grads = []
    for q in range(NQ):
        level = (q + 1.0) / (NQ + 1)
        r = target - predicted[:, q * PMAX : (q + 1) * PMAX]
        a = r * (-1.0 / SMOOTH)
        e = jnp.exp(-jnp.abs(a))
        recip = 1.0 / (1.0 + e)
        sigmoid = jnp.where(a >= 0, recip, e * recip)
        softplus = jnp.maximum(a, 0.0) + jnp.log(1.0 + e)
        loss = loss + rows_to_eight((level * r + SMOOTH * softplus) * mask)
        grads.append(((sigmoid - level) * mask).astype(BF))
    loss_ref[...] += loss
    grad_pred = jnp.concatenate(grads, axis=1)
    acc_ref[...] += dot_tn(final_in, grad_pred)
    grad_x, grad_gain = rms_backward(u, inverse, gain_row, dot_nt(grad_pred, whead_ref[...]))
    dx_ref[...] = grad_x
    dg_ref[...] += grad_gain

    @pl.when(step == pl.num_programs(0) - 1)
    def _():
        dw_ref[...] = acc_ref[...].astype(BF)


def head(x, targets, mask, group, arrays, gain):
    rows = x.shape[0]
    return pl.pallas_call(
        functools.partial(head_body, group),
        grid=(rows // TILE,),
        in_specs=[
            rows_spec(D),
            rows_spec(PMAX),
            rows_spec(PMAX),
        ]
        + [any_spec()] * group.parts
        + [whole_spec(gain.shape)],
        out_specs=[
            rows_spec(D),
            whole_spec((D, HEADW)),
            whole_spec((8, D)),
            whole_spec((8, PMAX)),
        ],
        out_shape=[
            jax.ShapeDtypeStruct((rows, D), F32),
            jax.ShapeDtypeStruct((D, HEADW), BF),
            jax.ShapeDtypeStruct((8, D), F32),
            jax.ShapeDtypeStruct((8, PMAX), F32),
        ],
        scratch_shapes=[
            pltpu.VMEM((D, HEADW), F32),
            pltpu.VMEM((D, HEADW), BF),
            semaphores(group),
        ],
        compiler_params=params(40),
        cost_estimate=pl.CostEstimate(
            flops=6 * rows * D * HEADW, bytes_accessed=8 << 20, transcendentals=0
        ),
    )(x, targets, mask, *arrays, gain)


def backward_body(names, extra, group, out_group, *refs):
    first, attn, ffn = "in" in names, "qkv" in names, "gu" in names
    take = Taker(refs)
    dout_ref = take()
    if attn:
        x_ref, qkv_ref, prob_ref, mixed_ref = take(4)
    if ffn:
        mid_ref, gu_ref = take(2)
    concat_ref = take() if first else None
    extras = {extra: take()} if extra else {}
    arrays = take.refs[: group.parts]
    take(group.parts)
    gain_ref = take()
    if attn:
        cos_ref, sin_ref, code_ref = take(3)
    dx_ref = None if first else take()
    out_arrays = take.refs[: out_group.parts]
    take(out_group.parts)
    if attn:
        dg_attn, db_ref = take(2)
    if ffn:
        dg_ffn = take()
    loads = [n for n in names if n != "in"]
    w = take.named(loads)
    acc = take.named(names)
    grads = take.named(names)
    sems, out_sems = take(2)
    if attn:
        dqkv_ref = take()
    if ffn:
        dgu_ref = take()
    step = pl.program_id(0)
    me, core = place(group)
    made = copies(group, arrays, me, down_fields(w), sems, outward=False)
    out_core = place(out_group)[1]
    sent = copies(
        out_group, out_arrays, me, {**down_fields(grads), **extras}, out_sems, outward=True
    )

    @pl.when(step == 0)
    def _():
        start_copies(group, made, core)
        for ref in acc.values():
            ref[...] = jnp.zeros_like(ref)
        if attn:
            dg_attn[...] = jnp.zeros_like(dg_attn)
            db_ref[...] = jnp.zeros_like(db_ref)
        if ffn:
            dg_ffn[...] = jnp.zeros_like(dg_ffn)
        wait_copies(made, list(made))

    dout = dout_ref[...]
    rows = dout.shape[0]
    grad_mid = dout
    if ffn:
        dout_low = dout.astype(BF)
        gate = gu_ref[:, :FF].astype(F32)
        up = gu_ref[:, FF:].astype(F32)
        sig = sigmoid_of(gate)
        silu = gate * sig
        acc["d"][...] += dot_tn((silu * up).astype(BF), dout_low)
        grad_hidden = dot_nt(dout_low, w["d"][...])
        dgu_ref[:, :FF] = (grad_hidden * up * (sig + silu * (1.0 - sig))).astype(BF)
        dgu_ref[:, FF:] = (grad_hidden * silu).astype(BF)
        u_mid, inverse_mid = unit(mid_ref[...])
        gain_mid = gain_ref[1:2, :]
        acc["gu"][...] += dot_tn((u_mid * gain_mid).astype(BF), dgu_ref[...])
        grad_mid, dgain_mid = rms_backward(
            u_mid, inverse_mid, gain_mid, dot_nt(dgu_ref[...], w["gu"][...])
        )
        dg_ffn[...] += dgain_mid
        grad_mid = grad_mid + dout
    grad_x = grad_mid
    if attn:
        grad_attn_low = grad_mid.astype(BF)
        acc["o"][...] += dot_tn(mixed_ref[...], grad_attn_low)
        grad_mixed = dot_nt(grad_attn_low, w["o"][...]).astype(BF)
        spots = [(b, p) for p in range(PAIRS) for b in range(rows // BUCKET)]
        dprobs = []
        for b, p in spots:
            here = slice(b * BUCKET, (b + 1) * BUCKET)
            dm2 = two_blocks(grad_mixed[here, p * LANES : (p + 1) * LANES])
            v = qkv_ref[here, 2 * D + p * LANES : 2 * D + (p + 1) * LANES]
            dprobs.append(dot_nt(v, dm2))
        dscores = []
        for (b, p), dprob in zip(spots, dprobs):
            prob = prob_ref[b * BUCKET : (b + 1) * BUCKET, p * LANES : (p + 1) * LANES].astype(F32)
            ds = prob * (dprob - jnp.sum(prob * dprob, axis=0, keepdims=True))
            dscores.append(ds.astype(BF))
        for p in range(PAIRS):
            other_sum = jnp.zeros((8, LANES), F32)
            same_sum = jnp.zeros((8, LANES), F32)
            for b in range(rows // BUCKET):
                ds = dscores[p * (rows // BUCKET) + b].astype(F32)
                same = code_ref[b * BUCKET : (b + 1) * BUCKET, :] > 0.5
                same_sum = same_sum + rows_to_eight(jnp.where(same, ds, 0.0))
                other_sum = other_sum + rows_to_eight(jnp.where(same, 0.0, ds))
            db_ref[p * 8 : (p + 1) * 8, :] += other_sum
            db_ref[(PAIRS + p) * 8 : (PAIRS + p + 1) * 8, :] += same_sum
        for (b, p), ds in zip(spots, dscores):
            here = slice(b * BUCKET, (b + 1) * BUCKET)
            cols = slice(p * LANES, (p + 1) * LANES)
            kcols = slice(D + p * LANES, D + (p + 1) * LANES)
            vcols = slice(2 * D + p * LANES, 2 * D + (p + 1) * LANES)
            cos = cos_ref[here, :] * HD ** (-0.5)
            sin = sin_ref[here, :] * HD ** (-0.5)
            dm2 = two_blocks(grad_mixed[here, cols])
            dq = fold_blocks(dot_tn(ds, qkv_ref[here, kcols]))
            dk = dot_nn(ds, two_blocks(qkv_ref[here, cols]))
            dv = dot_nn(prob_ref[here, cols], dm2)
            dqkv_ref[here, cols] = (dq * cos + swap_halves(dq * sin)).astype(BF)
            dqkv_ref[here, kcols] = (dk * cos + swap_halves(dk * sin)).astype(BF)
            dqkv_ref[here, vcols] = dv.astype(BF)
        u, inverse = unit(x_ref[...])
        gain_row = gain_ref[0:1, :]
        acc["qkv"][...] += dot_tn((u * gain_row).astype(BF), dqkv_ref[...])
        grad_x, dgain = rms_backward(u, inverse, gain_row, dot_nt(dqkv_ref[...], w["qkv"][...]))
        dg_attn[...] += dgain
        grad_x = grad_x + grad_mid
    if first:
        acc["in"][...] += dot_tn(grad_x.astype(BF), concat_ref[...])
    else:
        dx_ref[...] = grad_x

    @pl.when(step == pl.num_programs(0) - 1)
    def _():
        for name in names:
            grads[name][...] = acc[name][...].astype(BF)
        start_copies(out_group, sent, out_core)
        wait_copies(sent, list(sent))


def backward_layer(names, dout, saved, concat, extra, group, arrays, out_group, gain_pair, tables):
    first, attn, ffn = "in" in names, "qkv" in names, "gu" in names
    rows = dout.shape[0]
    args = [dout, *saved] + ([concat] if first else [])
    in_specs = [rows_spec(a.shape[1]) for a in args]
    if extra:
        args.append(extra[1])
        in_specs.append(whole_spec(extra[1].shape))
    args += [*arrays, gain_pair]
    in_specs += [any_spec()] * group.parts + [whole_spec(gain_pair.shape)]
    if attn:
        args += list(tables)
        in_specs += [rows_spec(LANES)] * 3
    out_specs, out_shape = [], []
    if not first:
        out_specs.append(rows_spec(D))
        out_shape.append(jax.ShapeDtypeStruct((rows, D), F32))
    slots = (out_group.shards, out_group.rows, out_group.width)
    out_specs += [any_spec()] * out_group.parts
    out_shape += [jax.ShapeDtypeStruct(slots, BF)] * out_group.parts
    small = ([(8, D), (48, LANES)] if attn else []) + ([(8, D)] if ffn else [])
    out_specs += [whole_spec(shape) for shape in small]
    out_shape += [jax.ShapeDtypeStruct(shape, F32) for shape in small]
    scratch = [pltpu.VMEM(WEIGHTS[n], BF) for n in names if n != "in"]
    scratch += [pltpu.VMEM(WEIGHTS[n], F32) for n in names]
    scratch += [pltpu.VMEM(WEIGHTS[n], BF) for n in names]
    scratch += [semaphores(group), semaphores(out_group)]
    scratch += [pltpu.VMEM((TILE, QKV), BF)] if attn else []
    scratch += [pltpu.VMEM((TILE, 2 * FF), BF)] if ffn else []
    size = sum(WEIGHTS[n][0] * WEIGHTS[n][1] for n in names)
    got = pl.pallas_call(
        functools.partial(backward_body, names, extra[0] if extra else None, group, out_group),
        grid=(rows // TILE,),
        in_specs=in_specs,
        out_specs=out_specs,
        out_shape=out_shape,
        scratch_shapes=scratch,
        compiler_params=params(56),
        cost_estimate=pl.CostEstimate(
            flops=4 * rows * size, bytes_accessed=48 * size, transcendentals=0
        ),
    )(*args)
    got = list(got)
    grad = None if first else got.pop(0)
    return grad, got[: out_group.parts], got[out_group.parts :]


def partners(sizes, fsdp_mask, dp_mask):
    fsdp, dp = sizes
    return [
        (f * dp + d, (f ^ fsdp_mask) * dp + (d ^ dp_mask)) for f in range(fsdp) for d in range(dp)
    ]


def slot_of(offset, masks):
    slot = 0
    for bit, mask in enumerate(masks):
        slot = slot + jnp.where((offset & mask) != 0, 1 << bit, 0)
    return slot


def swap(x, sizes, fsdp_mask, dp_mask):
    return lax.ppermute(x, AXES, partners(sizes, fsdp_mask, dp_mask))


def reorder(slots, masks):
    me = lax.axis_index("fsdp")
    return jnp.stack(
        [
            lax.dynamic_index_in_dim(slots, slot_of(me ^ j, masks), 0, keepdims=False)
            for j in range(slots.shape[0])
        ]
    )


class Gather:
    def __init__(self, parts, sizes):
        self.sizes = sizes
        self.four = len(parts) == 4
        self.mine = by_place(parts)[0][None]
        self.masks = masks_of(sizes[0])
        self.last = self.masks.pop() if self.four else 0
        self.got = ()

    def land(self):
        if self.got:
            self.mine = jnp.concatenate([self.mine, *self.got], axis=0)
            self.got = ()
        return self.mine

    def move(self, after=None):
        mine = self.land()
        if after is not None:
            mine, after.got = lax.optimization_barrier((mine, after.got))
        self.mine = mine
        self.got = (swap(mine, self.sizes, self.masks.pop(0), 0),)

    def ring(self):
        mine = self.land()
        self.got = (swap(mine, self.sizes, self.last, 0), swap(mine, self.sizes, 0, 2))

    def hold(self, x):
        x, self.got = lax.optimization_barrier((x, self.got))
        return x

    def arrays(self):
        if not self.four:
            mine = self.land()
            return mine, swap(mine, self.sizes, 0, 1)
        near, far = self.got
        half = near.shape[0] // 2
        corner = (
            swap(far[:half], self.sizes, self.last, 0),
            swap(near[half:], self.sizes, 0, 2),
        )
        mine = jnp.concatenate([self.mine, near], axis=0)
        far = jnp.concatenate([far, *corner], axis=0)
        return mine, swap(mine, self.sizes, 0, 1), far, swap(far, self.sizes, 0, 1)


def by_place(parts):
    place = lax.axis_index("dp") & (len(parts) - 1)
    found = []
    for distance in range(len(parts)):
        one = parts[distance]
        for other in range(1, len(parts)):
            one = jnp.where(place == other, parts[other ^ distance], one)
        found.append(one)
    return found


def by_core(mine, other):
    core = lax.axis_index("dp") & 1
    return jnp.where(core == 0, mine, other), jnp.where(core == 0, other, mine)


def add(a, b):
    return (a.astype(F32) + b.astype(F32)).astype(BF)


def to_slots(shards, masks):
    me = lax.axis_index("fsdp")
    slots = [None] * shards.shape[0]
    for v in range(shards.shape[0]):
        slots[slot_index(v, masks)] = lax.dynamic_index_in_dim(shards, me ^ v, 0, keepdims=False)
    return jnp.stack(slots)


class Scatter:
    def __init__(self, keep, give, sizes):
        self.sizes = sizes
        self.keep = keep
        self.got = swap(give, sizes, 0, 1)
        self.moves = [(mask, 0) for mask in reversed(masks_of(sizes[0]))]
        dp_mask = 2
        while dp_mask < sizes[1]:
            self.moves.append((0, dp_mask))
            dp_mask *= 2

    def ready(self):
        if self.moves and self.moves[0][0]:
            half = self.keep.shape[0] // 2
            self.away = add(self.keep[half:], self.got[half:])
            self.keep = add(self.keep[:half], self.got[:half])
        else:
            self.keep = add(self.keep, self.got)
            self.away = self.keep

    def move(self):
        self.got = swap(self.away, self.sizes, *self.moves.pop(0))

    def total(self):
        return add(self.keep, self.got)[0]


def hold(x, *scatters):
    for one in scatters:
        one.ready()
    held = lax.optimization_barrier((x, [(one.keep, one.away) for one in scatters]))
    for one, (keep, away) in zip(scatters, held[1]):
        one.keep, one.away = keep, away
        one.move()
    return held[0]


def after_landing(x, scatters):
    x, landed = lax.optimization_barrier((x, [one.got for one in scatters]))
    for one, got in zip(scatters, landed):
        one.got = got
    return x


def pad_rows(x, rows):
    return jnp.pad(x, ((0, 0),) * (x.ndim - 2) + ((0, rows - x.shape[-2]), (0, 0)))


def to_whole(group, whole, arrays, sizes):
    masks = masks_of(sizes[0])
    arrays = [reorder(a, masks) for a in by_place(arrays)]
    fields = group.unpack(arrays)
    fields = {n: p.reshape(1, p.shape[0] * p.shape[1], p.shape[2]) for n, p in fields.items()}
    return whole.pack(fields)


def from_whole(group, whole, arrays, sizes):
    fsdp = sizes[0]
    fields = whole.unpack(arrays)
    fields = {n: p.reshape(fsdp, p.shape[1] // fsdp, p.shape[2]) for n, p in fields.items()}
    arrays = group.pack(fields)
    if group.parts == 1:
        return arrays
    masks = masks_of(fsdp)
    return by_core(*[to_slots(a, masks) for a in arrays])


def rotary_tables(time_ids):
    frequency = THETA ** (-2.0 * jnp.arange(HD // 2, dtype=F32) / HD)
    phase = time_ids.astype(F32)[:, None] * frequency[None, :]
    cos, sin = jnp.cos(phase), jnp.sin(phase)
    return jnp.concatenate([cos] * 4, axis=1), jnp.concatenate([-sin, sin, -sin, sin], axis=1)


def live_slots(lengths):
    return jnp.arange(BUCKET, dtype=jnp.int32)[None, :] < lengths[:, None]


def target_mask(size_ids, lengths):
    widths = jnp.where(live_slots(lengths).reshape(size_ids.shape), PMAX >> (4 - size_ids), 0)
    return (jnp.arange(PMAX, dtype=jnp.int32)[None, :] < widths[:, None]).astype(F32)


def code_table(variate_ids, lengths):
    variates = variate_ids.reshape(-1, BUCKET)
    same = (variates[:, :, None] == variates[:, None, :]).astype(F32)
    code = jnp.where(live_slots(lengths)[:, :, None], same, -1.0).reshape(-1, BUCKET)
    return jnp.concatenate([code, code], axis=1)


def patch_concat(patches, size_ids):
    pieces = []
    for size_id in range(5):
        span = PMAX >> 4 - size_id
        chosen = (size_ids == size_id)[:, None]
        pieces.append(jnp.where(chosen, patches[:, :span], jnp.zeros((), BF)))
    pieces.append(jnp.zeros((patches.shape[0], 2 * PMAX - IN_CAT), BF))
    return jnp.concatenate(pieces, axis=1)


def adam_update(master, clipped, first_old, second_old, matrix):
    first_new = BETA_ONE * first_old + (1.0 - BETA_ONE) * clipped
    second_new = BETA_TWO * second_old + (1.0 - BETA_TWO) * clipped * clipped
    first_hat = first_new / (1.0 - BETA_ONE**STEP_NUM)
    second_hat = second_new / (1.0 - BETA_TWO**STEP_NUM)
    direction = first_hat / (jnp.sqrt(second_hat) + ADAM_EPS)
    if matrix:
        master_new = master - RATE_MATRIX * (direction + WEIGHT_DECAY * master)
    else:
        master_new = master - RATE_GAIN * direction
    return (master_new, first_new, second_new)


def sum_moves(sizes, dp_from=1):
    moves = []
    dp_mask = dp_from
    while dp_mask < sizes[1]:
        moves.append((0, dp_mask))
        dp_mask *= 2
    return moves + [(mask, 0) for mask in masks_of(sizes[0])]


def per_device(sizes, *args):
    patches, targets, size_ids, time_ids, variate_ids, lengths = args[:6]
    masters = args[6:14]
    firsts = args[14:22]
    seconds = args[22:30]
    w_in, w_qkv, w_o, w_gu, w_down, w_head, gains, var_bias = masters
    own = w_head.shape[0]
    down_rows = w_down.shape[1]
    direct = own % 16 == 0 and down_rows % 16 == 0
    attn_fields = [("qkv", QKV), ("o", D)]
    ffn_fields = [("d0", D), ("d1", D), ("gu", 2 * FF), ("d2", D)]
    plan = [
        (("in",) + ATTN, [("in", 2 * PMAX)] + attn_fields),
        (FFN, ffn_fields),
        (ATTN + FFN, attn_fields + ffn_fields),
        (ATTN + FFN, attn_fields + ffn_fields + [("head", HEADW)]),
    ]
    layers = [0, 0, 1, 2]
    count = len(plan)
    def groups_of(fields, parts):
        many = [Group(f, p, sizes[0], own, down_rows) for f, p in zip(fields, parts)]
        if direct:
            return many, many
        return many, [Group(f, p, 1, D, FF) for f, p in zip(fields, parts)]

    fields = [f for _, f in plan]
    groups, wholes = groups_of(fields, [2] * count)
    in_fields = [fields[0] + fields[1], fields[2], fields[3]]
    in_groups, in_wholes = groups_of(in_fields, [4, 2, 4])
    sources = [0, 0, 1, 2]

    in_rows = jnp.concatenate(
        [w_in.T, gains.T, jnp.zeros((own, 2 * PMAX - IN_CAT - NGAIN), F32)], axis=1
    ).astype(BF)
    def packed(layer, stacks, head_w=None):
        fields = {m: w[layer].astype(BF) for m, w in zip(("qkv", "o", "gu", "d"), stacks)}
        if layer == L - 1:
            fields["head"] = head_w.astype(BF)
        return in_groups[layer].pack({**fields, "in": in_rows})

    stacks = (w_qkv, w_o, w_gu, w_down)
    first = Gather(packed(0, stacks), sizes)
    first.move()
    stacks, head_w, time_ids = first.hold((stacks, w_head, time_ids))
    second, third = [Gather(packed(layer, stacks, head_w), sizes) for layer in (1, 2)]
    cos, sin = rotary_tables(time_ids)
    while first.masks:
        first.move()
    early = (patches, size_ids, variate_ids, lengths)
    early, second.mine = first.hold((early, second.mine))
    patches, size_ids, variate_ids, lengths = early
    first.ring()
    second.move()
    third.move(second)
    while second.masks:
        second.move()
    while len(third.masks) > 1:
        third.move()

    def arrived(layer):
        arrays = (first, second, third)[layer].arrays()
        return arrays if direct else to_whole(in_groups[layer], in_wholes[layer], arrays, sizes)

    tables = (cos, sin, code_table(variate_ids, lengths))
    concat = patch_concat(patches, size_ids)
    bias_lanes = jnp.repeat(var_bias, HD, axis=2).reshape(L, 2, PAIRS, LANES)
    bias_lanes = jnp.pad(bias_lanes, ((0, 0), (0, 0), (0, 8 - PAIRS), (0, 0)))
    bias_lanes = bias_lanes.reshape(L, 16, LANES)

    stream = concat
    kept = [None] * count
    loaded = []
    gain_pairs = [None] * (L + 1)
    for layer in range(L):
        if layer == 1:
            second.mine, third.got = lax.optimization_barrier((second.land(), third.got))
        loaded.append(arrived(layer))
        if layer == 0:
            third.mine, stream = lax.optimization_barrier((third.land(), stream))
            while third.masks:
                third.move()
        if layer == 1:
            third.ring()
        names = ATTN + FFN if layer else ("in",) + ATTN + FFN
        got = list(
            forward_layer(
                stream,
                names,
                in_wholes[layer],
                loaded[layer],
                gain_pairs[layer],
                bias_lanes[layer],
                tables,
            )
        )
        if layer == 0:
            stream, found = got[:2]
            got = got[2:]
            gain_pairs = [found[0:2], found[2:4], found[4:6], found[6:8]]
            kept[0] = [stream, *got[:3]]
            kept[1] = [got[3], got[5]]
        else:
            kept[layer + 1] = [stream, *got[:4], got[5]]
        stream = got[4]
        for one in (second, third)[layer:]:
            stream = one.hold(stream)
        if layer == 0:
            stream, size_ids, lengths = lax.optimization_barrier((stream, size_ids, lengths))
            mask = target_mask(size_ids, lengths)
            live = jnp.sum(mask)
    grad, head_grad, gain_grad, loss = head(
        stream, targets, mask, in_wholes[-1], loaded[-1], gain_pairs[L]
    )
    raw = [gain_grad, loss]
    totals = [None] * count
    for n in reversed(range(count)):
        names = plan[n][0]
        layer = layers[n]
        grad, arrays, small = backward_layer(
            names,
            grad,
            kept[n],
            concat,
            ("head", head_grad) if n == count - 1 else None,
            in_wholes[sources[n]],
            loaded[sources[n]],
            wholes[n],
            gain_pairs[layer],
            tables,
        )
        raw += small
        if not direct:
            arrays = from_whole(groups[n], wholes[n], arrays, sizes)
        keep, give = arrays
        flying = totals[n + 1 :]
        give = after_landing(give, flying)
        totals[n] = Scatter(keep, give, sizes)
        if n:
            grad = hold(grad, totals[n], *flying)

    raw = hold(raw, *totals)
    gain_grad, loss, *raw = raw
    gain_grads, bias_grads = {2 * L: gain_grad}, [None] * L
    for n in reversed(range(count)):
        names = plan[n][0]
        layer = layers[n]
        if "qkv" in names:
            gain_grads[2 * layer] = raw.pop(0)
            bias_grads[layer] = raw.pop(0).reshape(2, PAIRS, 8, 2, HD)
        if "gu" in names:
            gain_grads[2 * layer + 1] = raw.pop(0)
    gain_grads = [jnp.sum(gain_grads[g], axis=0) for g in range(NGAIN)]
    bias_grads = jnp.sum(jnp.stack(bias_grads), axis=(3, 5)).reshape(L, 2, H)

    small = jnp.concatenate([jnp.sum(loss)[None], live[None], bias_grads.reshape(-1)])
    small = jnp.pad(small, (0, D - small.shape[0]))
    rows = jnp.stack(gain_grads + [small])
    pending = list(zip(range(count), totals))
    own_parts = [None] * count
    first = True
    while pending:
        for n, one in pending:
            if not one.moves:
                own_parts[n] = one.total()
        pending = [(n, one) for n, one in pending if one.moves]
        if not pending:
            break
        if not first:
            hold((), *[one for _, one in pending])
        first = False
    squares = jnp.zeros((1, 1), F32)
    for n in range(count):
        squares = squares + groups[n].squares(own_parts[n])
    rows = rows + jnp.pad(squares, ((NGAIN, 0), (D - 1, 0)))
    for fsdp_mask, dp_mask in sum_moves(sizes):
        rows = rows + swap(rows, sizes, fsdp_mask, dp_mask)
    squares = rows[NGAIN, D - 1] / (sizes[1] // 2)
    loss_sum, total_count = rows[NGAIN, 0], rows[NGAIN, 1]
    inverse_count = 1.0 / total_count
    bias_grad = rows[NGAIN, 2 : 2 + var_bias.size].reshape(var_bias.shape) * inverse_count
    at_row = lax.broadcasted_iota(jnp.int32, rows.shape, 0)
    at_col = lax.broadcasted_iota(jnp.int32, rows.shape, 1)
    counted = (at_row < NGAIN) | ((at_col >= 2) & (at_col < 2 + var_bias.size))
    squares = squares + jnp.sum(jnp.where(counted, jnp.square(rows), 0.0))
    gain_all = rows[:NGAIN]
    gain_own = lax.dynamic_slice_in_dim(gain_all, lax.axis_index("fsdp") * own, own, axis=1)

    pieces = []
    for n in range(count):
        low, high = by_core(own_parts[n], swap(own_parts[n], sizes, 0, 1))
        pieces.append(groups[n].unpack((low, high)))
    in_piece = pieces[0]["in"][:, :IN_CAT]
    head_piece = pieces[-1]["head"]
    matrices = [[piece[m] for piece in pieces if m in piece] for m in ("qkv", "o", "gu", "d")]
    grad_norm = jnp.sqrt(squares) * inverse_count
    factor = jnp.minimum(1.0, CLIP_NORM / grad_norm)
    scale = factor * inverse_count

    gradients = [in_piece.T] + [jnp.stack(m) for m in matrices] + [head_piece, gain_own]
    clipped = [g.astype(F32) * scale for g in gradients] + [bias_grad * factor]
    fresh = [
        adam_update(masters[m], clipped[m], firsts[m], seconds[m], m < 6) for m in range(8)
    ]
    return (
        (loss_sum, total_count, grad_norm)
        + tuple(f[0] for f in fresh)
        + tuple(f[1] for f in fresh)
        + tuple(f[2] for f in fresh)
    )


def solution(mesh):
    sizes = (mesh.shape["fsdp"], mesh.shape["dp"])
    tokens = P(("fsdp", "dp"))
    tokens_two = P(("fsdp", "dp"), None)
    columns = P(None, "fsdp")
    stacked = P(None, "fsdp", None)
    states = (columns, stacked, stacked, stacked, stacked, P("fsdp", None), columns, P())
    in_specs = (tokens_two, tokens_two, tokens, tokens, tokens, tokens) + states * 3
    out_specs = (P(), P(), P()) + states * 3
    return jax.shard_map(
        functools.partial(per_device, sizes),
        mesh=mesh,
        in_specs=in_specs,
        out_specs=out_specs,
        check_vma=False,
    )
```

```python
import functools

import jax
import jax.numpy as jnp
from jax import lax
from jax.experimental import pallas as pl
from jax.experimental.pallas import tpu as pltpu
from jax.sharding import PartitionSpec as P

D = 384
H = 6
HD = 64
FF = 1024
PMAX = 128
NQ = 9
BUCKET = 64
L = 3
STEP_NUM = 10
IN_CAT = 248
NGAIN = 7
QKV = 3 * D
HEADW = NQ * PMAX
PAIRS = H // 2
LANES = 2 * HD

TILE = 256
FORWARD_TILE = 512

EPS_NORM = 1e-05
SMOOTH = 0.5
THETA = 10000.0
MASKED_SCORE = -1e30
CLIP_NORM = 0.001
BETA_ONE = 0.9
BETA_TWO = 0.95
ADAM_EPS = 1e-08
WEIGHT_DECAY = 0.1
RATE_MATRIX = 0.15
RATE_GAIN = 0.8

BF = jnp.bfloat16
F32 = jnp.float32
AXES = ("fsdp", "dp")


def dot_nn(a, b):
    return lax.dot_general(a, b, (((1,), (0,)), ((), ())), preferred_element_type=F32)


def dot_nt(a, b):
    return lax.dot_general(a, b, (((1,), (1,)), ((), ())), preferred_element_type=F32)


def dot_tn(a, b):
    return lax.dot_general(a, b, (((0,), (0,)), ((), ())), preferred_element_type=F32)


def unit(x):
    inverse = lax.rsqrt(jnp.mean(x * x, axis=-1, keepdims=True) + EPS_NORM)
    return x * inverse, inverse


def rms_backward(u, inverse, gain_row, grad):
    grad_unit = grad * gain_row
    grad_x = inverse * (grad_unit - u * jnp.mean(grad_unit * u, axis=-1, keepdims=True))
    return grad_x, rows_to_eight(grad * u)


def rows_to_eight(x):
    return jnp.sum(x.reshape(x.shape[0] // 8, 8, x.shape[1]), axis=0)


def lane_of(shape):
    return lax.broadcasted_iota(jnp.int32, shape, len(shape) - 1)


def swap_halves(x):
    lane = lane_of(x.shape)
    return jnp.where((lane & 32) == 0, pltpu.roll(x, 96, 1), pltpu.roll(x, 32, 1))


def low_lanes(shape):
    return lane_of(shape) < HD


def two_blocks(x):
    keep = low_lanes(x.shape)
    zero = jnp.zeros_like(x)
    return jnp.concatenate([jnp.where(keep, x, zero), jnp.where(keep, zero, x)], axis=0)


def fold_blocks(x):
    return jnp.where(low_lanes((BUCKET, LANES)), x[:BUCKET], x[BUCKET:])


def sigmoid_of(x):
    return 0.5 * jnp.tanh(0.5 * x) + 0.5


class Group:
    def __init__(self, fields, parts, shards, rows, down_rows):
        self.parts, self.shards, self.rows, self.down_rows = parts, shards, rows, down_rows
        used = sum(width for _, width in fields)
        self.width = -(-used // (parts * LANES)) * LANES
        self.pad = parts * self.width - used
        self.fields = fields
        self.pieces = []
        at = 0
        for name, width in fields:
            done = 0
            while done < width:
                part = (at + done) // self.width
                take = min(width - done, (part + 1) * self.width - at - done)
                self.pieces.append((part, at + done - part * self.width, name, done, take))
                done += take
            at += width
        masks = masks_of(shards)
        self.slots = [slot_index(v, masks) if parts > 1 else v for v in range(shards)]

    def row_span(self, name):
        if name[0] == "d":
            first = int(name[1]) * self.rows
            return first, min(self.rows, self.down_rows - first), self.down_rows
        return 0, self.rows, self.rows

    def pack(self, fields):
        fields = dict(fields)
        if "d" in fields:
            down = fields.pop("d")
            for i in range(3):
                part = down[..., i * self.rows : (i + 1) * self.rows, :]
                fields[f"d{i}"] = pad_rows(part, self.rows)
        parts = [[] for _ in range(self.parts)]
        for part, _, name, start, width in self.pieces:
            parts[part].append(fields[name][..., start : start + width])
        if self.pad:
            like = parts[-1][0]
            parts[-1].append(jnp.zeros(like.shape[:-1] + (self.pad,), like.dtype))
        return tuple(jnp.concatenate(p, axis=-1) for p in parts)

    def unpack(self, parts):
        found = {}
        for part, at, name, _, width in self.pieces:
            got = parts[part][..., at : at + width]
            found[name] = jnp.concatenate([found[name], got], axis=-1) if name in found else got
        if "d0" in found:
            downs = [found.pop(f"d{i}") for i in range(3)]
            downs[2] = downs[2][..., : self.row_span("d2")[1], :]
            found["d"] = jnp.concatenate(downs, axis=-2)
        return found


    def squares(self, own):
        own, core = lax.optimization_barrier((own, lax.axis_index("dp") & 1))
        row = lax.broadcasted_iota(jnp.int32, own.shape, 0)
        col = lax.broadcasted_iota(jnp.int32, own.shape, 1) + core * self.width
        used = col < sum(width for _, width in self.fields)
        for part, at, name, _, width in self.pieces:
            count = self.row_span(name)[1]
            if count < self.rows:
                start = part * self.width + at
                used = used & ((row < count) | (col < start) | (col >= start + width))
        return jnp.sum(jnp.where(used, jnp.square(own.astype(F32)), 0.0)).reshape(1, 1)


def place(group):
    if group.shards == 1:
        return 0, 0
    return lax.axis_index("fsdp"), lax.axis_index("dp") & (group.parts - 1)


def copies(group, arrays, me, targets, sems, outward):
    made = {}
    for n, (part, at, name, start, width) in enumerate(group.pieces):
        if name not in targets:
            continue
        first, count, stride = group.row_span(name)
        for v in range(group.shards):
            owner = v if group.parts == 1 else me ^ v
            row = owner * stride + first
            if not isinstance(row, int):
                row = pl.multiple_of(row, 16)
            whole = targets[name].at[pl.ds(row, count), pl.ds(start, width)]
            slots = [
                a.at[group.slots[v], pl.ds(0, count), pl.ds(at, width)] for a in arrays
            ]
            ends = [(whole, slot) if outward else (slot, whole) for slot in slots]
            pair = [functools.partial(pltpu.make_async_copy, a, b, sems.at[n, v]) for a, b in ends]
            made.setdefault(name, []).append((part, pair))
    return made


def start_copies(group, made, core):
    def go(which):
        for items in made.values():
            for part, pair in items:
                pair[part ^ which]().start()

    if group.shards == 1 or group.parts == 1:
        go(0)
    else:
        for which in range(group.parts):
            pl.when(core == which)(functools.partial(go, which))


def wait_copies(made, names):
    for name in names:
        for _, pair in made.get(name, []):
            pair[0]().wait()


def slot_index(v, masks):
    return sum((1 << bit) for bit, mask in enumerate(masks) if v & mask)


def masks_of(size):
    masks = []
    size //= 2
    while size:
        masks.append(size)
        size //= 2
    return masks


def any_spec():
    return pl.BlockSpec(memory_space=pl.ANY)


WEIGHTS = {"in": (D, 2 * PMAX), "qkv": (D, QKV), "o": (D, D), "gu": (D, 2 * FF), "d": (FF, D)}


def semaphores(group):
    return pltpu.SemaphoreType.DMA((len(group.pieces), group.shards))


class Taker:
    def __init__(self, refs):
        self.refs = list(refs)

    def __call__(self, count=1):
        taken, self.refs = self.refs[:count], self.refs[count:]
        return taken[0] if count == 1 else taken

    def named(self, names):
        return dict(zip(names, [self() for _ in names]))


def down_fields(targets):
    targets = dict(targets)
    if "d" in targets:
        down = targets.pop("d")
        targets.update(d0=down, d1=down, d2=down)
    return targets


ATTN, FFN = ("qkv", "o"), ("gu", "d")


def forward_body(names, group, *refs):
    first, attn, ffn = "in" in names, "qkv" in names, "gu" in names
    take = Taker(refs)
    x_ref = take()
    arrays = take.refs[: group.parts]
    take(group.parts)
    gain_ref = None if first else take()
    if attn:
        bias_ref, cos_ref, sin_ref, code_ref = take(4)
    if first:
        base_ref, rows_ref = take(2)
    if attn:
        qkv_ref, prob_ref, mixed_ref, mid_ref = take(4)
    if ffn:
        out_ref, gu_ref = take(2)
    w = take.named(names)
    sems = take()
    if first:
        gain_ref = take()
    me, core = place(group)
    made = copies(group, arrays, me, down_fields(w), sems, outward=False)
    opening = pl.program_id(0) == 0
    early = [n for n in made if n in ("in", "qkv")]
    late = [n for n in made if n not in early]

    @pl.when(opening)
    def _():
        start_copies(group, made, core)
        wait_copies(made, early)
        if first:
            turned = w["in"][:, PMAX:].astype(F32).T
            gain_ref[...] = turned[IN_CAT - PMAX : IN_CAT - PMAX + 8, :]
            rows_ref[...] = gain_ref[...]

    def rest():
        pl.when(opening)(functools.partial(wait_copies, made, late))

    if attn:
        if first:
            stream = dot_nt(x_ref[...], w["in"][...])
            base_ref[...] = stream
        else:
            stream = x_ref[...]
        rows = stream.shape[0]
        normed = (unit(stream)[0] * gain_ref[0:1, :]).astype(BF)
        cos = cos_ref[...]
        sin = sin_ref[...]
        qk = dot_nn(normed, w["qkv"][:, : 2 * D])
        for j in range(2 * PAIRS):
            cols = slice(j * LANES, (j + 1) * LANES)
            qkv_ref[:, cols] = (qk[:, cols] * cos + swap_halves(qk[:, cols]) * sin).astype(BF)
        qkv_ref[:, 2 * D :] = dot_nn(normed, w["qkv"][:, 2 * D :]).astype(BF)
        spots = [(b, p) for b in range(rows // BUCKET) for p in range(PAIRS)]
        scores = []
        for b, p in spots:
            here = slice(b * BUCKET, (b + 1) * BUCKET)
            q = qkv_ref[here, p * LANES : (p + 1) * LANES]
            k = qkv_ref[here, D + p * LANES : D + (p + 1) * LANES]
            scores.append(dot_nt(k, two_blocks(q)))
        probs = []
        for (b, p), score in zip(spots, scores):
            code = code_ref[b * BUCKET : (b + 1) * BUCKET, :]
            bias = jnp.where(code > 0.5, bias_ref[p + 8 : p + 9, :], bias_ref[p : p + 1, :])
            score = jnp.where(code < -0.5, MASKED_SCORE, score * HD ** (-0.5) + bias)
            e = jnp.exp(score - jnp.max(score, axis=0, keepdims=True))
            probs.append((e * (1.0 / jnp.sum(e, axis=0, keepdims=True))).astype(BF))
        for (b, p), prob in zip(spots, probs):
            here = slice(b * BUCKET, (b + 1) * BUCKET)
            cols = slice(p * LANES, (p + 1) * LANES)
            v = qkv_ref[here, 2 * D + p * LANES : 2 * D + (p + 1) * LANES]
            prob_ref[here, cols] = prob
            mixed_ref[here, cols] = fold_blocks(dot_tn(prob, v)).astype(BF)
        rest()
        middle = stream + dot_nn(mixed_ref[...], w["o"][...])
        mid_ref[...] = middle
    else:
        rest()
        middle = x_ref[...]
    if ffn:
        ffn_in = (unit(middle)[0] * gain_ref[1:2, :]).astype(BF)
        gate_up = dot_nn(ffn_in, w["gu"][...])
        gu_ref[...] = gate_up.astype(BF)
        gate = gate_up[:, :FF]
        hidden = (gate * sigmoid_of(gate) * gate_up[:, FF:]).astype(BF)
        out_ref[...] = middle + dot_nn(hidden, w["d"][...])


def rows_spec(width, tile=TILE):
    return pl.BlockSpec((tile, width), lambda i: (i, 0))


def whole_spec(shape):
    zeros = (0,) * len(shape)
    return pl.BlockSpec(shape, lambda i: zeros)


def params(limit):
    return pltpu.CompilerParams(
        dimension_semantics=("arbitrary",), vmem_limit_bytes=limit * 1024 * 1024
    )


def forward_layer(x, names, group, arrays, gain_pair, bias_rows, tables):
    first, attn, ffn = "in" in names, "qkv" in names, "gu" in names
    rows = x.shape[0]
    args = [x, *arrays]
    in_specs = [rows_spec(x.shape[1], FORWARD_TILE)] + [any_spec()] * group.parts
    if not first:
        args.append(gain_pair)
        in_specs.append(whole_spec(gain_pair.shape))
    if attn:
        args += [bias_rows, *tables]
        in_specs += [whole_spec(bias_rows.shape)] + [rows_spec(LANES, FORWARD_TILE)] * 3
    outs = [(D, F32)] if first else []
    outs += [(QKV, BF), (D, BF), (D, BF), (D, F32)] if attn else []
    outs += [(D, F32), (2 * FF, BF)] if ffn else []
    out_specs = [rows_spec(w, FORWARD_TILE) for w, _ in outs]
    out_shape = [jax.ShapeDtypeStruct((rows, w), t) for w, t in outs]
    scratch = [pltpu.VMEM(WEIGHTS[n], BF) for n in names] + [semaphores(group)]
    if first:
        out_specs.insert(1, whole_spec((8, D)))
        out_shape.insert(1, jax.ShapeDtypeStruct((8, D), F32))
        scratch.append(pltpu.VMEM((8, D), F32))
    size = sum(WEIGHTS[n][0] * WEIGHTS[n][1] for n in names)
    return pl.pallas_call(
        functools.partial(forward_body, names, group),
        grid=(rows // FORWARD_TILE,),
        in_specs=in_specs,
        out_specs=out_specs,
        out_shape=out_shape,
        scratch_shapes=scratch,
        compiler_params=params(48),
        cost_estimate=pl.CostEstimate(
            flops=2 * rows * size, bytes_accessed=24 * size, transcendentals=0
        ),
    )(*args)


def head_body(
    group,
    x_ref,
    target_ref,
    mask_ref,
    *refs,
):
    take = Taker(refs)
    arrays = take.refs[: group.parts]
    take(group.parts)
    gain_ref, dx_ref, dw_ref, dg_ref, loss_ref, acc_ref, whead_ref, sems = take(8)
    step = pl.program_id(0)
    me, core = place(group)
    made = copies(group, arrays, me, {"head": whead_ref}, sems, outward=False)

    @pl.when(step == 0)
    def _():
        acc_ref[...] = jnp.zeros_like(acc_ref)
        dg_ref[...] = jnp.zeros_like(dg_ref)
        loss_ref[...] = jnp.zeros_like(loss_ref)
        start_copies(group, made, core)
        wait_copies(made, ("head",))

    u, inverse = unit(x_ref[...])
    gain_row = gain_ref[0:1, :]
    final_in = (u * gain_row).astype(BF)
    predicted = dot_nn(final_in, whead_ref[...])
    target = target_ref[...]
    mask = mask_ref[...]
    loss = jnp.zeros((8, PMAX), F32)
    grads = []
    for q in range(NQ):
        level = (q + 1.0) / (NQ + 1)
        r = target - predicted[:, q * PMAX : (q + 1) * PMAX]
        a = r * (-1.0 / SMOOTH)
        e = jnp.exp(-jnp.abs(a))
        recip = 1.0 / (1.0 + e)
        sigmoid = jnp.where(a >= 0, recip, e * recip)
        softplus = jnp.maximum(a, 0.0) + jnp.log(1.0 + e)
        loss = loss + rows_to_eight((level * r + SMOOTH * softplus) * mask)
        grads.append(((sigmoid - level) * mask).astype(BF))
    loss_ref[...] += loss
    grad_pred = jnp.concatenate(grads, axis=1)
    acc_ref[...] += dot_tn(final_in, grad_pred)
    grad_x, grad_gain = rms_backward(u, inverse, gain_row, dot_nt(grad_pred, whead_ref[...]))
    dx_ref[...] = grad_x
    dg_ref[...] += grad_gain

    @pl.when(step == pl.num_programs(0) - 1)
    def _():
        dw_ref[...] = acc_ref[...].astype(BF)


def head(x, targets, mask, group, arrays, gain):
    rows = x.shape[0]
    return pl.pallas_call(
        functools.partial(head_body, group),
        grid=(rows // TILE,),
        in_specs=[
            rows_spec(D),
            rows_spec(PMAX),
            rows_spec(PMAX),
        ]
        + [any_spec()] * group.parts
        + [whole_spec(gain.shape)],
        out_specs=[
            rows_spec(D),
            whole_spec((D, HEADW)),
            whole_spec((8, D)),
            whole_spec((8, PMAX)),
        ],
        out_shape=[
            jax.ShapeDtypeStruct((rows, D), F32),
            jax.ShapeDtypeStruct((D, HEADW), BF),
            jax.ShapeDtypeStruct((8, D), F32),
            jax.ShapeDtypeStruct((8, PMAX), F32),
        ],
        scratch_shapes=[
            pltpu.VMEM((D, HEADW), F32),
            pltpu.VMEM((D, HEADW), BF),
            semaphores(group),
        ],
        compiler_params=params(40),
        cost_estimate=pl.CostEstimate(
            flops=6 * rows * D * HEADW, bytes_accessed=8 << 20, transcendentals=0
        ),
    )(x, targets, mask, *arrays, gain)


def backward_body(names, extra, group, out_group, *refs):
    first, attn, ffn = "in" in names, "qkv" in names, "gu" in names
    take = Taker(refs)
    dout_ref = take()
    if attn:
        x_ref, qkv_ref, prob_ref, mixed_ref = take(4)
    if ffn:
        mid_ref, gu_ref = take(2)
    concat_ref = take() if first else None
    extras = {extra: take()} if extra else {}
    arrays = take.refs[: group.parts]
    take(group.parts)
    gain_ref = take()
    if attn:
        cos_ref, sin_ref, code_ref = take(3)
    dx_ref = None if first else take()
    out_arrays = take.refs[: out_group.parts]
    take(out_group.parts)
    if attn:
        dg_attn, db_ref = take(2)
    if ffn:
        dg_ffn = take()
    loads = [n for n in names if n != "in"]
    w = take.named(loads)
    acc = take.named(names)
    grads = take.named(names)
    sems, out_sems = take(2)
    if attn:
        dqkv_ref = take()
    if ffn:
        dgu_ref = take()
    step = pl.program_id(0)
    me, core = place(group)
    made = copies(group, arrays, me, down_fields(w), sems, outward=False)
    out_core = place(out_group)[1]
    sent = copies(
        out_group, out_arrays, me, {**down_fields(grads), **extras}, out_sems, outward=True
    )

    @pl.when(step == 0)
    def _():
        start_copies(group, made, core)
        for ref in acc.values():
            ref[...] = jnp.zeros_like(ref)
        if attn:
            dg_attn[...] = jnp.zeros_like(dg_attn)
            db_ref[...] = jnp.zeros_like(db_ref)
        if ffn:
            dg_ffn[...] = jnp.zeros_like(dg_ffn)
        wait_copies(made, list(made))

    dout = dout_ref[...]
    rows = dout.shape[0]
    grad_mid = dout
    if ffn:
        dout_low = dout.astype(BF)
        gate = gu_ref[:, :FF].astype(F32)
        up = gu_ref[:, FF:].astype(F32)
        sig = sigmoid_of(gate)
        silu = gate * sig
        acc["d"][...] += dot_tn((silu * up).astype(BF), dout_low)
        grad_hidden = dot_nt(dout_low, w["d"][...])
        dgu_ref[:, :FF] = (grad_hidden * up * (sig + silu * (1.0 - sig))).astype(BF)
        dgu_ref[:, FF:] = (grad_hidden * silu).astype(BF)
        u_mid, inverse_mid = unit(mid_ref[...])
        gain_mid = gain_ref[1:2, :]
        acc["gu"][...] += dot_tn((u_mid * gain_mid).astype(BF), dgu_ref[...])
        grad_mid, dgain_mid = rms_backward(
            u_mid, inverse_mid, gain_mid, dot_nt(dgu_ref[...], w["gu"][...])
        )
        dg_ffn[...] += dgain_mid
        grad_mid = grad_mid + dout
    grad_x = grad_mid
    if attn:
        grad_attn_low = grad_mid.astype(BF)
        acc["o"][...] += dot_tn(mixed_ref[...], grad_attn_low)
        grad_mixed = dot_nt(grad_attn_low, w["o"][...]).astype(BF)
        spots = [(b, p) for p in range(PAIRS) for b in range(rows // BUCKET)]
        dprobs = []
        for b, p in spots:
            here = slice(b * BUCKET, (b + 1) * BUCKET)
            dm2 = two_blocks(grad_mixed[here, p * LANES : (p + 1) * LANES])
            v = qkv_ref[here, 2 * D + p * LANES : 2 * D + (p + 1) * LANES]
            dprobs.append(dot_nt(v, dm2))
        dscores = []
        for (b, p), dprob in zip(spots, dprobs):
            prob = prob_ref[b * BUCKET : (b + 1) * BUCKET, p * LANES : (p + 1) * LANES].astype(F32)
            ds = prob * (dprob - jnp.sum(prob * dprob, axis=0, keepdims=True))
            dscores.append(ds.astype(BF))
        for p in range(PAIRS):
            other_sum = jnp.zeros((8, LANES), F32)
            same_sum = jnp.zeros((8, LANES), F32)
            for b in range(rows // BUCKET):
                ds = dscores[p * (rows // BUCKET) + b].astype(F32)
                same = code_ref[b * BUCKET : (b + 1) * BUCKET, :] > 0.5
                same_sum = same_sum + rows_to_eight(jnp.where(same, ds, 0.0))
                other_sum = other_sum + rows_to_eight(jnp.where(same, 0.0, ds))
            db_ref[p * 8 : (p + 1) * 8, :] += other_sum
            db_ref[(PAIRS + p) * 8 : (PAIRS + p + 1) * 8, :] += same_sum
        for (b, p), ds in zip(spots, dscores):
            here = slice(b * BUCKET, (b + 1) * BUCKET)
            cols = slice(p * LANES, (p + 1) * LANES)
            kcols = slice(D + p * LANES, D + (p + 1) * LANES)
            vcols = slice(2 * D + p * LANES, 2 * D + (p + 1) * LANES)
            cos = cos_ref[here, :] * HD ** (-0.5)
            sin = sin_ref[here, :] * HD ** (-0.5)
            dm2 = two_blocks(grad_mixed[here, cols])
            dq = fold_blocks(dot_tn(ds, qkv_ref[here, kcols]))
            dk = dot_nn(ds, two_blocks(qkv_ref[here, cols]))
            dv = dot_nn(prob_ref[here, cols], dm2)
            dqkv_ref[here, cols] = (dq * cos + swap_halves(dq * sin)).astype(BF)
            dqkv_ref[here, kcols] = (dk * cos + swap_halves(dk * sin)).astype(BF)
            dqkv_ref[here, vcols] = dv.astype(BF)
        u, inverse = unit(x_ref[...])
        gain_row = gain_ref[0:1, :]
        acc["qkv"][...] += dot_tn((u * gain_row).astype(BF), dqkv_ref[...])
        grad_x, dgain = rms_backward(u, inverse, gain_row, dot_nt(dqkv_ref[...], w["qkv"][...]))
        dg_attn[...] += dgain
        grad_x = grad_x + grad_mid
    if first:
        acc["in"][...] += dot_tn(grad_x.astype(BF), concat_ref[...])
    else:
        dx_ref[...] = grad_x

    @pl.when(step == pl.num_programs(0) - 1)
    def _():
        for name in names:
            grads[name][...] = acc[name][...].astype(BF)
        start_copies(out_group, sent, out_core)
        wait_copies(sent, list(sent))


def backward_layer(names, dout, saved, concat, extra, group, arrays, out_group, gain_pair, tables):
    first, attn, ffn = "in" in names, "qkv" in names, "gu" in names
    rows = dout.shape[0]
    args = [dout, *saved] + ([concat] if first else [])
    in_specs = [rows_spec(a.shape[1]) for a in args]
    if extra:
        args.append(extra[1])
        in_specs.append(whole_spec(extra[1].shape))
    args += [*arrays, gain_pair]
    in_specs += [any_spec()] * group.parts + [whole_spec(gain_pair.shape)]
    if attn:
        args += list(tables)
        in_specs += [rows_spec(LANES)] * 3
    out_specs, out_shape = [], []
    if not first:
        out_specs.append(rows_spec(D))
        out_shape.append(jax.ShapeDtypeStruct((rows, D), F32))
    slots = (out_group.shards, out_group.rows, out_group.width)
    out_specs += [any_spec()] * out_group.parts
    out_shape += [jax.ShapeDtypeStruct(slots, BF)] * out_group.parts
    small = ([(8, D), (48, LANES)] if attn else []) + ([(8, D)] if ffn else [])
    out_specs += [whole_spec(shape) for shape in small]
    out_shape += [jax.ShapeDtypeStruct(shape, F32) for shape in small]
    scratch = [pltpu.VMEM(WEIGHTS[n], BF) for n in names if n != "in"]
    scratch += [pltpu.VMEM(WEIGHTS[n], F32) for n in names]
    scratch += [pltpu.VMEM(WEIGHTS[n], BF) for n in names]
    scratch += [semaphores(group), semaphores(out_group)]
    scratch += [pltpu.VMEM((TILE, QKV), BF)] if attn else []
    scratch += [pltpu.VMEM((TILE, 2 * FF), BF)] if ffn else []
    size = sum(WEIGHTS[n][0] * WEIGHTS[n][1] for n in names)
    got = pl.pallas_call(
        functools.partial(backward_body, names, extra[0] if extra else None, group, out_group),
        grid=(rows // TILE,),
        in_specs=in_specs,
        out_specs=out_specs,
        out_shape=out_shape,
        scratch_shapes=scratch,
        compiler_params=params(56),
        cost_estimate=pl.CostEstimate(
            flops=4 * rows * size, bytes_accessed=48 * size, transcendentals=0
        ),
    )(*args)
    got = list(got)
    grad = None if first else got.pop(0)
    return grad, got[: out_group.parts], got[out_group.parts :]


def partners(sizes, fsdp_mask, dp_mask):
    fsdp, dp = sizes
    return [
        (f * dp + d, (f ^ fsdp_mask) * dp + (d ^ dp_mask)) for f in range(fsdp) for d in range(dp)
    ]


def slot_of(offset, masks):
    slot = 0
    for bit, mask in enumerate(masks):
        slot = slot + jnp.where((offset & mask) != 0, 1 << bit, 0)
    return slot


def swap(x, sizes, fsdp_mask, dp_mask):
    return lax.ppermute(x, AXES, partners(sizes, fsdp_mask, dp_mask))


def reorder(slots, masks):
    me = lax.axis_index("fsdp")
    return jnp.stack(
        [
            lax.dynamic_index_in_dim(slots, slot_of(me ^ j, masks), 0, keepdims=False)
            for j in range(slots.shape[0])
        ]
    )


class Gather:
    def __init__(self, parts, sizes):
        self.sizes = sizes
        self.four = len(parts) == 4
        self.mine = by_place(parts)[0][None]
        self.masks = masks_of(sizes[0])
        self.last = self.masks.pop() if self.four else 0
        self.got = ()

    def land(self):
        if self.got:
            self.mine = jnp.concatenate([self.mine, *self.got], axis=0)
            self.got = ()
        return self.mine

    def move(self, after=None):
        mine = self.land()
        if after is not None:
            mine, after.got = lax.optimization_barrier((mine, after.got))
        self.mine = mine
        self.got = (swap(mine, self.sizes, self.masks.pop(0), 0),)

    def ring(self):
        mine = self.land()
        self.got = (swap(mine, self.sizes, self.last, 0), swap(mine, self.sizes, 0, 2))

    def hold(self, x):
        x, self.got = lax.optimization_barrier((x, self.got))
        return x

    def arrays(self):
        if not self.four:
            mine = self.land()
            return mine, swap(mine, self.sizes, 0, 1)
        near, far = self.got
        half = near.shape[0] // 2
        corner = (
            swap(far[:half], self.sizes, self.last, 0),
            swap(near[half:], self.sizes, 0, 2),
        )
        mine = jnp.concatenate([self.mine, near], axis=0)
        far = jnp.concatenate([far, *corner], axis=0)
        return mine, swap(mine, self.sizes, 0, 1), far, swap(far, self.sizes, 0, 1)


def by_place(parts):
    place = lax.axis_index("dp") & (len(parts) - 1)
    found = []
    for distance in range(len(parts)):
        one = parts[distance]
        for other in range(1, len(parts)):
            one = jnp.where(place == other, parts[other ^ distance], one)
        found.append(one)
    return found


def by_core(mine, other):
    core = lax.axis_index("dp") & 1
    return jnp.where(core == 0, mine, other), jnp.where(core == 0, other, mine)


def add(a, b):
    return (a.astype(F32) + b.astype(F32)).astype(BF)


def to_slots(shards, masks):
    me = lax.axis_index("fsdp")
    slots = [None] * shards.shape[0]
    for v in range(shards.shape[0]):
        slots[slot_index(v, masks)] = lax.dynamic_index_in_dim(shards, me ^ v, 0, keepdims=False)
    return jnp.stack(slots)


class Scatter:
    def __init__(self, keep, give, sizes):
        self.sizes = sizes
        self.keep = keep
        self.got = swap(give, sizes, 0, 1)
        self.moves = [(mask, 0) for mask in reversed(masks_of(sizes[0]))]
        dp_mask = 2
        while dp_mask < sizes[1]:
            self.moves.append((0, dp_mask))
            dp_mask *= 2

    def ready(self):
        if self.moves and self.moves[0][0]:
            half = self.keep.shape[0] // 2
            self.away = add(self.keep[half:], self.got[half:])
            self.keep = add(self.keep[:half], self.got[:half])
        else:
            self.keep = add(self.keep, self.got)
            self.away = self.keep

    def move(self):
        self.got = swap(self.away, self.sizes, *self.moves.pop(0))

    def total(self):
        return add(self.keep, self.got)[0]


def hold(x, *scatters):
    for one in scatters:
        one.ready()
    held = lax.optimization_barrier((x, [(one.keep, one.away) for one in scatters]))
    for one, (keep, away) in zip(scatters, held[1]):
        one.keep, one.away = keep, away
        one.move()
    return held[0]


def after_landing(x, scatters):
    x, landed = lax.optimization_barrier((x, [one.got for one in scatters]))
    for one, got in zip(scatters, landed):
        one.got = got
    return x


def pad_rows(x, rows):
    return jnp.pad(x, ((0, 0),) * (x.ndim - 2) + ((0, rows - x.shape[-2]), (0, 0)))


def to_whole(group, whole, arrays, sizes):
    masks = masks_of(sizes[0])
    arrays = [reorder(a, masks) for a in by_place(arrays)]
    fields = group.unpack(arrays)
    fields = {n: p.reshape(1, p.shape[0] * p.shape[1], p.shape[2]) for n, p in fields.items()}
    return whole.pack(fields)


def from_whole(group, whole, arrays, sizes):
    fsdp = sizes[0]
    fields = whole.unpack(arrays)
    fields = {n: p.reshape(fsdp, p.shape[1] // fsdp, p.shape[2]) for n, p in fields.items()}
    arrays = group.pack(fields)
    if group.parts == 1:
        return arrays
    masks = masks_of(fsdp)
    return by_core(*[to_slots(a, masks) for a in arrays])


def rotary_tables(time_ids):
    frequency = THETA ** (-2.0 * jnp.arange(HD // 2, dtype=F32) / HD)
    phase = time_ids.astype(F32)[:, None] * frequency[None, :]
    cos, sin = jnp.cos(phase), jnp.sin(phase)
    return jnp.concatenate([cos] * 4, axis=1), jnp.concatenate([-sin, sin, -sin, sin], axis=1)


def live_slots(lengths):
    return jnp.arange(BUCKET, dtype=jnp.int32)[None, :] < lengths[:, None]


def target_mask(size_ids, lengths):
    widths = jnp.where(live_slots(lengths).reshape(size_ids.shape), PMAX >> (4 - size_ids), 0)
    return (jnp.arange(PMAX, dtype=jnp.int32)[None, :] < widths[:, None]).astype(F32)


def code_table(variate_ids, lengths):
    variates = variate_ids.reshape(-1, BUCKET)
    same = (variates[:, :, None] == variates[:, None, :]).astype(F32)
    code = jnp.where(live_slots(lengths)[:, :, None], same, -1.0).reshape(-1, BUCKET)
    return jnp.concatenate([code, code], axis=1)


def patch_concat(patches, size_ids):
    pieces = []
    for size_id in range(5):
        span = PMAX >> 4 - size_id
        chosen = (size_ids == size_id)[:, None]
        pieces.append(jnp.where(chosen, patches[:, :span], jnp.zeros((), BF)))
    pieces.append(jnp.zeros((patches.shape[0], 2 * PMAX - IN_CAT), BF))
    return jnp.concatenate(pieces, axis=1)


def adam_update(master, clipped, first_old, second_old, matrix):
    first_new = BETA_ONE * first_old + (1.0 - BETA_ONE) * clipped
    second_new = BETA_TWO * second_old + (1.0 - BETA_TWO) * clipped * clipped
    first_hat = first_new / (1.0 - BETA_ONE**STEP_NUM)
    second_hat = second_new / (1.0 - BETA_TWO**STEP_NUM)
    direction = first_hat / (jnp.sqrt(second_hat) + ADAM_EPS)
    if matrix:
        master_new = master - RATE_MATRIX * (direction + WEIGHT_DECAY * master)
    else:
        master_new = master - RATE_GAIN * direction
    return (master_new, first_new, second_new)


def beside(x, sizes, across):
    moves = [(mask, 0) for mask in masks_of(sizes[0])]
    if across:
        moves = []
    dp_mask = 2 if across else 1
    while dp_mask < (sizes[1] if across else 2):
        moves.append((0, dp_mask))
        dp_mask *= 2
    for fsdp_mask, dp_mask in moves:
        x = x + swap(x, sizes, fsdp_mask, dp_mask)
    return x


STACKED = ("qkv", "o", "gu", "d")


def update_body(groups, layers, *refs):
    take = Taker(refs)
    scale_ref = take()
    parts = [take(group.parts) for group in groups]
    names = STACKED + ("head",)
    states = [take.named(names) for _ in range(3)]
    fresh = [take.named(names) for _ in range(3)]
    scale = scale_ref[0, 0]

    def one(name, index, grad):
        old = [state[name][index] for state in states]
        new = adam_update(old[0], grad.astype(F32) * scale, old[1], old[2], True)
        for target, value in zip(fresh, new):
            target[name][index] = value

    def layer_step(layer, place_here):
        for group, group_parts, at_layer in zip(groups, parts, layers):
            if at_layer != layer:
                continue
            for part, at, name, start, width in group.pieces:
                if name == "in":
                    continue
                first, count, _ = group.row_span(name)
                grad = group_parts[part ^ place_here][0:count, at : at + width]
                cols = slice(start, start + width)
                if name == "head":
                    one("head", (slice(0, count), cols), grad)
                else:
                    rows = slice(first, first + count) if name[0] == "d" else slice(0, count)
                    one(name[0] if name[0] == "d" else name, (0, rows, cols), grad)

    core = lax.axis_index("dp") & 1
    for layer in range(L):
        for which in range(2):
            chosen = (pl.program_id(0) == layer) & (core == which)
            pl.when(chosen)(functools.partial(layer_step, layer, which))


def update(groups, layers, parts, scale, states):
    def spec(x):
        if x.ndim == 2:
            return whole_spec(x.shape)
        return pl.BlockSpec((1,) + x.shape[1:], lambda i: (i, 0, 0))

    flat = [x for state in states for x in state]
    got = pl.pallas_call(
        functools.partial(update_body, groups, layers),
        grid=(L,),
        in_specs=[pl.BlockSpec(memory_space=pltpu.SMEM)]
        + [whole_spec(p.shape) for pair in parts for p in pair]
        + [spec(x) for x in flat],
        out_specs=[spec(x) for x in flat],
        out_shape=[jax.ShapeDtypeStruct(x.shape, F32) for x in flat],
        compiler_params=params(60),
        cost_estimate=pl.CostEstimate(flops=1 << 24, bytes_accessed=18 << 20, transcendentals=0),
    )(scale.reshape(1, 1), *[p for pair in parts for p in pair], *flat)
    return [got[i : i + len(states[0])] for i in range(0, len(flat), len(states[0]))]


def per_device(sizes, *args):
    patches, targets, size_ids, time_ids, variate_ids, lengths = args[:6]
    masters = args[6:14]
    firsts = args[14:22]
    seconds = args[22:30]
    w_in, w_qkv, w_o, w_gu, w_down, w_head, gains, var_bias = masters
    own = w_head.shape[0]
    down_rows = w_down.shape[1]
    direct = own % 16 == 0 and down_rows % 16 == 0
    attn_fields = [("qkv", QKV), ("o", D)]
    ffn_fields = [("d0", D), ("d1", D), ("gu", 2 * FF), ("d2", D)]
    plan = [
        (("in",) + ATTN, [("in", 2 * PMAX)] + attn_fields),
        (FFN, ffn_fields),
        (ATTN + FFN, attn_fields + ffn_fields),
        (ATTN + FFN, attn_fields + ffn_fields + [("head", HEADW)]),
    ]
    layers = [0, 0, 1, 2]
    count = len(plan)
    def groups_of(fields, parts):
        many = [Group(f, p, sizes[0], own, down_rows) for f, p in zip(fields, parts)]
        if direct:
            return many, many
        return many, [Group(f, p, 1, D, FF) for f, p in zip(fields, parts)]

    fields = [f for _, f in plan]
    groups, wholes = groups_of(fields, [2] * count)
    in_fields = [fields[0] + fields[1], fields[2], fields[3]]
    in_groups, in_wholes = groups_of(in_fields, [4, 2, 4])
    sources = [0, 0, 1, 2]

    in_rows = jnp.concatenate(
        [w_in.T, gains.T, jnp.zeros((own, 2 * PMAX - IN_CAT - NGAIN), F32)], axis=1
    ).astype(BF)
    def packed(layer, stacks, head_w=None):
        fields = {m: w[layer].astype(BF) for m, w in zip(("qkv", "o", "gu", "d"), stacks)}
        if layer == L - 1:
            fields["head"] = head_w.astype(BF)
        return in_groups[layer].pack({**fields, "in": in_rows})

    stacks = (w_qkv, w_o, w_gu, w_down)
    first = Gather(packed(0, stacks), sizes)
    first.move()
    stacks, head_w, time_ids = first.hold((stacks, w_head, time_ids))
    second, third = [Gather(packed(layer, stacks, head_w), sizes) for layer in (1, 2)]
    cos, sin = rotary_tables(time_ids)
    while first.masks:
        first.move()
    early = (patches, size_ids, variate_ids, lengths)
    early, second.mine = first.hold((early, second.mine))
    patches, size_ids, variate_ids, lengths = early
    first.ring()
    second.move()
    third.move(second)
    while second.masks:
        second.move()
    while len(third.masks) > 1:
        third.move()

    def arrived(layer):
        arrays = (first, second, third)[layer].arrays()
        return arrays if direct else to_whole(in_groups[layer], in_wholes[layer], arrays, sizes)

    tables = (cos, sin, code_table(variate_ids, lengths))
    concat = patch_concat(patches, size_ids)
    bias_lanes = jnp.repeat(var_bias, HD, axis=2).reshape(L, 2, PAIRS, LANES)
    bias_lanes = jnp.pad(bias_lanes, ((0, 0), (0, 0), (0, 8 - PAIRS), (0, 0)))
    bias_lanes = bias_lanes.reshape(L, 16, LANES)

    stream = concat
    kept = [None] * count
    loaded = []
    gain_pairs = [None] * (L + 1)
    for layer in range(L):
        if layer == 1:
            second.mine, third.got = lax.optimization_barrier((second.land(), third.got))
        loaded.append(arrived(layer))
        if layer == 0:
            third.mine, stream = lax.optimization_barrier((third.land(), stream))
            while third.masks:
                third.move()
        if layer == 1:
            third.ring()
        names = ATTN + FFN if layer else ("in",) + ATTN + FFN
        got = list(
            forward_layer(
                stream,
                names,
                in_wholes[layer],
                loaded[layer],
                gain_pairs[layer],
                bias_lanes[layer],
                tables,
            )
        )
        if layer == 0:
            stream, found = got[:2]
            got = got[2:]
            gain_pairs = [found[0:2], found[2:4], found[4:6], found[6:8]]
            kept[0] = [stream, *got[:3]]
            kept[1] = [got[3], got[5]]
        else:
            kept[layer + 1] = [stream, *got[:4], got[5]]
        stream = got[4]
        for one in (second, third)[layer:]:
            stream = one.hold(stream)
        if layer == 0:
            stream, size_ids, lengths = lax.optimization_barrier((stream, size_ids, lengths))
            mask = target_mask(size_ids, lengths)
            live = jnp.sum(mask)
    grad, head_grad, gain_grad, loss = head(
        stream, targets, mask, in_wholes[-1], loaded[-1], gain_pairs[L]
    )
    raw = [gain_grad, loss]
    totals = [None] * count
    for n in reversed(range(count)):
        names = plan[n][0]
        layer = layers[n]
        grad, arrays, small = backward_layer(
            names,
            grad,
            kept[n],
            concat,
            ("head", head_grad) if n == count - 1 else None,
            in_wholes[sources[n]],
            loaded[sources[n]],
            wholes[n],
            gain_pairs[layer],
            tables,
        )
        raw += small
        if not direct:
            arrays = from_whole(groups[n], wholes[n], arrays, sizes)
        keep, give = arrays
        flying = totals[n + 1 :]
        give = after_landing(give, flying)
        totals[n] = Scatter(keep, give, sizes)
        if n:
            grad = hold(grad, totals[n], *flying)

    raw = hold(raw, *totals)
    gain_grad, loss, *raw = raw
    gain_grads, bias_grads = {2 * L: gain_grad}, [None] * L
    for n in reversed(range(count)):
        names = plan[n][0]
        layer = layers[n]
        if "qkv" in names:
            gain_grads[2 * layer] = raw.pop(0)
            bias_grads[layer] = raw.pop(0).reshape(2, PAIRS, 8, 2, HD)
        if "gu" in names:
            gain_grads[2 * layer + 1] = raw.pop(0)
    gain_grads = [jnp.sum(gain_grads[g], axis=0) for g in range(NGAIN)]
    bias_grads = jnp.sum(jnp.stack(bias_grads), axis=(3, 5)).reshape(L, 2, H)

    small = jnp.concatenate([jnp.sum(loss)[None], live[None], bias_grads.reshape(-1)])
    small = jnp.pad(small, (0, D - small.shape[0]))
    rows = jnp.stack(gain_grads + [small])
    rows = beside(rows, sizes, across=True)
    pending = list(zip(range(count), totals))
    own_parts = [None] * count
    first = True
    while pending:
        for n, one in pending:
            if not one.moves:
                own_parts[n] = one.total()
        pending = [(n, one) for n, one in pending if one.moves]
        if not pending:
            break
        if not first:
            hold((), *[one for _, one in pending])
        first = False
    squares = jnp.zeros((1, 1), F32)
    for n, part in enumerate(own_parts):
        squares = squares + groups[n].squares(part)
    rows = beside(rows + jnp.pad(squares, ((NGAIN, 0), (D - 1, 0))), sizes, across=False)
    squares = rows[NGAIN, D - 1]
    loss_sum, total_count = rows[NGAIN, 0], rows[NGAIN, 1]
    inverse_count = 1.0 / total_count
    bias_grad = rows[NGAIN, 2 : 2 + var_bias.size].reshape(var_bias.shape) * inverse_count
    at_row = lax.broadcasted_iota(jnp.int32, rows.shape, 0)
    at_col = lax.broadcasted_iota(jnp.int32, rows.shape, 1)
    counted = (at_row < NGAIN) | ((at_col >= 2) & (at_col < 2 + var_bias.size))
    squares = squares + jnp.sum(jnp.where(counted, jnp.square(rows), 0.0))
    gain_all = rows[:NGAIN]
    gain_own = lax.dynamic_slice_in_dim(gain_all, lax.axis_index("fsdp") * own, own, axis=1)

    grad_norm = jnp.sqrt(squares) * inverse_count
    factor = jnp.minimum(1.0, CLIP_NORM / grad_norm)
    scale = factor * inverse_count


    pairs = [(part, swap(part, sizes, 0, 1)) for part in own_parts]
    whole_parts = [by_core(*pair) for pair in pairs]
    fresh = [None] * 8
    if direct:
        states = [[group_of[m] for m in (1, 2, 3, 4, 5)] for group_of in (masters, firsts, seconds)]
        new = update(groups, layers, pairs, scale, states)
        for at, m in enumerate((1, 2, 3, 4, 5)):
            fresh[m] = tuple(kind[at] for kind in new)
    pieces = [groups[n].unpack(whole_parts[n]) for n in range(count)]
    matrices = [[piece[m] for piece in pieces if m in piece] for m in STACKED]
    gradients = [pieces[0]["in"][:, :IN_CAT].T] + [jnp.stack(m) for m in matrices]
    gradients += [pieces[-1]["head"], gain_own]
    clipped = [g.astype(F32) * scale for g in gradients] + [bias_grad * factor]
    for m in range(8):
        if fresh[m] is None:
            fresh[m] = adam_update(masters[m], clipped[m], firsts[m], seconds[m], m < 6)
    return (
        (loss_sum, total_count, grad_norm)
        + tuple(f[0] for f in fresh)
        + tuple(f[1] for f in fresh)
        + tuple(f[2] for f in fresh)
    )


def solution(mesh):
    sizes = (mesh.shape["fsdp"], mesh.shape["dp"])
    tokens = P(("fsdp", "dp"))
    tokens_two = P(("fsdp", "dp"), None)
    columns = P(None, "fsdp")
    stacked = P(None, "fsdp", None)
    states = (columns, stacked, stacked, stacked, stacked, P("fsdp", None), columns, P())
    in_specs = (tokens_two, tokens_two, tokens, tokens, tokens, tokens) + states * 3
    out_specs = (P(), P(), P()) + states * 3
    return jax.shard_map(
        functools.partial(per_device, sizes),
        mesh=mesh,
        in_specs=in_specs,
        out_specs=out_specs,
        check_vma=False,
    )
```

```python
import functools

import jax
import jax.numpy as jnp
from jax import lax
from jax.experimental import pallas as pl
from jax.experimental.pallas import tpu as pltpu
from jax.sharding import PartitionSpec as P

D = 384
H = 6
HD = 64
FF = 1024
PMAX = 128
NQ = 9
BUCKET = 64
L = 3
STEP_NUM = 10
IN_CAT = 248
NGAIN = 7
QKV = 3 * D
HEADW = NQ * PMAX
PAIRS = H // 2
LANES = 2 * HD

TILE = 256
FORWARD_TILE = 512

EPS_NORM = 1e-05
SMOOTH = 0.5
THETA = 10000.0
MASKED_SCORE = -1e30
CLIP_NORM = 0.001
BETA_ONE = 0.9
BETA_TWO = 0.95
ADAM_EPS = 1e-08
WEIGHT_DECAY = 0.1
RATE_MATRIX = 0.15
RATE_GAIN = 0.8

BF = jnp.bfloat16
F32 = jnp.float32
AXES = ("fsdp", "dp")


def dot_nn(a, b):
    return lax.dot_general(a, b, (((1,), (0,)), ((), ())), preferred_element_type=F32)


def dot_nt(a, b):
    return lax.dot_general(a, b, (((1,), (1,)), ((), ())), preferred_element_type=F32)


def dot_tn(a, b):
    return lax.dot_general(a, b, (((0,), (0,)), ((), ())), preferred_element_type=F32)


def unit(x):
    inverse = lax.rsqrt(jnp.mean(x * x, axis=-1, keepdims=True) + EPS_NORM)
    return x * inverse, inverse


def rms_backward(u, inverse, gain_row, grad):
    grad_unit = grad * gain_row
    grad_x = inverse * (grad_unit - u * jnp.mean(grad_unit * u, axis=-1, keepdims=True))
    return grad_x, rows_to_eight(grad * u)


def rows_to_eight(x):
    return jnp.sum(x.reshape(x.shape[0] // 8, 8, x.shape[1]), axis=0)


def lane_of(shape):
    return lax.broadcasted_iota(jnp.int32, shape, len(shape) - 1)


def swap_halves(x):
    lane = lane_of(x.shape)
    return jnp.where((lane & 32) == 0, pltpu.roll(x, 96, 1), pltpu.roll(x, 32, 1))


def low_lanes(shape):
    return lane_of(shape) < HD


def two_blocks(x):
    keep = low_lanes(x.shape)
    zero = jnp.zeros_like(x)
    return jnp.concatenate([jnp.where(keep, x, zero), jnp.where(keep, zero, x)], axis=0)


def fold_blocks(x):
    return jnp.where(low_lanes((BUCKET, LANES)), x[:BUCKET], x[BUCKET:])


def sigmoid_of(x):
    return 0.5 * jnp.tanh(0.5 * x) + 0.5


class Group:
    def __init__(self, fields, parts, shards, rows, down_rows):
        self.parts, self.shards, self.rows, self.down_rows = parts, shards, rows, down_rows
        used = sum(width for _, width in fields)
        self.width = -(-used // (parts * LANES)) * LANES
        self.pad = parts * self.width - used
        self.fields = fields
        self.pieces = []
        at = 0
        for name, width in fields:
            done = 0
            while done < width:
                part = (at + done) // self.width
                take = min(width - done, (part + 1) * self.width - at - done)
                self.pieces.append((part, at + done - part * self.width, name, done, take))
                done += take
            at += width
        masks = masks_of(shards)
        self.slots = [slot_index(v, masks) if parts > 1 else v for v in range(shards)]

    def row_span(self, name):
        if name[0] == "d":
            first = int(name[1]) * self.rows
            return first, min(self.rows, self.down_rows - first), self.down_rows
        return 0, self.rows, self.rows

    def pack(self, fields):
        fields = dict(fields)
        if "d" in fields:
            down = fields.pop("d")
            for i in range(3):
                part = down[..., i * self.rows : (i + 1) * self.rows, :]
                fields[f"d{i}"] = pad_rows(part, self.rows)
        parts = [[] for _ in range(self.parts)]
        for part, _, name, start, width in self.pieces:
            parts[part].append(fields[name][..., start : start + width])
        if self.pad:
            like = parts[-1][0]
            parts[-1].append(jnp.zeros(like.shape[:-1] + (self.pad,), like.dtype))
        return tuple(jnp.concatenate(p, axis=-1) for p in parts)

    def unpack(self, parts):
        found = {}
        for part, at, name, _, width in self.pieces:
            got = parts[part][..., at : at + width]
            found[name] = jnp.concatenate([found[name], got], axis=-1) if name in found else got
        if "d0" in found:
            downs = [found.pop(f"d{i}") for i in range(3)]
            downs[2] = downs[2][..., : self.row_span("d2")[1], :]
            found["d"] = jnp.concatenate(downs, axis=-2)
        return found


    def squares(self, own):
        own, core = lax.optimization_barrier((own, lax.axis_index("dp") & 1))
        row = lax.broadcasted_iota(jnp.int32, own.shape, 0)
        col = lax.broadcasted_iota(jnp.int32, own.shape, 1) + core * self.width
        used = col < sum(width for _, width in self.fields)
        for part, at, name, _, width in self.pieces:
            count = self.row_span(name)[1]
            if count < self.rows:
                start = part * self.width + at
                used = used & ((row < count) | (col < start) | (col >= start + width))
        return jnp.sum(jnp.where(used, jnp.square(own.astype(F32)), 0.0)).reshape(1, 1)


def place(group):
    if group.shards == 1:
        return 0, 0
    return lax.axis_index("fsdp"), lax.axis_index("dp") & (group.parts - 1)


def copies(group, arrays, me, targets, sems, outward):
    made = {}
    for n, (part, at, name, start, width) in enumerate(group.pieces):
        if name not in targets:
            continue
        first, count, stride = group.row_span(name)
        for v in range(group.shards):
            owner = v if group.parts == 1 else me ^ v
            row = owner * stride + first
            if not isinstance(row, int):
                row = pl.multiple_of(row, 16)
            whole = targets[name].at[pl.ds(row, count), pl.ds(start, width)]
            slots = [
                a.at[group.slots[v], pl.ds(0, count), pl.ds(at, width)] for a in arrays
            ]
            ends = [(whole, slot) if outward else (slot, whole) for slot in slots]
            pair = [functools.partial(pltpu.make_async_copy, a, b, sems.at[n, v]) for a, b in ends]
            made.setdefault(name, []).append((part, pair))
    return made


def start_copies(group, made, core):
    def go(which):
        for items in made.values():
            for part, pair in items:
                pair[part ^ which]().start()

    if group.shards == 1 or group.parts == 1:
        go(0)
    else:
        for which in range(group.parts):
            pl.when(core == which)(functools.partial(go, which))


def wait_copies(made, names):
    for name in names:
        for _, pair in made.get(name, []):
            pair[0]().wait()


def slot_index(v, masks):
    return sum((1 << bit) for bit, mask in enumerate(masks) if v & mask)


def masks_of(size):
    masks = []
    size //= 2
    while size:
        masks.append(size)
        size //= 2
    return masks


def any_spec():
    return pl.BlockSpec(memory_space=pl.ANY)


WEIGHTS = {"in": (D, 2 * PMAX), "qkv": (D, QKV), "o": (D, D), "gu": (D, 2 * FF), "d": (FF, D)}


def semaphores(group):
    return pltpu.SemaphoreType.DMA((len(group.pieces), group.shards))


class Taker:
    def __init__(self, refs):
        self.refs = list(refs)

    def __call__(self, count=1):
        taken, self.refs = self.refs[:count], self.refs[count:]
        return taken[0] if count == 1 else taken

    def named(self, names):
        return dict(zip(names, [self() for _ in names]))


def down_fields(targets):
    targets = dict(targets)
    if "d" in targets:
        down = targets.pop("d")
        targets.update(d0=down, d1=down, d2=down)
    return targets


ATTN, FFN = ("qkv", "o"), ("gu", "d")


def forward_body(names, group, *refs):
    first, attn, ffn = "in" in names, "qkv" in names, "gu" in names
    take = Taker(refs)
    x_ref = take()
    arrays = take.refs[: group.parts]
    take(group.parts)
    gain_ref = None if first else take()
    if attn:
        bias_ref, cos_ref, sin_ref, code_ref = take(4)
    if first:
        base_ref, rows_ref = take(2)
    if attn:
        qkv_ref, prob_ref, mixed_ref, mid_ref = take(4)
    if ffn:
        out_ref, gu_ref = take(2)
    w = take.named(names)
    sems = take()
    if first:
        gain_ref = take()
    me, core = place(group)
    made = copies(group, arrays, me, down_fields(w), sems, outward=False)
    opening = pl.program_id(0) == 0
    early = [n for n in made if n in ("in", "qkv")]
    late = [n for n in made if n not in early]

    @pl.when(opening)
    def _():
        start_copies(group, made, core)
        wait_copies(made, early)
        if first:
            turned = w["in"][:, PMAX:].astype(F32).T
            gain_ref[...] = turned[IN_CAT - PMAX : IN_CAT - PMAX + 8, :]
            rows_ref[...] = gain_ref[...]

    def rest():
        pl.when(opening)(functools.partial(wait_copies, made, late))

    if attn:
        if first:
            stream = dot_nt(x_ref[...], w["in"][...])
            base_ref[...] = stream
        else:
            stream = x_ref[...]
        rows = stream.shape[0]
        normed = (unit(stream)[0] * gain_ref[0:1, :]).astype(BF)
        cos = cos_ref[...]
        sin = sin_ref[...]
        qk = dot_nn(normed, w["qkv"][:, : 2 * D])
        for j in range(2 * PAIRS):
            cols = slice(j * LANES, (j + 1) * LANES)
            qkv_ref[:, cols] = (qk[:, cols] * cos + swap_halves(qk[:, cols]) * sin).astype(BF)
        qkv_ref[:, 2 * D :] = dot_nn(normed, w["qkv"][:, 2 * D :]).astype(BF)
        spots = [(b, p) for b in range(rows // BUCKET) for p in range(PAIRS)]
        scores = []
        for b, p in spots:
            here = slice(b * BUCKET, (b + 1) * BUCKET)
            q = qkv_ref[here, p * LANES : (p + 1) * LANES]
            k = qkv_ref[here, D + p * LANES : D + (p + 1) * LANES]
            scores.append(dot_nt(k, two_blocks(q)))
        probs = []
        for (b, p), score in zip(spots, scores):
            code = code_ref[b * BUCKET : (b + 1) * BUCKET, :]
            bias = jnp.where(code > 0.5, bias_ref[p + 8 : p + 9, :], bias_ref[p : p + 1, :])
            score = jnp.where(code < -0.5, MASKED_SCORE, score * HD ** (-0.5) + bias)
            e = jnp.exp(score - jnp.max(score, axis=0, keepdims=True))
            probs.append((e * (1.0 / jnp.sum(e, axis=0, keepdims=True))).astype(BF))
        for (b, p), prob in zip(spots, probs):
            here = slice(b * BUCKET, (b + 1) * BUCKET)
            cols = slice(p * LANES, (p + 1) * LANES)
            v = qkv_ref[here, 2 * D + p * LANES : 2 * D + (p + 1) * LANES]
            prob_ref[here, cols] = prob
            mixed_ref[here, cols] = fold_blocks(dot_tn(prob, v)).astype(BF)
        rest()
        middle = stream + dot_nn(mixed_ref[...], w["o"][...])
        mid_ref[...] = middle
    else:
        rest()
        middle = x_ref[...]
    if ffn:
        ffn_in = (unit(middle)[0] * gain_ref[1:2, :]).astype(BF)
        gate_up = dot_nn(ffn_in, w["gu"][...])
        gu_ref[...] = gate_up.astype(BF)
        gate = gate_up[:, :FF]
        hidden = (gate * sigmoid_of(gate) * gate_up[:, FF:]).astype(BF)
        out_ref[...] = middle + dot_nn(hidden, w["d"][...])


def rows_spec(width, tile=TILE):
    return pl.BlockSpec((tile, width), lambda i: (i, 0))


def whole_spec(shape):
    zeros = (0,) * len(shape)
    return pl.BlockSpec(shape, lambda i: zeros)


def params(limit):
    return pltpu.CompilerParams(
        dimension_semantics=("arbitrary",), vmem_limit_bytes=limit * 1024 * 1024
    )


def forward_layer(x, names, group, arrays, gain_pair, bias_rows, tables):
    first, attn, ffn = "in" in names, "qkv" in names, "gu" in names
    rows = x.shape[0]
    args = [x, *arrays]
    in_specs = [rows_spec(x.shape[1], FORWARD_TILE)] + [any_spec()] * group.parts
    if not first:
        args.append(gain_pair)
        in_specs.append(whole_spec(gain_pair.shape))
    if attn:
        args += [bias_rows, *tables]
        in_specs += [whole_spec(bias_rows.shape)] + [rows_spec(LANES, FORWARD_TILE)] * 3
    outs = [(D, F32)] if first else []
    outs += [(QKV, BF), (D, BF), (D, BF), (D, F32)] if attn else []
    outs += [(D, F32), (2 * FF, BF)] if ffn else []
    out_specs = [rows_spec(w, FORWARD_TILE) for w, _ in outs]
    out_shape = [jax.ShapeDtypeStruct((rows, w), t) for w, t in outs]
    scratch = [pltpu.VMEM(WEIGHTS[n], BF) for n in names] + [semaphores(group)]
    if first:
        out_specs.insert(1, whole_spec((8, D)))
        out_shape.insert(1, jax.ShapeDtypeStruct((8, D), F32))
        scratch.append(pltpu.VMEM((8, D), F32))
    size = sum(WEIGHTS[n][0] * WEIGHTS[n][1] for n in names)
    return pl.pallas_call(
        functools.partial(forward_body, names, group),
        grid=(rows // FORWARD_TILE,),
        in_specs=in_specs,
        out_specs=out_specs,
        out_shape=out_shape,
        scratch_shapes=scratch,
        compiler_params=params(60),
        cost_estimate=pl.CostEstimate(
            flops=2 * rows * size, bytes_accessed=24 * size, transcendentals=0
        ),
    )(*args)


def head_body(
    group,
    x_ref,
    target_ref,
    mask_ref,
    *refs,
):
    take = Taker(refs)
    arrays = take.refs[: group.parts]
    take(group.parts)
    gain_ref, dx_ref, dw_ref, dg_ref, loss_ref, acc_ref, whead_ref, sems = take(8)
    step = pl.program_id(0)
    me, core = place(group)
    made = copies(group, arrays, me, {"head": whead_ref}, sems, outward=False)

    @pl.when(step == 0)
    def _():
        acc_ref[...] = jnp.zeros_like(acc_ref)
        dg_ref[...] = jnp.zeros_like(dg_ref)
        loss_ref[...] = jnp.zeros_like(loss_ref)
        start_copies(group, made, core)
        wait_copies(made, ("head",))

    u, inverse = unit(x_ref[...])
    gain_row = gain_ref[0:1, :]
    final_in = (u * gain_row).astype(BF)
    predicted = dot_nn(final_in, whead_ref[...])
    target = target_ref[...]
    mask = mask_ref[...]
    loss = jnp.zeros((8, PMAX), F32)
    grads = []
    for q in range(NQ):
        level = (q + 1.0) / (NQ + 1)
        r = target - predicted[:, q * PMAX : (q + 1) * PMAX]
        a = r * (-1.0 / SMOOTH)
        e = jnp.exp(-jnp.abs(a))
        recip = 1.0 / (1.0 + e)
        sigmoid = jnp.where(a >= 0, recip, e * recip)
        softplus = jnp.maximum(a, 0.0) + jnp.log(1.0 + e)
        loss = loss + rows_to_eight((level * r + SMOOTH * softplus) * mask)
        grads.append(((sigmoid - level) * mask).astype(BF))
    loss_ref[...] += loss
    grad_pred = jnp.concatenate(grads, axis=1)
    acc_ref[...] += dot_tn(final_in, grad_pred)
    grad_x, grad_gain = rms_backward(u, inverse, gain_row, dot_nt(grad_pred, whead_ref[...]))
    dx_ref[...] = grad_x
    dg_ref[...] += grad_gain

    @pl.when(step == pl.num_programs(0) - 1)
    def _():
        dw_ref[...] = acc_ref[...].astype(BF)


def head(x, targets, mask, group, arrays, gain):
    rows = x.shape[0]
    return pl.pallas_call(
        functools.partial(head_body, group),
        grid=(rows // TILE,),
        in_specs=[
            rows_spec(D),
            rows_spec(PMAX),
            rows_spec(PMAX),
        ]
        + [any_spec()] * group.parts
        + [whole_spec(gain.shape)],
        out_specs=[
            rows_spec(D),
            whole_spec((D, HEADW)),
            whole_spec((8, D)),
            whole_spec((8, PMAX)),
        ],
        out_shape=[
            jax.ShapeDtypeStruct((rows, D), F32),
            jax.ShapeDtypeStruct((D, HEADW), BF),
            jax.ShapeDtypeStruct((8, D), F32),
            jax.ShapeDtypeStruct((8, PMAX), F32),
        ],
        scratch_shapes=[
            pltpu.VMEM((D, HEADW), F32),
            pltpu.VMEM((D, HEADW), BF),
            semaphores(group),
        ],
        compiler_params=params(60),
        cost_estimate=pl.CostEstimate(
            flops=6 * rows * D * HEADW, bytes_accessed=8 << 20, transcendentals=0
        ),
    )(x, targets, mask, *arrays, gain)


def backward_body(names, extra, group, out_group, *refs):
    first, attn, ffn = "in" in names, "qkv" in names, "gu" in names
    take = Taker(refs)
    dout_ref = take()
    if attn:
        x_ref, qkv_ref, prob_ref, mixed_ref = take(4)
    if ffn:
        mid_ref, gu_ref = take(2)
    concat_ref = take() if first else None
    extras = {extra: take()} if extra else {}
    arrays = take.refs[: group.parts]
    take(group.parts)
    gain_ref = take()
    if attn:
        cos_ref, sin_ref, code_ref = take(3)
    dx_ref = None if first else take()
    out_arrays = take.refs[: out_group.parts]
    take(out_group.parts)
    if attn:
        dg_attn, db_ref = take(2)
    if ffn:
        dg_ffn = take()
    loads = [n for n in names if n != "in"]
    w = take.named(loads)
    acc = take.named(names)
    grads = take.named(names)
    sems, out_sems = take(2)
    if attn:
        dqkv_ref = take()
    if ffn:
        dgu_ref = take()
    step = pl.program_id(0)
    me, core = place(group)
    made = copies(group, arrays, me, down_fields(w), sems, outward=False)
    out_core = place(out_group)[1]
    sent = copies(
        out_group, out_arrays, me, {**down_fields(grads), **extras}, out_sems, outward=True
    )

    @pl.when(step == 0)
    def _():
        start_copies(group, made, core)
        for ref in acc.values():
            ref[...] = jnp.zeros_like(ref)
        if attn:
            dg_attn[...] = jnp.zeros_like(dg_attn)
            db_ref[...] = jnp.zeros_like(db_ref)
        if ffn:
            dg_ffn[...] = jnp.zeros_like(dg_ffn)
        wait_copies(made, list(made))

    dout = dout_ref[...]
    rows = dout.shape[0]
    grad_mid = dout
    if ffn:
        dout_low = dout.astype(BF)
        gate = gu_ref[:, :FF].astype(F32)
        up = gu_ref[:, FF:].astype(F32)
        sig = sigmoid_of(gate)
        silu = gate * sig
        acc["d"][...] += dot_tn((silu * up).astype(BF), dout_low)
        grad_hidden = dot_nt(dout_low, w["d"][...])
        dgu_ref[:, :FF] = (grad_hidden * up * (sig + silu * (1.0 - sig))).astype(BF)
        dgu_ref[:, FF:] = (grad_hidden * silu).astype(BF)
        u_mid, inverse_mid = unit(mid_ref[...])
        gain_mid = gain_ref[1:2, :]
        acc["gu"][...] += dot_tn((u_mid * gain_mid).astype(BF), dgu_ref[...])
        grad_mid, dgain_mid = rms_backward(
            u_mid, inverse_mid, gain_mid, dot_nt(dgu_ref[...], w["gu"][...])
        )
        dg_ffn[...] += dgain_mid
        grad_mid = grad_mid + dout
    grad_x = grad_mid
    if attn:
        grad_attn_low = grad_mid.astype(BF)
        acc["o"][...] += dot_tn(mixed_ref[...], grad_attn_low)
        grad_mixed = dot_nt(grad_attn_low, w["o"][...]).astype(BF)
        spots = [(b, p) for p in range(PAIRS) for b in range(rows // BUCKET)]
        dprobs = []
        for b, p in spots:
            here = slice(b * BUCKET, (b + 1) * BUCKET)
            dm2 = two_blocks(grad_mixed[here, p * LANES : (p + 1) * LANES])
            v = qkv_ref[here, 2 * D + p * LANES : 2 * D + (p + 1) * LANES]
            dprobs.append(dot_nt(v, dm2))
        dscores = []
        for (b, p), dprob in zip(spots, dprobs):
            prob = prob_ref[b * BUCKET : (b + 1) * BUCKET, p * LANES : (p + 1) * LANES].astype(F32)
            ds = prob * (dprob - jnp.sum(prob * dprob, axis=0, keepdims=True))
            dscores.append(ds.astype(BF))
        for p in range(PAIRS):
            other_sum = jnp.zeros((8, LANES), F32)
            same_sum = jnp.zeros((8, LANES), F32)
            for b in range(rows // BUCKET):
                ds = dscores[p * (rows // BUCKET) + b].astype(F32)
                same = code_ref[b * BUCKET : (b + 1) * BUCKET, :] > 0.5
                same_sum = same_sum + rows_to_eight(jnp.where(same, ds, 0.0))
                other_sum = other_sum + rows_to_eight(jnp.where(same, 0.0, ds))
            db_ref[p * 8 : (p + 1) * 8, :] += other_sum
            db_ref[(PAIRS + p) * 8 : (PAIRS + p + 1) * 8, :] += same_sum
        for (b, p), ds in zip(spots, dscores):
            here = slice(b * BUCKET, (b + 1) * BUCKET)
            cols = slice(p * LANES, (p + 1) * LANES)
            kcols = slice(D + p * LANES, D + (p + 1) * LANES)
            vcols = slice(2 * D + p * LANES, 2 * D + (p + 1) * LANES)
            cos = cos_ref[here, :] * HD ** (-0.5)
            sin = sin_ref[here, :] * HD ** (-0.5)
            dm2 = two_blocks(grad_mixed[here, cols])
            dq = fold_blocks(dot_tn(ds, qkv_ref[here, kcols]))
            dk = dot_nn(ds, two_blocks(qkv_ref[here, cols]))
            dv = dot_nn(prob_ref[here, cols], dm2)
            dqkv_ref[here, cols] = (dq * cos + swap_halves(dq * sin)).astype(BF)
            dqkv_ref[here, kcols] = (dk * cos + swap_halves(dk * sin)).astype(BF)
            dqkv_ref[here, vcols] = dv.astype(BF)
        u, inverse = unit(x_ref[...])
        gain_row = gain_ref[0:1, :]
        acc["qkv"][...] += dot_tn((u * gain_row).astype(BF), dqkv_ref[...])
        grad_x, dgain = rms_backward(u, inverse, gain_row, dot_nt(dqkv_ref[...], w["qkv"][...]))
        dg_attn[...] += dgain
        grad_x = grad_x + grad_mid
    if first:
        acc["in"][...] += dot_tn(grad_x.astype(BF), concat_ref[...])
    else:
        dx_ref[...] = grad_x

    @pl.when(step == pl.num_programs(0) - 1)
    def _():
        for name in names:
            grads[name][...] = acc[name][...].astype(BF)
        start_copies(out_group, sent, out_core)
        wait_copies(sent, list(sent))


def backward_layer(names, dout, saved, concat, extra, group, arrays, out_group, gain_pair, tables):
    first, attn, ffn = "in" in names, "qkv" in names, "gu" in names
    rows = dout.shape[0]
    args = [dout, *saved] + ([concat] if first else [])
    in_specs = [rows_spec(a.shape[1]) for a in args]
    if extra:
        args.append(extra[1])
        in_specs.append(whole_spec(extra[1].shape))
    args += [*arrays, gain_pair]
    in_specs += [any_spec()] * group.parts + [whole_spec(gain_pair.shape)]
    if attn:
        args += list(tables)
        in_specs += [rows_spec(LANES)] * 3
    out_specs, out_shape = [], []
    if not first:
        out_specs.append(rows_spec(D))
        out_shape.append(jax.ShapeDtypeStruct((rows, D), F32))
    slots = (out_group.shards, out_group.rows, out_group.width)
    out_specs += [any_spec()] * out_group.parts
    out_shape += [jax.ShapeDtypeStruct(slots, BF)] * out_group.parts
    small = ([(8, D), (48, LANES)] if attn else []) + ([(8, D)] if ffn else [])
    out_specs += [whole_spec(shape) for shape in small]
    out_shape += [jax.ShapeDtypeStruct(shape, F32) for shape in small]
    scratch = [pltpu.VMEM(WEIGHTS[n], BF) for n in names if n != "in"]
    scratch += [pltpu.VMEM(WEIGHTS[n], F32) for n in names]
    scratch += [pltpu.VMEM(WEIGHTS[n], BF) for n in names]
    scratch += [semaphores(group), semaphores(out_group)]
    scratch += [pltpu.VMEM((TILE, QKV), BF)] if attn else []
    scratch += [pltpu.VMEM((TILE, 2 * FF), BF)] if ffn else []
    size = sum(WEIGHTS[n][0] * WEIGHTS[n][1] for n in names)
    got = pl.pallas_call(
        functools.partial(backward_body, names, extra[0] if extra else None, group, out_group),
        grid=(rows // TILE,),
        in_specs=in_specs,
        out_specs=out_specs,
        out_shape=out_shape,
        scratch_shapes=scratch,
        compiler_params=params(60),
        cost_estimate=pl.CostEstimate(
            flops=4 * rows * size, bytes_accessed=48 * size, transcendentals=0
        ),
    )(*args)
    got = list(got)
    grad = None if first else got.pop(0)
    return grad, got[: out_group.parts], got[out_group.parts :]


def partners(sizes, fsdp_mask, dp_mask):
    fsdp, dp = sizes
    return [
        (f * dp + d, (f ^ fsdp_mask) * dp + (d ^ dp_mask)) for f in range(fsdp) for d in range(dp)
    ]


def slot_of(offset, masks):
    slot = 0
    for bit, mask in enumerate(masks):
        slot = slot + jnp.where((offset & mask) != 0, 1 << bit, 0)
    return slot


def swap(x, sizes, fsdp_mask, dp_mask):
    return lax.ppermute(x, AXES, partners(sizes, fsdp_mask, dp_mask))


def reorder(slots, masks):
    me = lax.axis_index("fsdp")
    return jnp.stack(
        [
            lax.dynamic_index_in_dim(slots, slot_of(me ^ j, masks), 0, keepdims=False)
            for j in range(slots.shape[0])
        ]
    )


class Gather:
    def __init__(self, parts, sizes):
        self.sizes = sizes
        self.four = len(parts) == 4
        self.mine = by_place(parts)[0][None]
        self.masks = masks_of(sizes[0])
        self.last = self.masks.pop() if self.four else 0
        self.got = ()

    def land(self):
        if self.got:
            self.mine = jnp.concatenate([self.mine, *self.got], axis=0)
            self.got = ()
        return self.mine

    def move(self, after=None):
        mine = self.land()
        if after is not None:
            mine, after.got = lax.optimization_barrier((mine, after.got))
        self.mine = mine
        self.got = (swap(mine, self.sizes, self.masks.pop(0), 0),)

    def ring(self):
        mine = self.land()
        self.got = (swap(mine, self.sizes, self.last, 0), swap(mine, self.sizes, 0, 2))

    def hold(self, x):
        x, self.got = lax.optimization_barrier((x, self.got))
        return x

    def arrays(self):
        if not self.four:
            mine = self.land()
            return mine, swap(mine, self.sizes, 0, 1)
        near, far = self.got
        half = near.shape[0] // 2
        corner = (
            swap(far[:half], self.sizes, self.last, 0),
            swap(near[half:], self.sizes, 0, 2),
        )
        mine = jnp.concatenate([self.mine, near], axis=0)
        far = jnp.concatenate([far, *corner], axis=0)
        return mine, swap(mine, self.sizes, 0, 1), far, swap(far, self.sizes, 0, 1)


def by_place(parts):
    place = lax.axis_index("dp") & (len(parts) - 1)
    found = []
    for distance in range(len(parts)):
        one = parts[distance]
        for other in range(1, len(parts)):
            one = jnp.where(place == other, parts[other ^ distance], one)
        found.append(one)
    return found


def by_core(mine, other):
    core = lax.axis_index("dp") & 1
    return jnp.where(core == 0, mine, other), jnp.where(core == 0, other, mine)


def add(a, b):
    return (a.astype(F32) + b.astype(F32)).astype(BF)


def to_slots(shards, masks):
    me = lax.axis_index("fsdp")
    slots = [None] * shards.shape[0]
    for v in range(shards.shape[0]):
        slots[slot_index(v, masks)] = lax.dynamic_index_in_dim(shards, me ^ v, 0, keepdims=False)
    return jnp.stack(slots)


class Scatter:
    def __init__(self, keep, give, sizes):
        self.sizes = sizes
        self.keep = keep
        self.got = swap(give, sizes, 0, 1)
        self.moves = [(mask, 0) for mask in reversed(masks_of(sizes[0]))]
        dp_mask = 2
        while dp_mask < sizes[1]:
            self.moves.append((0, dp_mask))
            dp_mask *= 2

    def ready(self):
        if self.moves and self.moves[0][0]:
            half = self.keep.shape[0] // 2
            self.away = add(self.keep[half:], self.got[half:])
            self.keep = add(self.keep[:half], self.got[:half])
        else:
            self.keep = add(self.keep, self.got)
            self.away = self.keep

    def move(self):
        self.got = swap(self.away, self.sizes, *self.moves.pop(0))

    def total(self):
        return add(self.keep, self.got)[0]


def hold(x, *scatters):
    for one in scatters:
        one.ready()
    held = lax.optimization_barrier((x, [(one.keep, one.away) for one in scatters]))
    for one, (keep, away) in zip(scatters, held[1]):
        one.keep, one.away = keep, away
        one.move()
    return held[0]


def after_landing(x, scatters):
    x, landed = lax.optimization_barrier((x, [one.got for one in scatters]))
    for one, got in zip(scatters, landed):
        one.got = got
    return x


def pad_rows(x, rows):
    return jnp.pad(x, ((0, 0),) * (x.ndim - 2) + ((0, rows - x.shape[-2]), (0, 0)))


def to_whole(group, whole, arrays, sizes):
    masks = masks_of(sizes[0])
    arrays = [reorder(a, masks) for a in by_place(arrays)]
    fields = group.unpack(arrays)
    fields = {n: p.reshape(1, p.shape[0] * p.shape[1], p.shape[2]) for n, p in fields.items()}
    return whole.pack(fields)


def from_whole(group, whole, arrays, sizes):
    fsdp = sizes[0]
    fields = whole.unpack(arrays)
    fields = {n: p.reshape(fsdp, p.shape[1] // fsdp, p.shape[2]) for n, p in fields.items()}
    arrays = group.pack(fields)
    if group.parts == 1:
        return arrays
    masks = masks_of(fsdp)
    return by_core(*[to_slots(a, masks) for a in arrays])


def rotary_tables(time_ids):
    frequency = THETA ** (-2.0 * jnp.arange(HD // 2, dtype=F32) / HD)
    phase = time_ids.astype(F32)[:, None] * frequency[None, :]
    cos, sin = jnp.cos(phase), jnp.sin(phase)
    return jnp.concatenate([cos] * 4, axis=1), jnp.concatenate([-sin, sin, -sin, sin], axis=1)


def live_slots(lengths):
    return jnp.arange(BUCKET, dtype=jnp.int32)[None, :] < lengths[:, None]


def target_mask(size_ids, lengths):
    widths = jnp.where(live_slots(lengths).reshape(size_ids.shape), PMAX >> (4 - size_ids), 0)
    return (jnp.arange(PMAX, dtype=jnp.int32)[None, :] < widths[:, None]).astype(F32)


def code_table(variate_ids, lengths):
    variates = variate_ids.reshape(-1, BUCKET)
    same = (variates[:, :, None] == variates[:, None, :]).astype(F32)
    code = jnp.where(live_slots(lengths)[:, :, None], same, -1.0).reshape(-1, BUCKET)
    return jnp.concatenate([code, code], axis=1)


def patch_concat(patches, size_ids):
    pieces = []
    for size_id in range(5):
        span = PMAX >> 4 - size_id
        chosen = (size_ids == size_id)[:, None]
        pieces.append(jnp.where(chosen, patches[:, :span], jnp.zeros((), BF)))
    pieces.append(jnp.zeros((patches.shape[0], 2 * PMAX - IN_CAT), BF))
    return jnp.concatenate(pieces, axis=1)


def adam_update(master, clipped, first_old, second_old, matrix):
    first_new = BETA_ONE * first_old + (1.0 - BETA_ONE) * clipped
    second_new = BETA_TWO * second_old + (1.0 - BETA_TWO) * clipped * clipped
    first_hat = first_new * (1.0 / (1.0 - BETA_ONE**STEP_NUM))
    second_hat = second_new * (1.0 / (1.0 - BETA_TWO**STEP_NUM))
    direction = first_hat / (jnp.sqrt(second_hat) + ADAM_EPS)
    if matrix:
        master_new = master - RATE_MATRIX * (direction + WEIGHT_DECAY * master)
    else:
        master_new = master - RATE_GAIN * direction
    return (master_new, first_new, second_new)


def beside(x, sizes, across):
    moves = [(mask, 0) for mask in masks_of(sizes[0])]
    if across:
        moves = []
    dp_mask = 2 if across else 1
    while dp_mask < (sizes[1] if across else 2):
        moves.append((0, dp_mask))
        dp_mask *= 2
    for fsdp_mask, dp_mask in moves:
        x = x + swap(x, sizes, fsdp_mask, dp_mask)
    return x


STACKED = ("qkv", "o", "gu", "d")


def update_body(groups, layers, *refs):
    take = Taker(refs)
    scale_ref = take()
    parts = [take(group.parts) for group in groups]
    names = STACKED + ("head",)
    states = [take.named(names) for _ in range(3)]
    fresh = [take.named(names) for _ in range(3)]
    scale = scale_ref[0, 0]

    def one(name, index, grad):
        old = [state[name][index] for state in states]
        new = adam_update(old[0], grad.astype(F32) * scale, old[1], old[2], True)
        for target, value in zip(fresh, new):
            target[name][index] = value

    def layer_step(layer, place_here):
        for group, group_parts, at_layer in zip(groups, parts, layers):
            if at_layer != layer:
                continue
            for part, at, name, start, width in group.pieces:
                if name == "in":
                    continue
                first, count, _ = group.row_span(name)
                grad = group_parts[part ^ place_here][0:count, at : at + width]
                cols = slice(start, start + width)
                if name == "head":
                    one("head", (slice(0, count), cols), grad)
                else:
                    rows = slice(first, first + count) if name[0] == "d" else slice(0, count)
                    one(name[0] if name[0] == "d" else name, (0, rows, cols), grad)

    core = lax.axis_index("dp") & 1
    for layer in range(L):
        for which in range(2):
            chosen = (pl.program_id(0) == layer) & (core == which)
            pl.when(chosen)(functools.partial(layer_step, layer, which))


def update(groups, layers, parts, scale, states):
    def spec(x):
        if x.ndim == 2:
            return whole_spec(x.shape)
        return pl.BlockSpec((1,) + x.shape[1:], lambda i: (i, 0, 0))

    flat = [x for state in states for x in state]
    got = pl.pallas_call(
        functools.partial(update_body, groups, layers),
        grid=(L,),
        in_specs=[pl.BlockSpec(memory_space=pltpu.SMEM)]
        + [whole_spec(p.shape) for pair in parts for p in pair]
        + [spec(x) for x in flat],
        out_specs=[spec(x) for x in flat],
        out_shape=[jax.ShapeDtypeStruct(x.shape, F32) for x in flat],
        compiler_params=params(60),
        cost_estimate=pl.CostEstimate(flops=1 << 24, bytes_accessed=18 << 20, transcendentals=0),
    )(scale.reshape(1, 1), *[p for pair in parts for p in pair], *flat)
    return [got[i : i + len(states[0])] for i in range(0, len(flat), len(states[0]))]


def per_device(sizes, *args):
    patches, targets, size_ids, time_ids, variate_ids, lengths = args[:6]
    masters = args[6:14]
    firsts = args[14:22]
    seconds = args[22:30]
    w_in, w_qkv, w_o, w_gu, w_down, w_head, gains, var_bias = masters
    own = w_head.shape[0]
    down_rows = w_down.shape[1]
    direct = own % 16 == 0 and down_rows % 16 == 0
    attn_fields = [("qkv", QKV), ("o", D)]
    ffn_fields = [("d0", D), ("d1", D), ("gu", 2 * FF), ("d2", D)]
    plan = [
        (("in",) + ATTN, [("in", 2 * PMAX)] + attn_fields),
        (FFN, ffn_fields),
        (ATTN + FFN, attn_fields + ffn_fields),
        (ATTN + FFN, attn_fields + ffn_fields + [("head", HEADW)]),
    ]
    layers = [0, 0, 1, 2]
    count = len(plan)
    def groups_of(fields, parts):
        many = [Group(f, p, sizes[0], own, down_rows) for f, p in zip(fields, parts)]
        if direct:
            return many, many
        return many, [Group(f, p, 1, D, FF) for f, p in zip(fields, parts)]

    fields = [f for _, f in plan]
    groups, wholes = groups_of(fields, [2] * count)
    in_fields = [fields[0] + fields[1], fields[2], fields[3]]
    in_groups, in_wholes = groups_of(in_fields, [4, 2, 4])
    sources = [0, 0, 1, 2]

    in_rows = jnp.concatenate(
        [w_in.T, gains.T, jnp.zeros((own, 2 * PMAX - IN_CAT - NGAIN), F32)], axis=1
    ).astype(BF)
    def packed(layer, stacks, head_w=None):
        fields = {m: w[layer].astype(BF) for m, w in zip(("qkv", "o", "gu", "d"), stacks)}
        if layer == L - 1:
            fields["head"] = head_w.astype(BF)
        return in_groups[layer].pack({**fields, "in": in_rows})

    stacks = (w_qkv, w_o, w_gu, w_down)
    first = Gather(packed(0, stacks), sizes)
    first.move()
    stacks, head_w, time_ids = first.hold((stacks, w_head, time_ids))
    second, third = [Gather(packed(layer, stacks, head_w), sizes) for layer in (1, 2)]
    cos, sin = rotary_tables(time_ids)
    while first.masks:
        first.move()
    early = (patches, size_ids, variate_ids, lengths)
    early, second.mine = first.hold((early, second.mine))
    patches, size_ids, variate_ids, lengths = early
    first.ring()
    second.move()
    third.move(second)
    while second.masks:
        second.move()
    while len(third.masks) > 1:
        third.move()

    def arrived(layer):
        arrays = (first, second, third)[layer].arrays()
        return arrays if direct else to_whole(in_groups[layer], in_wholes[layer], arrays, sizes)

    tables = (cos, sin, code_table(variate_ids, lengths))
    concat = patch_concat(patches, size_ids)
    bias_lanes = jnp.repeat(var_bias, HD, axis=2).reshape(L, 2, PAIRS, LANES)
    bias_lanes = jnp.pad(bias_lanes, ((0, 0), (0, 0), (0, 8 - PAIRS), (0, 0)))
    bias_lanes = bias_lanes.reshape(L, 16, LANES)

    stream = concat
    kept = [None] * count
    loaded = []
    gain_pairs = [None] * (L + 1)
    for layer in range(L):
        if layer == 1:
            second.mine, third.got = lax.optimization_barrier((second.land(), third.got))
        loaded.append(arrived(layer))
        if layer == 0:
            third.mine, stream = lax.optimization_barrier((third.land(), stream))
            while third.masks:
                third.move()
        if layer == 1:
            third.ring()
        names = ATTN + FFN if layer else ("in",) + ATTN + FFN
        got = list(
            forward_layer(
                stream,
                names,
                in_wholes[layer],
                loaded[layer],
                gain_pairs[layer],
                bias_lanes[layer],
                tables,
            )
        )
        if layer == 0:
            stream, found = got[:2]
            got = got[2:]
            gain_pairs = [found[0:2], found[2:4], found[4:6], found[6:8]]
            kept[0] = [stream, *got[:3]]
            kept[1] = [got[3], got[5]]
        else:
            kept[layer + 1] = [stream, *got[:4], got[5]]
        stream = got[4]
        for one in (second, third)[layer:]:
            stream = one.hold(stream)
        if layer == 0:
            stream, size_ids, lengths = lax.optimization_barrier((stream, size_ids, lengths))
            mask = target_mask(size_ids, lengths)
            live = jnp.sum(mask)
    grad, head_grad, gain_grad, loss = head(
        stream, targets, mask, in_wholes[-1], loaded[-1], gain_pairs[L]
    )
    raw = [gain_grad, loss]
    totals = [None] * count
    for n in reversed(range(count)):
        names = plan[n][0]
        layer = layers[n]
        grad, arrays, small = backward_layer(
            names,
            grad,
            kept[n],
            concat,
            ("head", head_grad) if n == count - 1 else None,
            in_wholes[sources[n]],
            loaded[sources[n]],
            wholes[n],
            gain_pairs[layer],
            tables,
        )
        raw += small
        if not direct:
            arrays = from_whole(groups[n], wholes[n], arrays, sizes)
        keep, give = arrays
        flying = totals[n + 1 :]
        give = after_landing(give, flying[1:] if n == 1 else flying)
        totals[n] = Scatter(keep, give, sizes)
        if n:
            grad = hold(grad, totals[n], *flying)

    raw = hold(raw, *totals)
    gain_grad, loss, *raw = raw
    gain_grads, bias_grads = {2 * L: gain_grad}, [None] * L
    for n in reversed(range(count)):
        names = plan[n][0]
        layer = layers[n]
        if "qkv" in names:
            gain_grads[2 * layer] = raw.pop(0)
            bias_grads[layer] = raw.pop(0).reshape(2, PAIRS, 8, 2, HD)
        if "gu" in names:
            gain_grads[2 * layer + 1] = raw.pop(0)
    gain_grads = [jnp.sum(gain_grads[g], axis=0) for g in range(NGAIN)]
    bias_grads = jnp.sum(jnp.stack(bias_grads), axis=(3, 5)).reshape(L, 2, H)

    small = jnp.concatenate([jnp.sum(loss)[None], live[None], bias_grads.reshape(-1)])
    small = jnp.pad(small, (0, D - small.shape[0]))
    rows = jnp.stack(gain_grads + [small])
    rows = beside(rows, sizes, across=True)
    pending = list(zip(range(count), totals))
    own_parts = [None] * count
    first = True
    while pending:
        for n, one in pending:
            if not one.moves:
                own_parts[n] = one.total()
        pending = [(n, one) for n, one in pending if one.moves]
        if not pending:
            break
        if not first:
            hold((), *[one for _, one in pending])
        first = False
    squares = jnp.zeros((1, 1), F32)
    for n, part in enumerate(own_parts):
        squares = squares + groups[n].squares(part)
    rows = beside(rows + jnp.pad(squares, ((NGAIN, 0), (D - 1, 0))), sizes, across=False)
    squares = rows[NGAIN, D - 1]
    loss_sum, total_count = rows[NGAIN, 0], rows[NGAIN, 1]
    inverse_count = 1.0 / total_count
    bias_grad = rows[NGAIN, 2 : 2 + var_bias.size].reshape(var_bias.shape) * inverse_count
    at_row = lax.broadcasted_iota(jnp.int32, rows.shape, 0)
    at_col = lax.broadcasted_iota(jnp.int32, rows.shape, 1)
    counted = (at_row < NGAIN) | ((at_col >= 2) & (at_col < 2 + var_bias.size))
    squares = squares + jnp.sum(jnp.where(counted, jnp.square(rows), 0.0))
    gain_all = rows[:NGAIN]
    gain_own = lax.dynamic_slice_in_dim(gain_all, lax.axis_index("fsdp") * own, own, axis=1)

    grad_norm = jnp.sqrt(squares) * inverse_count
    factor = jnp.minimum(1.0, CLIP_NORM / grad_norm)
    scale = factor * inverse_count


    pairs = [(part, swap(part, sizes, 0, 1)) for part in own_parts]
    whole_parts = [by_core(*pair) for pair in pairs]
    fresh = [None] * 8
    if direct:
        states = [[group_of[m] for m in (1, 2, 3, 4, 5)] for group_of in (masters, firsts, seconds)]
        new = update(groups, layers, pairs, scale, states)
        for at, m in enumerate((1, 2, 3, 4, 5)):
            fresh[m] = tuple(kind[at] for kind in new)
    pieces = [groups[n].unpack(whole_parts[n]) for n in range(count)]
    matrices = [[piece[m] for piece in pieces if m in piece] for m in STACKED]
    gradients = [pieces[0]["in"][:, :IN_CAT].T] + [jnp.stack(m) for m in matrices]
    gradients += [pieces[-1]["head"], gain_own]
    clipped = [g.astype(F32) * scale for g in gradients] + [bias_grad * factor]
    for m in range(8):
        if fresh[m] is None:
            fresh[m] = adam_update(masters[m], clipped[m], firsts[m], seconds[m], m < 6)
    return (
        (loss_sum, total_count, grad_norm)
        + tuple(f[0] for f in fresh)
        + tuple(f[1] for f in fresh)
        + tuple(f[2] for f in fresh)
    )


def solution(mesh):
    sizes = (mesh.shape["fsdp"], mesh.shape["dp"])
    tokens = P(("fsdp", "dp"))
    tokens_two = P(("fsdp", "dp"), None)
    columns = P(None, "fsdp")
    stacked = P(None, "fsdp", None)
    states = (columns, stacked, stacked, stacked, stacked, P("fsdp", None), columns, P())
    in_specs = (tokens_two, tokens_two, tokens, tokens, tokens, tokens) + states * 3
    out_specs = (P(), P(), P()) + states * 3
    return jax.shard_map(
        functools.partial(per_device, sizes),
        mesh=mesh,
        in_specs=in_specs,
        out_specs=out_specs,
        check_vma=False,
    )
```

```python
import functools

import jax
import jax.numpy as jnp
from jax import lax
from jax.experimental import pallas as pl
from jax.experimental.pallas import tpu as pltpu
from jax.sharding import PartitionSpec as P

D = 384
H = 6
HD = 64
FF = 1024
PMAX = 128
NQ = 9
BUCKET = 64
L = 3
STEP_NUM = 10
IN_CAT = 248
NGAIN = 7
QKV = 3 * D
HEADW = NQ * PMAX
PAIRS = H // 2
LANES = 2 * HD

TILE = 256
FORWARD_TILE = 1024

EPS_NORM = 1e-05
SMOOTH = 0.5
THETA = 10000.0
MASKED_SCORE = -1e30
CLIP_NORM = 0.001
BETA_ONE = 0.9
BETA_TWO = 0.95
ADAM_EPS = 1e-08
WEIGHT_DECAY = 0.1
RATE_MATRIX = 0.15
RATE_GAIN = 0.8

BF = jnp.bfloat16
F32 = jnp.float32
AXES = ("fsdp", "dp")


def dot_nn(a, b):
    return lax.dot_general(a, b, (((1,), (0,)), ((), ())), preferred_element_type=F32)


def dot_nt(a, b):
    return lax.dot_general(a, b, (((1,), (1,)), ((), ())), preferred_element_type=F32)


def dot_tn(a, b):
    return lax.dot_general(a, b, (((0,), (0,)), ((), ())), preferred_element_type=F32)


def unit(x):
    inverse = lax.rsqrt(jnp.mean(x * x, axis=-1, keepdims=True) + EPS_NORM)
    return x * inverse, inverse


def rms_backward(u, inverse, gain_row, grad):
    grad_unit = grad * gain_row
    grad_x = inverse * (grad_unit - u * jnp.mean(grad_unit * u, axis=-1, keepdims=True))
    return grad_x, rows_to_eight(grad * u)


def rows_to_eight(x):
    return jnp.sum(x.reshape(x.shape[0] // 8, 8, x.shape[1]), axis=0)


def lane_of(shape):
    return lax.broadcasted_iota(jnp.int32, shape, len(shape) - 1)


def swap_halves(x):
    lane = lane_of(x.shape)
    return jnp.where((lane & 32) == 0, pltpu.roll(x, 96, 1), pltpu.roll(x, 32, 1))


def low_lanes(shape):
    return lane_of(shape) < HD


def two_blocks(x):
    keep = low_lanes(x.shape)
    zero = jnp.zeros_like(x)
    return jnp.concatenate([jnp.where(keep, x, zero), jnp.where(keep, zero, x)], axis=0)


def fold_blocks(x):
    return jnp.where(low_lanes((BUCKET, LANES)), x[:BUCKET], x[BUCKET:])


def sigmoid_of(x):
    return 0.5 * jnp.tanh(0.5 * x) + 0.5


class Group:
    def __init__(self, fields, parts, shards, rows, down_rows):
        self.parts, self.shards, self.rows, self.down_rows = parts, shards, rows, down_rows
        used = sum(width for _, width in fields)
        self.width = -(-used // (parts * LANES)) * LANES
        self.pad = parts * self.width - used
        self.fields = fields
        self.pieces = []
        at = 0
        for name, width in fields:
            done = 0
            while done < width:
                part = (at + done) // self.width
                take = min(width - done, (part + 1) * self.width - at - done)
                self.pieces.append((part, at + done - part * self.width, name, done, take))
                done += take
            at += width
        masks = masks_of(shards)
        self.slots = [slot_index(v, masks) if parts > 1 else v for v in range(shards)]

    def row_span(self, name):
        if name[0] == "d":
            first = int(name[1]) * self.rows
            return first, min(self.rows, self.down_rows - first), self.down_rows
        return 0, self.rows, self.rows

    def pack(self, fields):
        fields = dict(fields)
        if "d" in fields:
            down = fields.pop("d")
            for i in range(3):
                part = down[..., i * self.rows : (i + 1) * self.rows, :]
                fields[f"d{i}"] = pad_rows(part, self.rows)
        parts = [[] for _ in range(self.parts)]
        for part, _, name, start, width in self.pieces:
            parts[part].append(fields[name][..., start : start + width])
        if self.pad:
            like = parts[-1][0]
            parts[-1].append(jnp.zeros(like.shape[:-1] + (self.pad,), like.dtype))
        return tuple(jnp.concatenate(p, axis=-1) for p in parts)

    def unpack(self, parts):
        found = {}
        for part, at, name, _, width in self.pieces:
            got = parts[part][..., at : at + width]
            found[name] = jnp.concatenate([found[name], got], axis=-1) if name in found else got
        if "d0" in found:
            downs = [found.pop(f"d{i}") for i in range(3)]
            downs[2] = downs[2][..., : self.row_span("d2")[1], :]
            found["d"] = jnp.concatenate(downs, axis=-2)
        return found


    def squares(self, own):
        own, core = lax.optimization_barrier((own, lax.axis_index("dp") & 1))
        row = lax.broadcasted_iota(jnp.int32, own.shape, 0)
        col = lax.broadcasted_iota(jnp.int32, own.shape, 1) + core * self.width
        used = col < sum(width for _, width in self.fields)
        for part, at, name, _, width in self.pieces:
            count = self.row_span(name)[1]
            if count < self.rows:
                start = part * self.width + at
                used = used & ((row < count) | (col < start) | (col >= start + width))
        return jnp.sum(jnp.where(used, jnp.square(own.astype(F32)), 0.0)).reshape(1, 1)


def place(group):
    if group.shards == 1:
        return 0, 0
    return lax.axis_index("fsdp"), lax.axis_index("dp") & (group.parts - 1)


def copies(group, arrays, me, targets, sems, outward):
    made = {}
    for n, (part, at, name, start, width) in enumerate(group.pieces):
        if name not in targets:
            continue
        first, count, stride = group.row_span(name)
        for v in range(group.shards):
            owner = v if group.parts == 1 else me ^ v
            row = owner * stride + first
            if not isinstance(row, int):
                row = pl.multiple_of(row, 16)
            whole = targets[name].at[pl.ds(row, count), pl.ds(start, width)]
            slots = [
                a.at[group.slots[v], pl.ds(0, count), pl.ds(at, width)] for a in arrays
            ]
            ends = [(whole, slot) if outward else (slot, whole) for slot in slots]
            pair = [functools.partial(pltpu.make_async_copy, a, b, sems.at[n, v]) for a, b in ends]
            made.setdefault(name, []).append((part, pair))
    return made


def start_copies(group, made, core):
    def go(which):
        for items in made.values():
            for part, pair in items:
                pair[part ^ which]().start()

    if group.shards == 1 or group.parts == 1:
        go(0)
    else:
        for which in range(group.parts):
            pl.when(core == which)(functools.partial(go, which))


def wait_copies(made, names):
    for name in names:
        for _, pair in made.get(name, []):
            pair[0]().wait()


def slot_index(v, masks):
    return sum((1 << bit) for bit, mask in enumerate(masks) if v & mask)


def masks_of(size):
    masks = []
    size //= 2
    while size:
        masks.append(size)
        size //= 2
    return masks


def any_spec():
    return pl.BlockSpec(memory_space=pl.ANY)


WEIGHTS = {"in": (D, 2 * PMAX), "qkv": (D, QKV), "o": (D, D), "gu": (D, 2 * FF), "d": (FF, D)}


def semaphores(group):
    return pltpu.SemaphoreType.DMA((len(group.pieces), group.shards))


class Taker:
    def __init__(self, refs):
        self.refs = list(refs)

    def __call__(self, count=1):
        taken, self.refs = self.refs[:count], self.refs[count:]
        return taken[0] if count == 1 else taken

    def named(self, names):
        return dict(zip(names, [self() for _ in names]))


def down_fields(targets):
    targets = dict(targets)
    if "d" in targets:
        down = targets.pop("d")
        targets.update(d0=down, d1=down, d2=down)
    return targets


ATTN, FFN = ("qkv", "o"), ("gu", "d")


def forward_body(names, group, *refs):
    first, attn, ffn = "in" in names, "qkv" in names, "gu" in names
    take = Taker(refs)
    x_ref = take()
    arrays = take.refs[: group.parts]
    take(group.parts)
    gain_ref = None if first else take()
    if attn:
        bias_ref, cos_ref, sin_ref, code_ref = take(4)
    if first:
        base_ref, rows_ref = take(2)
    if attn:
        qkv_ref, prob_ref, mixed_ref, mid_ref = take(4)
    if ffn:
        out_ref, gu_ref = take(2)
    w = take.named(names)
    sems = take()
    if first:
        gain_ref = take()
    me, core = place(group)
    made = copies(group, arrays, me, down_fields(w), sems, outward=False)
    opening = pl.program_id(0) == 0
    early = [n for n in made if n in ("in", "qkv")]
    late = [n for n in made if n not in early]

    @pl.when(opening)
    def _():
        start_copies(group, made, core)
        wait_copies(made, early)
        if first:
            turned = w["in"][:, PMAX:].astype(F32).T
            gain_ref[...] = turned[IN_CAT - PMAX : IN_CAT - PMAX + 8, :]
            rows_ref[...] = gain_ref[...]

    def rest():
        pl.when(opening)(functools.partial(wait_copies, made, late))

    if attn:
        if first:
            stream = dot_nt(x_ref[...], w["in"][...])
            base_ref[...] = stream
        else:
            stream = x_ref[...]
        rows = stream.shape[0]
        normed = (unit(stream)[0] * gain_ref[0:1, :]).astype(BF)
        cos = cos_ref[...]
        sin = sin_ref[...]
        qk = dot_nn(normed, w["qkv"][:, : 2 * D])
        for j in range(2 * PAIRS):
            cols = slice(j * LANES, (j + 1) * LANES)
            qkv_ref[:, cols] = (qk[:, cols] * cos + swap_halves(qk[:, cols]) * sin).astype(BF)
        qkv_ref[:, 2 * D :] = dot_nn(normed, w["qkv"][:, 2 * D :]).astype(BF)
        spots = [(b, p) for b in range(rows // BUCKET) for p in range(PAIRS)]
        scores = []
        for b, p in spots:
            here = slice(b * BUCKET, (b + 1) * BUCKET)
            q = qkv_ref[here, p * LANES : (p + 1) * LANES]
            k = qkv_ref[here, D + p * LANES : D + (p + 1) * LANES]
            scores.append(dot_nt(k, two_blocks(q)))
        probs = []
        for (b, p), score in zip(spots, scores):
            code = code_ref[b * BUCKET : (b + 1) * BUCKET, :]
            bias = jnp.where(code > 0.5, bias_ref[p + 8 : p + 9, :], bias_ref[p : p + 1, :])
            score = jnp.where(code < -0.5, MASKED_SCORE, score * HD ** (-0.5) + bias)
            e = jnp.exp(score - jnp.max(score, axis=0, keepdims=True))
            probs.append((e * (1.0 / jnp.sum(e, axis=0, keepdims=True))).astype(BF))
        for (b, p), prob in zip(spots, probs):
            here = slice(b * BUCKET, (b + 1) * BUCKET)
            cols = slice(p * LANES, (p + 1) * LANES)
            v = qkv_ref[here, 2 * D + p * LANES : 2 * D + (p + 1) * LANES]
            prob_ref[here, cols] = prob
            mixed_ref[here, cols] = fold_blocks(dot_tn(prob, v)).astype(BF)
        rest()
        middle = stream + dot_nn(mixed_ref[...], w["o"][...])
        mid_ref[...] = middle
    else:
        rest()
        middle = x_ref[...]
    if ffn:
        ffn_in = (unit(middle)[0] * gain_ref[1:2, :]).astype(BF)
        gate_up = dot_nn(ffn_in, w["gu"][...])
        gu_ref[...] = gate_up.astype(BF)
        gate = gate_up[:, :FF]
        hidden = (gate * sigmoid_of(gate) * gate_up[:, FF:]).astype(BF)
        out_ref[...] = middle + dot_nn(hidden, w["d"][...])


def rows_spec(width, tile=TILE):
    return pl.BlockSpec((tile, width), lambda i: (i, 0))


def whole_spec(shape):
    zeros = (0,) * len(shape)
    return pl.BlockSpec(shape, lambda i: zeros)


def params(limit):
    return pltpu.CompilerParams(
        dimension_semantics=("arbitrary",), vmem_limit_bytes=limit * 1024 * 1024
    )


def forward_layer(x, names, group, arrays, gain_pair, bias_rows, tables):
    first, attn, ffn = "in" in names, "qkv" in names, "gu" in names
    rows = x.shape[0]
    args = [x, *arrays]
    in_specs = [rows_spec(x.shape[1], FORWARD_TILE)] + [any_spec()] * group.parts
    if not first:
        args.append(gain_pair)
        in_specs.append(whole_spec(gain_pair.shape))
    if attn:
        args += [bias_rows, *tables]
        in_specs += [whole_spec(bias_rows.shape)] + [rows_spec(LANES, FORWARD_TILE)] * 3
    outs = [(D, F32)] if first else []
    outs += [(QKV, BF), (D, BF), (D, BF), (D, F32)] if attn else []
    outs += [(D, F32), (2 * FF, BF)] if ffn else []
    out_specs = [rows_spec(w, FORWARD_TILE) for w, _ in outs]
    out_shape = [jax.ShapeDtypeStruct((rows, w), t) for w, t in outs]
    scratch = [pltpu.VMEM(WEIGHTS[n], BF) for n in names] + [semaphores(group)]
    if first:
        out_specs.insert(1, whole_spec((8, D)))
        out_shape.insert(1, jax.ShapeDtypeStruct((8, D), F32))
        scratch.append(pltpu.VMEM((8, D), F32))
    size = sum(WEIGHTS[n][0] * WEIGHTS[n][1] for n in names)
    return pl.pallas_call(
        functools.partial(forward_body, names, group),
        grid=(rows // FORWARD_TILE,),
        in_specs=in_specs,
        out_specs=out_specs,
        out_shape=out_shape,
        scratch_shapes=scratch,
        compiler_params=params(60),
        cost_estimate=pl.CostEstimate(
            flops=2 * rows * size, bytes_accessed=24 * size, transcendentals=0
        ),
    )(*args)


def head_body(
    group,
    x_ref,
    target_ref,
    mask_ref,
    *refs,
):
    take = Taker(refs)
    arrays = take.refs[: group.parts]
    take(group.parts)
    gain_ref, dx_ref, dw_ref, dg_ref, loss_ref, acc_ref, whead_ref, sems = take(8)
    step = pl.program_id(0)
    me, core = place(group)
    made = copies(group, arrays, me, {"head": whead_ref}, sems, outward=False)

    @pl.when(step == 0)
    def _():
        acc_ref[...] = jnp.zeros_like(acc_ref)
        dg_ref[...] = jnp.zeros_like(dg_ref)
        loss_ref[...] = jnp.zeros_like(loss_ref)
        start_copies(group, made, core)
        wait_copies(made, ("head",))

    u, inverse = unit(x_ref[...])
    gain_row = gain_ref[0:1, :]
    final_in = (u * gain_row).astype(BF)
    predicted = dot_nn(final_in, whead_ref[...])
    target = target_ref[...]
    mask = mask_ref[...]
    loss = jnp.zeros((8, PMAX), F32)
    grads = []
    for q in range(NQ):
        level = (q + 1.0) / (NQ + 1)
        r = target - predicted[:, q * PMAX : (q + 1) * PMAX]
        a = r * (-1.0 / SMOOTH)
        e = jnp.exp(-jnp.abs(a))
        recip = 1.0 / (1.0 + e)
        sigmoid = jnp.where(a >= 0, recip, e * recip)
        softplus = jnp.maximum(a, 0.0) + jnp.log(1.0 + e)
        loss = loss + rows_to_eight((level * r + SMOOTH * softplus) * mask)
        grads.append(((sigmoid - level) * mask).astype(BF))
    loss_ref[...] += loss
    grad_pred = jnp.concatenate(grads, axis=1)
    acc_ref[...] += dot_tn(final_in, grad_pred)
    grad_x, grad_gain = rms_backward(u, inverse, gain_row, dot_nt(grad_pred, whead_ref[...]))
    dx_ref[...] = grad_x
    dg_ref[...] += grad_gain

    @pl.when(step == pl.num_programs(0) - 1)
    def _():
        dw_ref[...] = acc_ref[...].astype(BF)


def head(x, targets, mask, group, arrays, gain):
    rows = x.shape[0]
    return pl.pallas_call(
        functools.partial(head_body, group),
        grid=(rows // TILE,),
        in_specs=[
            rows_spec(D),
            rows_spec(PMAX),
            rows_spec(PMAX),
        ]
        + [any_spec()] * group.parts
        + [whole_spec(gain.shape)],
        out_specs=[
            rows_spec(D),
            whole_spec((D, HEADW)),
            whole_spec((8, D)),
            whole_spec((8, PMAX)),
        ],
        out_shape=[
            jax.ShapeDtypeStruct((rows, D), F32),
            jax.ShapeDtypeStruct((D, HEADW), BF),
            jax.ShapeDtypeStruct((8, D), F32),
            jax.ShapeDtypeStruct((8, PMAX), F32),
        ],
        scratch_shapes=[
            pltpu.VMEM((D, HEADW), F32),
            pltpu.VMEM((D, HEADW), BF),
            semaphores(group),
        ],
        compiler_params=params(60),
        cost_estimate=pl.CostEstimate(
            flops=6 * rows * D * HEADW, bytes_accessed=8 << 20, transcendentals=0
        ),
    )(x, targets, mask, *arrays, gain)


def backward_body(names, extra, group, out_group, *refs):
    first, attn, ffn = "in" in names, "qkv" in names, "gu" in names
    take = Taker(refs)
    dout_ref = take()
    if attn:
        x_ref, qkv_ref, prob_ref, mixed_ref = take(4)
    if ffn:
        mid_ref, gu_ref = take(2)
    concat_ref = take() if first else None
    extras = {extra: take()} if extra else {}
    arrays = take.refs[: group.parts]
    take(group.parts)
    gain_ref = take()
    if attn:
        cos_ref, sin_ref, code_ref = take(3)
    dx_ref = None if first else take()
    out_arrays = take.refs[: out_group.parts]
    take(out_group.parts)
    if attn:
        dg_attn, db_ref = take(2)
    if ffn:
        dg_ffn = take()
    loads = [n for n in names if n != "in"]
    w = take.named(loads)
    acc = take.named(names)
    grads = take.named(names)
    sems, out_sems = take(2)
    if attn:
        dqkv_ref = take()
    if ffn:
        dgu_ref = take()
    step = pl.program_id(0)
    me, core = place(group)
    made = copies(group, arrays, me, down_fields(w), sems, outward=False)
    out_core = place(out_group)[1]
    sent = copies(
        out_group, out_arrays, me, {**down_fields(grads), **extras}, out_sems, outward=True
    )

    @pl.when(step == 0)
    def _():
        start_copies(group, made, core)
        for ref in acc.values():
            ref[...] = jnp.zeros_like(ref)
        if attn:
            dg_attn[...] = jnp.zeros_like(dg_attn)
            db_ref[...] = jnp.zeros_like(db_ref)
        if ffn:
            dg_ffn[...] = jnp.zeros_like(dg_ffn)
        wait_copies(made, list(made))

    dout = dout_ref[...]
    rows = dout.shape[0]
    grad_mid = dout
    if ffn:
        dout_low = dout.astype(BF)
        gate = gu_ref[:, :FF].astype(F32)
        up = gu_ref[:, FF:].astype(F32)
        sig = sigmoid_of(gate)
        silu = gate * sig
        acc["d"][...] += dot_tn((silu * up).astype(BF), dout_low)
        grad_hidden = dot_nt(dout_low, w["d"][...])
        dgu_ref[:, :FF] = (grad_hidden * up * (sig + silu * (1.0 - sig))).astype(BF)
        dgu_ref[:, FF:] = (grad_hidden * silu).astype(BF)
        u_mid, inverse_mid = unit(mid_ref[...])
        gain_mid = gain_ref[1:2, :]
        acc["gu"][...] += dot_tn((u_mid * gain_mid).astype(BF), dgu_ref[...])
        grad_mid, dgain_mid = rms_backward(
            u_mid, inverse_mid, gain_mid, dot_nt(dgu_ref[...], w["gu"][...])
        )
        dg_ffn[...] += dgain_mid
        grad_mid = grad_mid + dout
    grad_x = grad_mid
    if attn:
        grad_attn_low = grad_mid.astype(BF)
        acc["o"][...] += dot_tn(mixed_ref[...], grad_attn_low)
        grad_mixed = dot_nt(grad_attn_low, w["o"][...]).astype(BF)
        spots = [(b, p) for p in range(PAIRS) for b in range(rows // BUCKET)]
        dprobs = []
        for b, p in spots:
            here = slice(b * BUCKET, (b + 1) * BUCKET)
            dm2 = two_blocks(grad_mixed[here, p * LANES : (p + 1) * LANES])
            v = qkv_ref[here, 2 * D + p * LANES : 2 * D + (p + 1) * LANES]
            dprobs.append(dot_nt(v, dm2))
        dscores = []
        for (b, p), dprob in zip(spots, dprobs):
            prob = prob_ref[b * BUCKET : (b + 1) * BUCKET, p * LANES : (p + 1) * LANES].astype(F32)
            ds = prob * (dprob - jnp.sum(prob * dprob, axis=0, keepdims=True))
            dscores.append(ds.astype(BF))
        for p in range(PAIRS):
            other_sum = jnp.zeros((8, LANES), F32)
            same_sum = jnp.zeros((8, LANES), F32)
            for b in range(rows // BUCKET):
                ds = dscores[p * (rows // BUCKET) + b].astype(F32)
                same = code_ref[b * BUCKET : (b + 1) * BUCKET, :] > 0.5
                same_sum = same_sum + rows_to_eight(jnp.where(same, ds, 0.0))
                other_sum = other_sum + rows_to_eight(jnp.where(same, 0.0, ds))
            db_ref[p * 8 : (p + 1) * 8, :] += other_sum
            db_ref[(PAIRS + p) * 8 : (PAIRS + p + 1) * 8, :] += same_sum
        for (b, p), ds in zip(spots, dscores):
            here = slice(b * BUCKET, (b + 1) * BUCKET)
            cols = slice(p * LANES, (p + 1) * LANES)
            kcols = slice(D + p * LANES, D + (p + 1) * LANES)
            vcols = slice(2 * D + p * LANES, 2 * D + (p + 1) * LANES)
            cos = cos_ref[here, :] * HD ** (-0.5)
            sin = sin_ref[here, :] * HD ** (-0.5)
            dm2 = two_blocks(grad_mixed[here, cols])
            dq = fold_blocks(dot_tn(ds, qkv_ref[here, kcols]))
            dk = dot_nn(ds, two_blocks(qkv_ref[here, cols]))
            dv = dot_nn(prob_ref[here, cols], dm2)
            dqkv_ref[here, cols] = (dq * cos + swap_halves(dq * sin)).astype(BF)
            dqkv_ref[here, kcols] = (dk * cos + swap_halves(dk * sin)).astype(BF)
            dqkv_ref[here, vcols] = dv.astype(BF)
        u, inverse = unit(x_ref[...])
        gain_row = gain_ref[0:1, :]
        acc["qkv"][...] += dot_tn((u * gain_row).astype(BF), dqkv_ref[...])
        grad_x, dgain = rms_backward(u, inverse, gain_row, dot_nt(dqkv_ref[...], w["qkv"][...]))
        dg_attn[...] += dgain
        grad_x = grad_x + grad_mid
    if first:
        acc["in"][...] += dot_tn(grad_x.astype(BF), concat_ref[...])
    else:
        dx_ref[...] = grad_x

    @pl.when(step == pl.num_programs(0) - 1)
    def _():
        for name in names:
            grads[name][...] = acc[name][...].astype(BF)
        start_copies(out_group, sent, out_core)
        wait_copies(sent, list(sent))


def backward_layer(names, dout, saved, concat, extra, group, arrays, out_group, gain_pair, tables):
    first, attn, ffn = "in" in names, "qkv" in names, "gu" in names
    rows = dout.shape[0]
    args = [dout, *saved] + ([concat] if first else [])
    in_specs = [rows_spec(a.shape[1]) for a in args]
    if extra:
        args.append(extra[1])
        in_specs.append(whole_spec(extra[1].shape))
    args += [*arrays, gain_pair]
    in_specs += [any_spec()] * group.parts + [whole_spec(gain_pair.shape)]
    if attn:
        args += list(tables)
        in_specs += [rows_spec(LANES)] * 3
    out_specs, out_shape = [], []
    if not first:
        out_specs.append(rows_spec(D))
        out_shape.append(jax.ShapeDtypeStruct((rows, D), F32))
    slots = (out_group.shards, out_group.rows, out_group.width)
    out_specs += [any_spec()] * out_group.parts
    out_shape += [jax.ShapeDtypeStruct(slots, BF)] * out_group.parts
    small = ([(8, D), (48, LANES)] if attn else []) + ([(8, D)] if ffn else [])
    out_specs += [whole_spec(shape) for shape in small]
    out_shape += [jax.ShapeDtypeStruct(shape, F32) for shape in small]
    scratch = [pltpu.VMEM(WEIGHTS[n], BF) for n in names if n != "in"]
    scratch += [pltpu.VMEM(WEIGHTS[n], F32) for n in names]
    scratch += [pltpu.VMEM(WEIGHTS[n], BF) for n in names]
    scratch += [semaphores(group), semaphores(out_group)]
    scratch += [pltpu.VMEM((TILE, QKV), BF)] if attn else []
    scratch += [pltpu.VMEM((TILE, 2 * FF), BF)] if ffn else []
    size = sum(WEIGHTS[n][0] * WEIGHTS[n][1] for n in names)
    got = pl.pallas_call(
        functools.partial(backward_body, names, extra[0] if extra else None, group, out_group),
        grid=(rows // TILE,),
        in_specs=in_specs,
        out_specs=out_specs,
        out_shape=out_shape,
        scratch_shapes=scratch,
        compiler_params=params(60),
        cost_estimate=pl.CostEstimate(
            flops=4 * rows * size, bytes_accessed=48 * size, transcendentals=0
        ),
    )(*args)
    got = list(got)
    grad = None if first else got.pop(0)
    return grad, got[: out_group.parts], got[out_group.parts :]


def partners(sizes, fsdp_mask, dp_mask):
    fsdp, dp = sizes
    return [
        (f * dp + d, (f ^ fsdp_mask) * dp + (d ^ dp_mask)) for f in range(fsdp) for d in range(dp)
    ]


def slot_of(offset, masks):
    slot = 0
    for bit, mask in enumerate(masks):
        slot = slot + jnp.where((offset & mask) != 0, 1 << bit, 0)
    return slot


def swap(x, sizes, fsdp_mask, dp_mask):
    return lax.ppermute(x, AXES, partners(sizes, fsdp_mask, dp_mask))


def reorder(slots, masks):
    me = lax.axis_index("fsdp")
    return jnp.stack(
        [
            lax.dynamic_index_in_dim(slots, slot_of(me ^ j, masks), 0, keepdims=False)
            for j in range(slots.shape[0])
        ]
    )


class Gather:
    def __init__(self, parts, sizes):
        self.sizes = sizes
        self.four = len(parts) == 4
        self.mine = by_place(parts)[0][None]
        self.masks = masks_of(sizes[0])
        self.last = self.masks.pop() if self.four else 0
        self.got = ()

    def land(self):
        if self.got:
            self.mine = jnp.concatenate([self.mine, *self.got], axis=0)
            self.got = ()
        return self.mine

    def move(self, after=None):
        mine = self.land()
        if after is not None:
            mine, after.got = lax.optimization_barrier((mine, after.got))
        self.mine = mine
        self.got = (swap(mine, self.sizes, self.masks.pop(0), 0),)

    def ring(self):
        mine = self.land()
        self.got = (swap(mine, self.sizes, self.last, 0), swap(mine, self.sizes, 0, 2))

    def hold(self, x):
        x, self.got = lax.optimization_barrier((x, self.got))
        return x

    def arrays(self):
        if not self.four:
            mine = self.land()
            return mine, swap(mine, self.sizes, 0, 1)
        near, far = self.got
        half = near.shape[0] // 2
        corner = (
            swap(far[:half], self.sizes, self.last, 0),
            swap(near[half:], self.sizes, 0, 2),
        )
        mine = jnp.concatenate([self.mine, near], axis=0)
        far = jnp.concatenate([far, *corner], axis=0)
        return mine, swap(mine, self.sizes, 0, 1), far, swap(far, self.sizes, 0, 1)


def by_place(parts):
    place = lax.axis_index("dp") & (len(parts) - 1)
    found = []
    for distance in range(len(parts)):
        one = parts[distance]
        for other in range(1, len(parts)):
            one = jnp.where(place == other, parts[other ^ distance], one)
        found.append(one)
    return found


def by_core(mine, other):
    core = lax.axis_index("dp") & 1
    return jnp.where(core == 0, mine, other), jnp.where(core == 0, other, mine)


def add(a, b):
    return (a.astype(F32) + b.astype(F32)).astype(BF)


def to_slots(shards, masks):
    me = lax.axis_index("fsdp")
    slots = [None] * shards.shape[0]
    for v in range(shards.shape[0]):
        slots[slot_index(v, masks)] = lax.dynamic_index_in_dim(shards, me ^ v, 0, keepdims=False)
    return jnp.stack(slots)


class Scatter:
    def __init__(self, keep, give, sizes):
        self.sizes = sizes
        self.keep = keep
        self.got = swap(give, sizes, 0, 1)
        self.moves = [(mask, 0) for mask in reversed(masks_of(sizes[0]))]
        dp_mask = 2
        while dp_mask < sizes[1]:
            self.moves.append((0, dp_mask))
            dp_mask *= 2

    def ready(self):
        if self.moves and self.moves[0][0]:
            half = self.keep.shape[0] // 2
            self.away = add(self.keep[half:], self.got[half:])
            self.keep = add(self.keep[:half], self.got[:half])
        else:
            self.keep = add(self.keep, self.got)
            self.away = self.keep

    def move(self):
        self.got = swap(self.away, self.sizes, *self.moves.pop(0))

    def total(self):
        return add(self.keep, self.got)[0]


def hold(x, *scatters):
    for one in scatters:
        one.ready()
    held = lax.optimization_barrier((x, [(one.keep, one.away) for one in scatters]))
    for one, (keep, away) in zip(scatters, held[1]):
        one.keep, one.away = keep, away
        one.move()
    return held[0]


def after_landing(x, scatters):
    x, landed = lax.optimization_barrier((x, [one.got for one in scatters]))
    for one, got in zip(scatters, landed):
        one.got = got
    return x


def pad_rows(x, rows):
    return jnp.pad(x, ((0, 0),) * (x.ndim - 2) + ((0, rows - x.shape[-2]), (0, 0)))


def to_whole(group, whole, arrays, sizes):
    masks = masks_of(sizes[0])
    arrays = [reorder(a, masks) for a in by_place(arrays)]
    fields = group.unpack(arrays)
    fields = {n: p.reshape(1, p.shape[0] * p.shape[1], p.shape[2]) for n, p in fields.items()}
    return whole.pack(fields)


def from_whole(group, whole, arrays, sizes):
    fsdp = sizes[0]
    fields = whole.unpack(arrays)
    fields = {n: p.reshape(fsdp, p.shape[1] // fsdp, p.shape[2]) for n, p in fields.items()}
    arrays = group.pack(fields)
    if group.parts == 1:
        return arrays
    masks = masks_of(fsdp)
    return by_core(*[to_slots(a, masks) for a in arrays])


def rotary_tables(time_ids):
    frequency = THETA ** (-2.0 * jnp.arange(HD // 2, dtype=F32) / HD)
    phase = time_ids.astype(F32)[:, None] * frequency[None, :]
    cos, sin = jnp.cos(phase), jnp.sin(phase)
    return jnp.concatenate([cos] * 4, axis=1), jnp.concatenate([-sin, sin, -sin, sin], axis=1)


def live_slots(lengths):
    return jnp.arange(BUCKET, dtype=jnp.int32)[None, :] < lengths[:, None]


def target_mask(size_ids, lengths):
    widths = jnp.where(live_slots(lengths).reshape(size_ids.shape), PMAX >> (4 - size_ids), 0)
    return (jnp.arange(PMAX, dtype=jnp.int32)[None, :] < widths[:, None]).astype(F32)


def code_table(variate_ids, lengths):
    variates = variate_ids.reshape(-1, BUCKET)
    same = (variates[:, :, None] == variates[:, None, :]).astype(F32)
    code = jnp.where(live_slots(lengths)[:, :, None], same, -1.0).reshape(-1, BUCKET)
    return jnp.concatenate([code, code], axis=1)


def patch_concat(patches, size_ids):
    pieces = []
    for size_id in range(5):
        span = PMAX >> 4 - size_id
        chosen = (size_ids == size_id)[:, None]
        pieces.append(jnp.where(chosen, patches[:, :span], jnp.zeros((), BF)))
    pieces.append(jnp.zeros((patches.shape[0], 2 * PMAX - IN_CAT), BF))
    return jnp.concatenate(pieces, axis=1)


def adam_update(master, clipped, first_old, second_old, matrix):
    first_new = BETA_ONE * first_old + (1.0 - BETA_ONE) * clipped
    second_new = BETA_TWO * second_old + (1.0 - BETA_TWO) * clipped * clipped
    first_hat = first_new * (1.0 / (1.0 - BETA_ONE**STEP_NUM))
    second_hat = second_new * (1.0 / (1.0 - BETA_TWO**STEP_NUM))
    direction = first_hat / (jnp.sqrt(second_hat) + ADAM_EPS)
    if matrix:
        master_new = master - RATE_MATRIX * (direction + WEIGHT_DECAY * master)
    else:
        master_new = master - RATE_GAIN * direction
    return (master_new, first_new, second_new)


def beside(x, sizes, across):
    moves = [(mask, 0) for mask in masks_of(sizes[0])]
    if across:
        moves = []
    dp_mask = 2 if across else 1
    while dp_mask < (sizes[1] if across else 2):
        moves.append((0, dp_mask))
        dp_mask *= 2
    for fsdp_mask, dp_mask in moves:
        x = x + swap(x, sizes, fsdp_mask, dp_mask)
    return x


STACKED = ("qkv", "o", "gu", "d")


def update_body(groups, layers, *refs):
    take = Taker(refs)
    scale_ref = take()
    parts = [take(group.parts) for group in groups]
    names = STACKED + ("head",)
    states = [take.named(names) for _ in range(3)]
    fresh = [take.named(names) for _ in range(3)]
    scale = scale_ref[0, 0]

    def one(name, index, grad):
        old = [state[name][index] for state in states]
        new = adam_update(old[0], grad.astype(F32) * scale, old[1], old[2], True)
        for target, value in zip(fresh, new):
            target[name][index] = value

    def layer_step(layer, place_here):
        for group, group_parts, at_layer in zip(groups, parts, layers):
            if at_layer != layer:
                continue
            for part, at, name, start, width in group.pieces:
                if name == "in":
                    continue
                first, count, _ = group.row_span(name)
                grad = group_parts[part ^ place_here][0:count, at : at + width]
                cols = slice(start, start + width)
                if name == "head":
                    one("head", (slice(0, count), cols), grad)
                else:
                    rows = slice(first, first + count) if name[0] == "d" else slice(0, count)
                    one(name[0] if name[0] == "d" else name, (0, rows, cols), grad)

    core = lax.axis_index("dp") & 1
    for layer in range(L):
        for which in range(2):
            chosen = (pl.program_id(0) == layer) & (core == which)
            pl.when(chosen)(functools.partial(layer_step, layer, which))


def update(groups, layers, parts, scale, states):
    def spec(x):
        if x.ndim == 2:
            return whole_spec(x.shape)
        return pl.BlockSpec((1,) + x.shape[1:], lambda i: (i, 0, 0))

    flat = [x for state in states for x in state]
    got = pl.pallas_call(
        functools.partial(update_body, groups, layers),
        grid=(L,),
        in_specs=[pl.BlockSpec(memory_space=pltpu.SMEM)]
        + [whole_spec(p.shape) for pair in parts for p in pair]
        + [spec(x) for x in flat],
        out_specs=[spec(x) for x in flat],
        out_shape=[jax.ShapeDtypeStruct(x.shape, F32) for x in flat],
        compiler_params=params(60),
        cost_estimate=pl.CostEstimate(flops=1 << 24, bytes_accessed=18 << 20, transcendentals=0),
    )(scale.reshape(1, 1), *[p for pair in parts for p in pair], *flat)
    return [got[i : i + len(states[0])] for i in range(0, len(flat), len(states[0]))]


def per_device(sizes, *args):
    patches, targets, size_ids, time_ids, variate_ids, lengths = args[:6]
    masters = args[6:14]
    firsts = args[14:22]
    seconds = args[22:30]
    w_in, w_qkv, w_o, w_gu, w_down, w_head, gains, var_bias = masters
    own = w_head.shape[0]
    down_rows = w_down.shape[1]
    direct = own % 16 == 0 and down_rows % 16 == 0
    attn_fields = [("qkv", QKV), ("o", D)]
    ffn_fields = [("d0", D), ("d1", D), ("gu", 2 * FF), ("d2", D)]
    plan = [
        (("in",) + ATTN, [("in", 2 * PMAX)] + attn_fields),
        (FFN, ffn_fields),
        (ATTN + FFN, attn_fields + ffn_fields),
        (ATTN + FFN, attn_fields + ffn_fields + [("head", HEADW)]),
    ]
    layers = [0, 0, 1, 2]
    count = len(plan)
    def groups_of(fields, parts):
        many = [Group(f, p, sizes[0], own, down_rows) for f, p in zip(fields, parts)]
        if direct:
            return many, many
        return many, [Group(f, p, 1, D, FF) for f, p in zip(fields, parts)]

    fields = [f for _, f in plan]
    groups, wholes = groups_of(fields, [2] * count)
    in_fields = [fields[0] + fields[1], fields[2], fields[3]]
    in_groups, in_wholes = groups_of(in_fields, [4, 2, 4])
    sources = [0, 0, 1, 2]

    in_rows = jnp.concatenate(
        [w_in.T, gains.T, jnp.zeros((own, 2 * PMAX - IN_CAT - NGAIN), F32)], axis=1
    ).astype(BF)
    def packed(layer, stacks, head_w=None):
        fields = {m: w[layer].astype(BF) for m, w in zip(("qkv", "o", "gu", "d"), stacks)}
        if layer == L - 1:
            fields["head"] = head_w.astype(BF)
        return in_groups[layer].pack({**fields, "in": in_rows})

    stacks = (w_qkv, w_o, w_gu, w_down)
    first = Gather(packed(0, stacks), sizes)
    first.move()
    stacks, head_w, time_ids = first.hold((stacks, w_head, time_ids))
    second, third = [Gather(packed(layer, stacks, head_w), sizes) for layer in (1, 2)]
    cos, sin = rotary_tables(time_ids)
    while first.masks:
        first.move()
    early = (patches, size_ids, variate_ids, lengths)
    early, second.mine = first.hold((early, second.mine))
    patches, size_ids, variate_ids, lengths = early
    first.ring()
    second.move()
    third.move(second)
    while second.masks:
        second.move()
    while len(third.masks) > 1:
        third.move()

    def arrived(layer):
        arrays = (first, second, third)[layer].arrays()
        return arrays if direct else to_whole(in_groups[layer], in_wholes[layer], arrays, sizes)

    tables = (cos, sin, code_table(variate_ids, lengths))
    concat = patch_concat(patches, size_ids)
    bias_lanes = jnp.repeat(var_bias, HD, axis=2).reshape(L, 2, PAIRS, LANES)
    bias_lanes = jnp.pad(bias_lanes, ((0, 0), (0, 0), (0, 8 - PAIRS), (0, 0)))
    bias_lanes = bias_lanes.reshape(L, 16, LANES)

    stream = concat
    kept = [None] * count
    loaded = []
    gain_pairs = [None] * (L + 1)
    for layer in range(L):
        if layer == 1:
            second.mine, third.got = lax.optimization_barrier((second.land(), third.got))
        loaded.append(arrived(layer))
        if layer == 0:
            third.mine, stream = lax.optimization_barrier((third.land(), stream))
            while third.masks:
                third.move()
        if layer == 1:
            third.ring()
        names = ATTN + FFN if layer else ("in",) + ATTN + FFN
        got = list(
            forward_layer(
                stream,
                names,
                in_wholes[layer],
                loaded[layer],
                gain_pairs[layer],
                bias_lanes[layer],
                tables,
            )
        )
        if layer == 0:
            stream, found = got[:2]
            got = got[2:]
            gain_pairs = [found[0:2], found[2:4], found[4:6], found[6:8]]
            kept[0] = [stream, *got[:3]]
            kept[1] = [got[3], got[5]]
        else:
            kept[layer + 1] = [stream, *got[:4], got[5]]
        stream = got[4]
        for one in (second, third)[layer:]:
            stream = one.hold(stream)
        if layer == 0:
            stream, size_ids, lengths = lax.optimization_barrier((stream, size_ids, lengths))
            mask = target_mask(size_ids, lengths)
            live = jnp.sum(mask)
    grad, head_grad, gain_grad, loss = head(
        stream, targets, mask, in_wholes[-1], loaded[-1], gain_pairs[L]
    )
    raw = [gain_grad, loss]
    totals = [None] * count
    for n in reversed(range(count)):
        names = plan[n][0]
        layer = layers[n]
        grad, arrays, small = backward_layer(
            names,
            grad,
            kept[n],
            concat,
            ("head", head_grad) if n == count - 1 else None,
            in_wholes[sources[n]],
            loaded[sources[n]],
            wholes[n],
            gain_pairs[layer],
            tables,
        )
        raw += small
        if not direct:
            arrays = from_whole(groups[n], wholes[n], arrays, sizes)
        keep, give = arrays
        flying = totals[n + 1 :]
        give = after_landing(give, flying[1:] if n == 1 else flying)
        totals[n] = Scatter(keep, give, sizes)
        if n:
            grad = hold(grad, totals[n], *flying)

    raw = hold(raw, *totals)
    gain_grad, loss, *raw = raw
    gain_grads, bias_grads = {2 * L: gain_grad}, [None] * L
    for n in reversed(range(count)):
        names = plan[n][0]
        layer = layers[n]
        if "qkv" in names:
            gain_grads[2 * layer] = raw.pop(0)
            bias_grads[layer] = raw.pop(0).reshape(2, PAIRS, 8, 2, HD)
        if "gu" in names:
            gain_grads[2 * layer + 1] = raw.pop(0)
    gain_grads = [jnp.sum(gain_grads[g], axis=0) for g in range(NGAIN)]
    bias_grads = jnp.sum(jnp.stack(bias_grads), axis=(3, 5)).reshape(L, 2, H)

    small = jnp.concatenate([jnp.sum(loss)[None], live[None], bias_grads.reshape(-1)])
    small = jnp.pad(small, (0, D - small.shape[0]))
    rows = jnp.stack(gain_grads + [small])
    rows = beside(rows, sizes, across=True)
    pending = list(zip(range(count), totals))
    own_parts = [None] * count
    first = True
    while pending:
        for n, one in pending:
            if not one.moves:
                own_parts[n] = one.total()
        pending = [(n, one) for n, one in pending if one.moves]
        if not pending:
            break
        if not first:
            hold((), *[one for _, one in pending])
        first = False
    squares = jnp.zeros((1, 1), F32)
    for n, part in enumerate(own_parts):
        squares = squares + groups[n].squares(part)
    rows = beside(rows + jnp.pad(squares, ((NGAIN, 0), (D - 1, 0))), sizes, across=False)
    squares = rows[NGAIN, D - 1]
    loss_sum, total_count = rows[NGAIN, 0], rows[NGAIN, 1]
    inverse_count = 1.0 / total_count
    bias_grad = rows[NGAIN, 2 : 2 + var_bias.size].reshape(var_bias.shape) * inverse_count
    at_row = lax.broadcasted_iota(jnp.int32, rows.shape, 0)
    at_col = lax.broadcasted_iota(jnp.int32, rows.shape, 1)
    counted = (at_row < NGAIN) | ((at_col >= 2) & (at_col < 2 + var_bias.size))
    squares = squares + jnp.sum(jnp.where(counted, jnp.square(rows), 0.0))
    gain_all = rows[:NGAIN]
    gain_own = lax.dynamic_slice_in_dim(gain_all, lax.axis_index("fsdp") * own, own, axis=1)

    grad_norm = jnp.sqrt(squares) * inverse_count
    factor = jnp.minimum(1.0, CLIP_NORM / grad_norm)
    scale = factor * inverse_count


    pairs = [(part, swap(part, sizes, 0, 1)) for part in own_parts]
    whole_parts = [by_core(*pair) for pair in pairs]
    fresh = [None] * 8
    if direct:
        states = [[group_of[m] for m in (1, 2, 3, 4, 5)] for group_of in (masters, firsts, seconds)]
        new = update(groups, layers, pairs, scale, states)
        for at, m in enumerate((1, 2, 3, 4, 5)):
            fresh[m] = tuple(kind[at] for kind in new)
    pieces = [groups[n].unpack(whole_parts[n]) for n in range(count)]
    matrices = [[piece[m] for piece in pieces if m in piece] for m in STACKED]
    gradients = [pieces[0]["in"][:, :IN_CAT].T] + [jnp.stack(m) for m in matrices]
    gradients += [pieces[-1]["head"], gain_own]
    clipped = [g.astype(F32) * scale for g in gradients] + [bias_grad * factor]
    for m in range(8):
        if fresh[m] is None:
            fresh[m] = adam_update(masters[m], clipped[m], firsts[m], seconds[m], m < 6)
    return (
        (loss_sum, total_count, grad_norm)
        + tuple(f[0] for f in fresh)
        + tuple(f[1] for f in fresh)
        + tuple(f[2] for f in fresh)
    )


def solution(mesh):
    sizes = (mesh.shape["fsdp"], mesh.shape["dp"])
    tokens = P(("fsdp", "dp"))
    tokens_two = P(("fsdp", "dp"), None)
    columns = P(None, "fsdp")
    stacked = P(None, "fsdp", None)
    states = (columns, stacked, stacked, stacked, stacked, P("fsdp", None), columns, P())
    in_specs = (tokens_two, tokens_two, tokens, tokens, tokens, tokens) + states * 3
    out_specs = (P(), P(), P()) + states * 3
    return jax.shard_map(
        functools.partial(per_device, sizes),
        mesh=mesh,
        in_specs=in_specs,
        out_specs=out_specs,
        check_vma=False,
    )
```
